256 devices in a mesh: ctx: 32 (over x, y, core), head: 8 (over z).
Axes of the slice: x: 4, y: 4, z: 8, core: 2. Of those that a mesh axis runs over, the one named last changes fastest.
Arguments:
- queries: bfloat16 [8192, 4096], P('ctx', 'head'), may hold values from -6 to 6
- keys_in: bfloat16 [8192, 4096], P('ctx', 'head'), may hold values from -6 to 6
- values: bfloat16 [8192, 4096], P('ctx', 'head'), may hold values from -12 to 12
- norm_gain: float32 [4096], P('head'), may hold values from 0.25 to 1.75
- out_grad: bfloat16 [8192, 4096], P('ctx', 'head'), may hold values from -6 to 6
Outputs:
- normed: bfloat16 [8192, 4096], P('ctx', 'head')
- query_grad: bfloat16 [8192, 4096], P('ctx', 'head')
- key_grad: bfloat16 [8192, 4096], P('ctx', 'head')
- value_grad: bfloat16 [8192, 4096], P('ctx', 'head')
- gain_grad: float32 [4096], P('head')
The draws below stay inside these ranges and needn't reach their ends.
All inputs are finite; a program needn't handle non-finite values.
Results may differ from the reference program's by a relative error of at most 0.02.
The reference program's roundings to bfloat16 on the way count: a program that leaves them out, or rounds other values in their place, can miss the bound.
Values may be sent and summed in bfloat16 or wider, within the bound.
No kernel may reach another device: no remote copies, remote signals or barrier semaphores. Data moves between devices by JAX's collectives and lax.ppermute only.
A program may use at most 64 MiB of HBM per device.

```python
import jax
import jax.numpy as jnp
from jax import lax

DH = 128
M = 256
ITERS = 2
HEADS = 32
WIDTH = 4096
TOKENS = 8192


def segment_rows(key):
    base = jax.random.normal(key, (M, HEADS * DH), jnp.float32)
    level = 0.5 * jnp.sqrt(1.0 + 2.0 * jnp.arange(M, dtype=jnp.float32) / M)
    return base * level[:, None]


def draw_queries(key, part):
    rows = segment_rows(key)
    key = jax.random.fold_in(key, 11)
    noise = jax.random.normal(key, (TOKENS, HEADS * DH), jnp.float32)
    whole = jnp.repeat(rows, TOKENS // M, axis=0) + 0.5 * noise
    return jnp.clip(whole, -6.0, 6.0).astype(jnp.bfloat16)


def draw_keys_in(key, part):
    rows = segment_rows(key)
    key = jax.random.fold_in(key, 17)
    noise = jax.random.normal(key, (TOKENS, HEADS * DH), jnp.float32)
    whole = jnp.repeat(rows, TOKENS // M, axis=0) + 0.5 * noise
    return jnp.clip(whole, -6.0, 6.0).astype(jnp.bfloat16)


def draw_values(key, part):
    key = jax.random.fold_in(key, 13)
    feature_total = HEADS * DH
    noise = jax.random.normal(key, (TOKENS, feature_total), jnp.float32)
    columns = jnp.sqrt(1.0 + 2.0 * jnp.arange(feature_total, dtype=jnp.float32) / (feature_total - 1))
    noise = noise * columns[None, :]
    return jnp.clip(noise, -12.0, 12.0).astype(jnp.bfloat16)


def levels(stream_key, extent, shards, smallest, top_value):
    def one(position, shards_of):
        draws = jax.random.uniform(jax.random.fold_in(jax.random.fold_in(stream_key, 6), position), (shards_of,), jnp.float32, smallest / len(shards), top_value / len(shards))
        return jnp.repeat(jnp.exp(draws), extent[position] // shards_of).reshape((-1,) + (1,) * (len(extent) - position - 1))

    loudness = one(*shards[0])
    for cut in shards[1:]:
        loudness = loudness * one(*cut)
    return loudness


def bell_draw(stream_key, extent, scale, most, cuts=(), kind=jnp.bfloat16):
    result = scale * jax.random.normal(stream_key, extent, jnp.float32)
    if cuts:
        result = result * levels(stream_key, extent, cuts, -0.22, 0.18)
    return jnp.clip(result, -most, most).astype(kind)


def setup_inputs(seed: int = 0) -> dict:
    keys = jax.random.split(jax.random.key(seed), 6)
    return {
        "queries": draw_queries(jax.random.fold_in(keys[5], 71), 0),
        "keys_in": draw_keys_in(jax.random.fold_in(keys[5], 71), 0),
        "values": draw_values(jax.random.fold_in(keys[5], 71), 0),
        "norm_gain": jnp.clip(1.0 + 0.15 * jax.random.normal(keys[3], (WIDTH,), jnp.float32), 0.25, 1.75),
        "out_grad": bell_draw(keys[4], (TOKENS, WIDTH), 1.0, 6.0, ((0, 32), (1, 8))),
    }


HIGH_PRECISION = lax.Precision.HIGHEST
EPS = 1e-06

def newton_inverse(matrix):
    column_total = lax.optimization_barrier(jnp.max(lax.optimization_barrier(jnp.sum(matrix, axis=-2)), axis=-1))
    factor = lax.stop_gradient(1.0 / column_total)
    approx = jnp.swapaxes(matrix, -1, -2) * factor[..., None, None]
    identity_m = jnp.eye(matrix.shape[-1], dtype=jnp.float32)
    for sweep_index in range(ITERS):
        product = jnp.einsum('...ij,...jk->...ik', matrix, approx, precision=HIGH_PRECISION)
        inner_term = 7.0 * identity_m - product
        inner_term = 15.0 * identity_m - jnp.einsum('...ij,...jk->...ik', product, inner_term, precision=HIGH_PRECISION)
        inner_term = 13.0 * identity_m - jnp.einsum('...ij,...jk->...ik', product, inner_term, precision=HIGH_PRECISION)
        approx = 0.25 * jnp.einsum('...ij,...jk->...ik', approx, inner_term, precision=HIGH_PRECISION)
    return approx

def mix_weights(kernel_two, context):
    return jnp.einsum('...ij,...jk->...ik', newton_inverse(kernel_two), context, precision=HIGH_PRECISION)

def landmark_means(tokens_block):
    seg_len = tokens_block.shape[0] // M
    summed = lax.optimization_barrier(jnp.sum(tokens_block.reshape(M, seg_len, tokens_block.shape[1]).astype(jnp.float32), axis=1))
    return (summed / seg_len).astype(jnp.bfloat16)

def head_forward(query_h, key_h, value_h):
    scale_q = DH ** (-0.5)
    land_q = landmark_means(query_h)
    land_k = landmark_means(key_h)
    kernel_one = jax.nn.softmax(jnp.dot(query_h, land_k.T, preferred_element_type=jnp.float32) * scale_q, axis=-1)
    kernel_first_batched = kernel_one.astype(jnp.bfloat16)
    kernel_two = jax.nn.softmax(jnp.dot(land_q, land_k.T, preferred_element_type=jnp.float32) * scale_q, axis=-1)
    score_three = jnp.dot(land_q, key_h.T, preferred_element_type=jnp.float32) * scale_q
    row_top = lax.optimization_barrier(jnp.max(score_three, axis=-1))
    exp_three = jnp.exp(score_three - row_top[:, None])
    totals = lax.optimization_barrier(jnp.sum(exp_three, axis=-1))
    exp_third_batched = exp_three.astype(jnp.bfloat16)
    weighted = jnp.dot(exp_third_batched, value_h, preferred_element_type=jnp.float32)
    context = weighted / totals[:, None]
    mixing_batched = mix_weights(kernel_two, context).astype(jnp.bfloat16)
    attended = jnp.dot(kernel_first_batched, mixing_batched, preferred_element_type=jnp.float32)
    return (attended, land_q, land_k, kernel_one, kernel_first_batched, kernel_two, exp_three, exp_third_batched, totals, context, mixing_batched)

def head_backward(query_h, key_h, value_h, dout_h):
    scale_q = DH ** (-0.5)
    seg_len = query_h.shape[0] // M
    attended, land_q, land_k, kernel_one, kernel_first_batched, kernel_two, exp_three, exp_third_batched, totals, context, mixing_batched = head_forward(query_h, key_h, value_h)
    grad_mixing = jnp.dot(kernel_first_batched.T, dout_h, preferred_element_type=jnp.float32)
    gradient_kernel_first = jnp.dot(dout_h, mixing_batched.T, preferred_element_type=jnp.float32)
    gradient_score_first = (kernel_one * (gradient_kernel_first - lax.optimization_barrier(jnp.sum(kernel_one * gradient_kernel_first, axis=-1, keepdims=True)))).astype(jnp.bfloat16)
    query_one = jnp.dot(gradient_score_first, land_k, preferred_element_type=jnp.float32) * scale_q
    keyland_one = jnp.dot(gradient_score_first.T, query_h, preferred_element_type=jnp.float32) * scale_q
    unused, pull_back = jax.vjp(mix_weights, kernel_two, context)
    grad_ktwo, grad_context = pull_back(grad_mixing)
    gradient_score_second = kernel_two * (grad_ktwo - lax.optimization_barrier(jnp.sum(kernel_two * grad_ktwo, axis=-1, keepdims=True)))
    queryland_two = jnp.dot(gradient_score_second, land_k.astype(jnp.float32), precision=HIGH_PRECISION) * scale_q
    keyland_two = jnp.dot(gradient_score_second.T, land_q.astype(jnp.float32), precision=HIGH_PRECISION) * scale_q
    grad_totals = -lax.optimization_barrier(jnp.sum(grad_context * context, axis=-1)) / totals
    weighted_gradient = (grad_context / totals[:, None]).astype(jnp.bfloat16)
    grad_exp = jnp.dot(weighted_gradient, value_h.T, preferred_element_type=jnp.float32) + grad_totals[:, None]
    gradient_score_third = (exp_three * grad_exp).astype(jnp.bfloat16)
    value_grad = jnp.dot(exp_third_batched.T, weighted_gradient, preferred_element_type=jnp.float32).astype(jnp.bfloat16)
    queryland_three = jnp.dot(gradient_score_third, key_h, preferred_element_type=jnp.float32) * scale_q
    key_three = jnp.dot(gradient_score_third.T, land_q, preferred_element_type=jnp.float32) * scale_q
    query_land = queryland_two + queryland_three
    key_land = keyland_one + keyland_two
    query_grad = (query_one + jnp.repeat(query_land, seg_len, axis=0) / seg_len).astype(jnp.bfloat16)
    key_grad = (key_three + jnp.repeat(key_land, seg_len, axis=0) / seg_len).astype(jnp.bfloat16)
    return (query_grad, key_grad, value_grad)

def reference(queries, keys_in, values, norm_gain, out_grad):

    def split_heads(tokens_block):
        return jnp.moveaxis(tokens_block.reshape(TOKENS, HEADS, DH), 1, 0)

    def join_heads(tokens_block):
        return jnp.moveaxis(tokens_block, 0, 1).reshape(TOKENS, HEADS * DH)
    query_per_head = split_heads(queries)
    key_per_head = split_heads(keys_in)
    value_per_head = split_heads(values)

    def forward_only(triple):
        return head_forward(triple[0], triple[1], triple[2])[0]
    output = join_heads(lax.map(forward_only, (query_per_head, key_per_head, value_per_head)))
    feature_total = HEADS * DH
    root_inv = lax.rsqrt(lax.optimization_barrier(jnp.sum(output * output, axis=-1)) / feature_total + EPS)
    normed = (output * root_inv[:, None] * norm_gain).astype(jnp.bfloat16)
    grad_float = out_grad.astype(jnp.float32)
    scaled_grad = grad_float * norm_gain
    slope_dot = lax.optimization_barrier(jnp.sum(scaled_grad * output, axis=-1)) * root_inv / feature_total
    d_output = (root_inv[:, None] * (scaled_grad - output * (root_inv * slope_dot)[:, None])).astype(jnp.bfloat16)
    gain_grad = lax.optimization_barrier(jnp.sum(grad_float * output * root_inv[:, None], axis=0))

    def backward_only(quad):
        return head_backward(quad[0], quad[1], quad[2], quad[3])
    query_grad, key_grad, value_grad = lax.map(backward_only, (query_per_head, key_per_head, value_per_head, split_heads(d_output)))
    return (normed, join_heads(query_grad), join_heads(key_grad), join_heads(value_grad), gain_grad)
```

```python
import jax
import jax.numpy as jnp
from jax import lax
from jax.sharding import PartitionSpec as P

DH = 128
M = 256
EPS = 1e-06
HIGHEST = lax.Precision.HIGHEST
F32 = jnp.float32
BF16 = jnp.bfloat16
SCALE = DH ** (-0.5)


def exact(a, b, dims=(((1,), (0,)), ((), ()))):
    return lax.dot_general(a, b, dims, precision=HIGHEST, preferred_element_type=F32)


def exchange(parts, axis):
    return lax.all_to_all(parts, axis, 0, 0)


def spread(mine, axis):
    count = lax.axis_size(axis)
    return exchange(jnp.broadcast_to(mine[None], (count,) + mine.shape), axis)


def high_low(x):
    high = x.astype(BF16).astype(F32)
    return high, x - high


def landmark_means(tokens_block, seg_len):
    summed = jnp.sum(
        tokens_block.reshape(-1, seg_len, tokens_block.shape[1]).astype(F32), axis=1
    )
    return (summed / seg_len).astype(BF16)


def cubic(x, p):
    two = 7.0 * x - exact(x, p)
    four = 15.0 * x - exact(two, p)
    return 13.0 * x - exact(four, p), (x, two, four)


def cubic_back(grad, saved, p):
    x, two, four = saved
    d_five = -grad
    d_four = exact(d_five, p)
    d_three = -d_four
    d_two = exact(d_three, p)
    d_one = -d_two
    d_x = 13.0 * grad + 15.0 * d_four + 7.0 * d_two + exact(d_one, p)
    d_p = exact(
        jnp.concatenate([four, two, x], 0),
        jnp.concatenate([d_five, d_three, d_one], 0),
        (((0,), (0,)), ((), ())),
    )
    return d_x, d_p


def inverse_setup(lq, lk):
    ktwo = jax.nn.softmax(
        lax.dot_general(lq, lk, (((1,), (1,)), ((), ())), preferred_element_type=F32) * SCALE,
        axis=-1,
    )
    factor = 1.0 / jnp.max(jnp.sum(ktwo, axis=0))
    p0 = factor * exact(ktwo, ktwo, (((1,), (1,)), ((), ())))
    eye = jnp.eye(M, dtype=F32)
    h1 = 7.0 * eye - p0
    h2 = 15.0 * eye - exact(p0, h1)
    h3 = 13.0 * eye - exact(p0, h2)
    p1 = 0.25 * exact(p0, h3)
    return ktwo, factor, p0, p1, (h1, h2, h3)


def on_device(queries, keys_in, values, norm_gain, out_grad):
    tok, width_dev = queries.shape
    heads = width_dev // DH
    n_ctx = lax.axis_size("ctx")
    per_head = n_ctx // heads
    cols = DH // per_head
    land_dev = M // n_ctx
    seg_len = tok // land_dev
    feature_total = width_dev * lax.axis_size("head")
    my_head = lax.axis_index("ctx") // per_head

    q3 = queries.reshape(tok, heads, DH)
    k3 = keys_in.reshape(tok, heads, DH)
    v3 = values.reshape(tok, heads, DH)

    own = jnp.concatenate(
        [landmark_means(queries, seg_len), landmark_means(keys_in, seg_len)], axis=1
    )
    land = spread(own, "ctx").reshape(M, 2 * width_dev)
    lq = land[:, :width_dev].reshape(M, heads, DH)
    lk = land[:, width_dev:].reshape(M, heads, DH)

    score_three = jnp.einsum("thd,lhd->htl", k3, lq, preferred_element_type=F32) * SCALE
    shift = jnp.max(score_three, axis=1).astype(BF16).astype(F32)
    exp_local = jnp.exp(score_three - shift[:, None])
    tot_high, tot_low = high_low(jnp.sum(exp_local, axis=1))
    weighted = jnp.einsum(
        "thd,htl->hdl", v3, exp_local.astype(BF16), preferred_element_type=F32
    )
    stats = jnp.stack([shift, tot_high, tot_low], axis=1)
    stats = jnp.pad(stats, ((0, 0), (0, 5), (0, 0)))
    stats = jnp.broadcast_to(stats[:, None], (heads, per_head, 8, M))
    parts = jnp.concatenate([weighted.reshape(heads, per_head, cols, M), stats], axis=2)
    got = exchange(parts.reshape(n_ctx, cols + 8, M).astype(BF16), "ctx").astype(F32)

    my_lq = lax.dynamic_slice_in_dim(land, my_head * DH, DH, 1)
    my_lk = lax.dynamic_slice_in_dim(land, width_dev + my_head * DH, DH, 1)
    ktwo, factor, p0, p1, hs = inverse_setup(my_lq, my_lk)

    shifts = got[:, cols]
    top = jnp.max(shifts, axis=0)
    fade = jnp.exp(shifts - top)
    totals = jnp.sum(fade * (got[:, cols + 1] + got[:, cols + 2]), axis=0)
    context = jnp.sum(fade[:, None] * got[:, :cols], axis=0) / totals

    inner, saved_inner = cubic(context, p1)
    outer, saved_outer = cubic(inner, p0)
    my_mixing = (factor / 16.0) * exact(outer, ktwo)
    mixing = spread(my_mixing.astype(BF16), "ctx").reshape(heads, DH, M)

    kernel_one = jax.nn.softmax(
        jnp.einsum("thd,lhd->htl", q3, lk, preferred_element_type=F32) * SCALE, axis=-1
    )
    kernel_one_b = kernel_one.astype(BF16)
    output = jnp.einsum(
        "htl,hdl->thd", kernel_one_b, mixing, preferred_element_type=F32
    ).reshape(tok, width_dev)
    grad_float = out_grad.astype(F32)
    scaled_grad = grad_float * norm_gain
    sums = jnp.stack(
        [jnp.sum(output * output, axis=-1), jnp.sum(scaled_grad * output, axis=-1)]
    )
    sums = jnp.sum(spread(sums, "head"), axis=0)
    root_inv = lax.rsqrt(sums[0] / feature_total + EPS)[:, None]
    slope_dot = sums[1][:, None] * root_inv / feature_total
    normed = (output * root_inv * norm_gain).astype(BF16)
    d_output = (root_inv * (scaled_grad - output * (root_inv * slope_dot))).astype(BF16)
    local_gain = jnp.sum(grad_float * output * root_inv, axis=0)
    d3 = d_output.reshape(tok, heads, DH)

    local_mixing = jnp.einsum("thd,htl->hdl", d3, kernel_one_b, preferred_element_type=F32)
    gain_row = jnp.concatenate(high_low(local_gain.reshape(heads, 1, DH)), axis=2)
    gain_row = jnp.pad(gain_row, ((0, 0), (0, 7), (0, 0)))
    gain_row = jnp.broadcast_to(gain_row[:, None], (heads, per_head, 8, M))
    parts = jnp.concatenate(
        [local_mixing.reshape(heads, per_head, cols, M), gain_row], axis=2
    )
    got = exchange(parts.reshape(n_ctx, cols + 8, M).astype(BF16), "ctx").astype(F32)
    got = jnp.sum(got, axis=0)
    g_mixing = got[:cols]
    gain_high, gain_low = high_low(got[cols : cols + 1, :DH] + got[cols : cols + 1, DH:])

    g_kernel = jnp.einsum("thd,hdl->htl", d3, mixing, preferred_element_type=F32)
    g_sone = (
        kernel_one * (g_kernel - jnp.sum(kernel_one * g_kernel, axis=-1, keepdims=True))
    ).astype(BF16)
    query_one = jnp.einsum("htl,lhd->thd", g_sone, lk, preferred_element_type=F32) * SCALE
    keyland = jnp.einsum("htl,thd->hld", g_sone, q3, preferred_element_type=F32) * SCALE

    d_outer = (factor / 16.0) * exact(g_mixing, ktwo, (((1,), (1,)), ((), ())))
    d_inner, d_p0 = cubic_back(d_outer, saved_outer, p0)
    g_context, d_p1 = cubic_back(d_inner, saved_inner, p1)
    g_weighted = g_context / totals
    gt_high, gt_low = high_low(-jnp.sum(g_context * context, axis=0, keepdims=True) / totals)
    mine = jnp.concatenate(
        [
            g_weighted,
            gt_high,
            gt_low,
            jnp.concatenate([gain_high, gain_low], axis=1),
            top[None],
            jnp.zeros((4, M), F32),
        ],
        axis=0,
    )
    got = spread(mine.astype(BF16), "ctx").reshape(heads, per_head, cols + 8, M)
    g_weighted_b = got[:, :, :cols].reshape(heads, DH, M)
    rows = got[:, :, cols:].astype(F32)
    g_totals = jnp.sum(rows[:, :, 0] + rows[:, :, 1], axis=1)
    gain_grad = (rows[:, 0, 2, :DH] + rows[:, 0, 2, DH:]).reshape(width_dev)
    tops = rows[:, 0, 3]

    h1, h2, h3 = hs
    d_h3 = 0.25 * exact(p0, d_p1)
    d_h2 = -exact(p0, d_h3)
    d_h1 = -exact(p0, d_h2)
    d_p0 = d_p0 + 0.25 * exact(d_p1, h3) - exact(d_h3, h2) - exact(d_h2, h1) - d_h1
    d_ktwo = (factor / 16.0) * exact(
        outer, g_mixing, (((0,), (0,)), ((), ()))
    ) + factor * exact(d_p0 + d_p0.T, ktwo)
    g_stwo = ktwo * (d_ktwo - jnp.sum(ktwo * d_ktwo, axis=-1, keepdims=True))
    queryland_two = exact(g_stwo, my_lk.astype(F32)) * SCALE
    keyland_two = exact(g_stwo, my_lq.astype(F32), (((0,), (0,)), ((), ()))) * SCALE

    exp_three = jnp.exp(score_three - tops[:, None])
    g_exp = (
        jnp.einsum("thd,hdl->htl", v3, g_weighted_b, preferred_element_type=F32)
        + g_totals[:, None]
    )
    g_sthree = (exp_three * g_exp).astype(BF16)
    value_grad = (
        jnp.einsum(
            "htl,hdl->thd", exp_three.astype(BF16), g_weighted_b, preferred_element_type=F32
        )
        .astype(BF16)
        .reshape(tok, width_dev)
    )
    queryland = jnp.einsum("htl,thd->hld", g_sthree, k3, preferred_element_type=F32) * SCALE
    key_three = jnp.einsum("htl,lhd->thd", g_sthree, lq, preferred_element_type=F32) * SCALE

    mine_here = (jnp.arange(heads) == my_head)[:, None, None]
    queryland = queryland + jnp.where(mine_here, queryland_two[None], 0.0)
    keyland = keyland + jnp.where(mine_here, keyland_two[None], 0.0)
    both = jnp.concatenate([queryland, keyland], axis=0).astype(BF16)
    both = jnp.transpose(both, (1, 0, 2)).reshape(n_ctx, land_dev, 2 * width_dev)
    landed = jnp.sum(exchange(both, "ctx").astype(F32), axis=0) / seg_len

    def finish(per_token, per_land):
        total = per_token.reshape(land_dev, seg_len, width_dev) + per_land[:, None]
        return total.reshape(tok, width_dev).astype(BF16)

    query_grad = finish(query_one, landed[:, :width_dev])
    key_grad = finish(key_three, landed[:, width_dev:])
    return (normed, query_grad, key_grad, value_grad, gain_grad)


def solution(mesh):
    return jax.shard_map(
        on_device,
        mesh=mesh,
        in_specs=(
            P("ctx", "head"),
            P("ctx", "head"),
            P("ctx", "head"),
            P("head"),
            P("ctx", "head"),
        ),
        out_specs=(
            P("ctx", "head"),
            P("ctx", "head"),
            P("ctx", "head"),
            P("ctx", "head"),
            P("head"),
        ),
        check_vma=False,
    )
```

```python
import functools

import jax
import jax.numpy as jnp
from jax import lax
from jax.experimental import pallas as pl
from jax.experimental.pallas import tpu as pltpu
from jax.sharding import PartitionSpec as P

DH = 128
M = 256
EPS = 1e-06
F32 = jnp.float32
BF16 = jnp.bfloat16
SCALE = DH ** (-0.5)
VMEM_BYTES = 32 * 1024 * 1024

NN = (((1,), (0,)), ((), ()))
NT = (((1,), (1,)), ((), ()))
TN = (((0,), (0,)), ((), ()))


def dot(a, b, dims=NN):
    return lax.dot_general(a, b, dims, preferred_element_type=F32)


def exact(a, b, dims=NN):
    return lax.dot_general(
        a, b, dims, precision=lax.Precision.HIGHEST, preferred_element_type=F32
    )


def exchange(parts, axis):
    return lax.all_to_all(parts, axis, 0, 0)


def high_low(x):
    high = x.astype(BF16).astype(F32)
    return high, x - high


def rows_of(*rows):
    index = lax.broadcasted_iota(jnp.int32, (8, rows[0].shape[1]), 0)
    out = jnp.zeros((8, rows[0].shape[1]), F32)
    for place, row in enumerate(rows):
        out = jnp.where(index == place, row, out)
    return out


def eye_times(value):
    row = lax.broadcasted_iota(jnp.int32, (M, M), 0)
    col = lax.broadcasted_iota(jnp.int32, (M, M), 1)
    return jnp.where(row == col, value, 0.0).astype(F32)


def head_cols(h):
    return slice(h * DH, (h + 1) * DH)


def call(body, outs, *args, scalars=0, flops=0, name):
    nbytes = sum(a.size * a.dtype.itemsize for a in (*args, *outs))
    in_specs = [pl.BlockSpec(memory_space=pltpu.SMEM)] * scalars + [
        pl.BlockSpec(memory_space=pltpu.VMEM)
    ] * (len(args) - scalars)
    return pl.pallas_call(
        body,
        out_shape=outs,
        in_specs=in_specs,
        out_specs=[pl.BlockSpec(memory_space=pltpu.VMEM)] * len(outs),
        compiler_params=pltpu.CompilerParams(vmem_limit_bytes=VMEM_BYTES),
        cost_estimate=pl.CostEstimate(flops=flops, bytes_accessed=nbytes, transcendentals=0),
        name=name,
    )(*args)


def shape(*dims, dtype=F32):
    return jax.ShapeDtypeStruct(dims, dtype)


def means_body(q_ref, k_ref, out_ref):
    count, land_dev, both = out_ref.shape
    width = both // 2
    seg_len = q_ref.shape[0] // land_dev
    means = [
        jnp.sum(ref[...].astype(F32).reshape(land_dev, seg_len, width), axis=1) / seg_len
        for ref in (q_ref, k_ref)
    ]
    own = jnp.concatenate(means, axis=1).astype(BF16)
    for place in range(count):
        out_ref[place] = own


def context_body(land_ref, k_ref, v_ref, out_ref):
    count, rows, _ = out_ref.shape
    heads = k_ref.shape[1] // DH
    per_head = count // heads
    cols = DH // per_head
    for h in range(heads):
        score = dot(k_ref[:, head_cols(h)], land_ref[:, head_cols(h)], NT) * SCALE
        shift = jnp.max(score, axis=0, keepdims=True).astype(BF16).astype(F32)
        exp_local = jnp.exp(score - shift)
        high, low = high_low(jnp.sum(exp_local, axis=0, keepdims=True))
        weighted = dot(v_ref[:, head_cols(h)], exp_local.astype(BF16), TN)
        stats = rows_of(shift, high, low)
        for j in range(per_head):
            out_ref[h * per_head + j] = jnp.concatenate(
                [weighted[j * cols : (j + 1) * cols], stats], axis=0
            ).astype(BF16)


def inverse_body(head_ref, land_ref, out_ref, factor_ref):
    width = land_ref.shape[1] // 2
    at = pl.multiple_of(head_ref[0] * DH, DH)
    lq = land_ref[:, pl.ds(at, DH)]
    lk = land_ref[:, pl.ds(at + width, DH)]
    score = dot(lq, lk, NT) * SCALE
    top = jnp.exp(score - jnp.max(score, axis=1, keepdims=True))
    ktwo = top / jnp.sum(top, axis=1, keepdims=True)
    factor = 1.0 / jnp.max(jnp.sum(ktwo, axis=0, keepdims=True), axis=1, keepdims=True)
    x = factor * exact(ktwo, ktwo, NT)
    h2 = eye_times(15.0) - exact(x, eye_times(7.0) - x)
    h3 = eye_times(13.0) - exact(x, h2)
    p1 = 0.25 * exact(x, h3)
    b2 = eye_times(15.0) - exact(p1, eye_times(7.0) - p1)
    b3 = eye_times(13.0) - exact(p1, b2)
    out_ref[0] = (factor * 0.0625) * exact(b3, exact(h3, ktwo))
    out_ref[1] = ktwo
    out_ref[2] = x
    out_ref[3] = h2
    out_ref[4] = h3
    out_ref[5] = p1
    out_ref[6] = b2
    out_ref[7] = b3
    factor_ref[...] = jnp.broadcast_to(factor, (8, 128))


def mixing_body(got_ref, inv_ref, out_ref, ctx_ref, stat_ref):
    count, rows, _ = got_ref.shape
    cols = rows - 8
    top = got_ref[0].astype(F32)[cols:]
    for place in range(1, count):
        top = jnp.maximum(top, got_ref[place].astype(F32)[cols:])
    top = top[0:1]
    total = jnp.zeros((1, M), F32)
    weighted = jnp.zeros((cols, M), F32)
    for place in range(count):
        part = got_ref[place].astype(F32)
        fade = jnp.exp(part[cols : cols + 1] - top)
        total = total + fade * (part[cols + 1 : cols + 2] + part[cols + 2 : cols + 3])
        weighted = weighted + fade * part[:cols]
    context = weighted / total
    mixing = exact(context, inv_ref[0]).astype(BF16)
    for place in range(count):
        out_ref[place] = mixing
    ctx_ref[...] = context
    stat_ref[...] = rows_of(total, top)


def kernel_one_body(q_ref, land_ref, out_ref):
    heads = q_ref.shape[1] // DH
    for h in range(heads):
        score = dot(q_ref[:, head_cols(h)], land_ref[:, head_cols(heads + h)], NT) * SCALE
        top = jnp.exp(score - jnp.max(score, axis=1, keepdims=True))
        out_ref[h] = top / jnp.sum(top, axis=1, keepdims=True)


def output_body(kone_ref, mix_ref, og_ref, gain_ref, out_ref, sum_ref):
    heads = kone_ref.shape[0]
    tok = kone_ref.shape[1]
    squares = jnp.zeros((tok, DH), F32)
    slopes = jnp.zeros((tok, DH), F32)
    for h in range(heads):
        out = dot(kone_ref[h].astype(BF16), mix_ref[h], NT)
        out_ref[:, head_cols(h)] = out
        scaled = og_ref[:, head_cols(h)].astype(F32) * gain_ref[:, head_cols(h)]
        squares = squares + out * out
        slopes = slopes + scaled * out
    ones = jnp.ones((8, DH), F32)
    both = rows_of(exact(ones, squares, NT)[0:1], exact(ones, slopes, NT)[0:1])
    for place in range(sum_ref.shape[0]):
        sum_ref[place] = both[:2]


def norm_body(sum_ref, out_ref, og_ref, gain_ref, kone_ref, normed_ref, dout_ref, part_ref):
    heads, tok, _ = kone_ref.shape
    count, rows, _ = part_ref.shape
    per_head = count // heads
    cols = rows - 8
    features = heads * DH * sum_ref.shape[0]
    total = sum_ref[0]
    for place in range(1, sum_ref.shape[0]):
        total = total + sum_ref[place]
    root_inv = lax.rsqrt(total[0:1] / features + EPS)
    slope = total[1:2] * root_inv / features
    columns = jnp.transpose(rows_of(root_inv, root_inv * slope))
    root_inv = columns[:, 0:1]
    bent = columns[:, 1:2]
    for h in range(heads):
        gain = gain_ref[:, head_cols(h)]
        out = out_ref[:, head_cols(h)]
        grad = og_ref[:, head_cols(h)].astype(F32)
        straight = out * root_inv
        normed_ref[:, head_cols(h)] = (straight * gain).astype(BF16)
        d_out = (root_inv * (grad * gain - out * bent)).astype(BF16)
        dout_ref[:, head_cols(h)] = d_out
        g_mixing = dot(d_out, kone_ref[h].astype(BF16), TN)
        high, low = high_low(jnp.sum(grad * straight, axis=0, keepdims=True))
        gain_rows = rows_of(jnp.concatenate([high, low], axis=1))
        for j in range(per_head):
            part_ref[h * per_head + j] = jnp.concatenate(
                [g_mixing[j * cols : (j + 1) * cols], gain_rows], axis=0
            ).astype(BF16)


def query_body(dout_ref, mix_ref, kone_ref, q_ref, land_ref, query_ref, keyland_ref):
    heads = kone_ref.shape[0]
    for h in range(heads):
        g_kernel = dot(dout_ref[:, head_cols(h)], mix_ref[h])
        kone = kone_ref[h]
        inner = jnp.sum(kone * g_kernel, axis=1, keepdims=True)
        g_score = (kone * (g_kernel - inner)).astype(BF16)
        query_ref[:, head_cols(h)] = dot(g_score, land_ref[:, head_cols(heads + h)]) * SCALE
        keyland_ref[:, head_cols(h)] = dot(g_score, q_ref[:, head_cols(h)], TN) * SCALE


def grad_context_body(got_ref, inv_ref, ctx_ref, stat_ref, out_ref, g_ref):
    count, rows, _ = got_ref.shape
    cols = rows - 8
    got = got_ref[0].astype(F32)
    for place in range(1, count):
        got = got + got_ref[place].astype(F32)
    g_mixing = got[:cols]
    gain = got[cols : cols + 1]
    gain_high, gain_low = high_low(gain[:, :DH] + gain[:, DH:])
    total = stat_ref[0:1]
    g_context = exact(g_mixing, inv_ref[0], NT)
    high, low = high_low(-jnp.sum(g_context * ctx_ref[...], axis=0, keepdims=True) / total)
    tail = rows_of(high, low, jnp.concatenate([gain_high, gain_low], axis=1), stat_ref[1:2])
    mine = jnp.concatenate([g_context / total, tail], axis=0).astype(BF16)
    for place in range(count):
        out_ref[place] = mine
    g_ref[...] = g_mixing


def inverse_back_body(head_ref, inv_ref, factor_ref, ctx_ref, g_ref, land_ref, ql_ref, kl_ref):
    width = land_ref.shape[1] // 2
    at = pl.multiple_of(head_ref[0] * DH, DH)
    lq = land_ref[:, pl.ds(at, DH)].astype(F32)
    lk = land_ref[:, pl.ds(at + width, DH)].astype(F32)
    factor = factor_ref[0:1, 0:1]
    ktwo, x, h2, h3, p1, b2, b3 = [inv_ref[place] for place in range(1, 8)]
    context = ctx_ref[...]
    g_mixing = g_ref[...]
    inner = exact(context, b3)
    outer = exact(inner, h3)
    d_outer = (factor * 0.0625) * exact(g_mixing, ktwo, NT)
    d_inner = exact(d_outer, h3)
    d_b3 = exact(context, d_inner, TN)
    d_b2 = -exact(p1, d_b3)
    d_b1 = -exact(p1, d_b2)
    d_p1 = -exact(d_b3, b2) - exact(d_b2, eye_times(7.0) - p1) - d_b1
    d_h3 = exact(inner, d_outer, TN) + 0.25 * exact(x, d_p1)
    d_h2 = -exact(x, d_h3)
    d_h1 = -exact(x, d_h2)
    d_x = 0.25 * exact(d_p1, h3) - exact(d_h3, h2) - exact(d_h2, eye_times(7.0) - x) - d_h1
    d_ktwo = (factor * 0.0625) * exact(outer, g_mixing, TN) + factor * exact(
        d_x + jnp.transpose(d_x), ktwo
    )
    g_score = ktwo * (d_ktwo - jnp.sum(ktwo * d_ktwo, axis=1, keepdims=True))
    ql_ref[...] = exact(g_score, lk) * SCALE
    kl_ref[...] = exact(g_score, lq, TN) * SCALE


def three_back(got_ref, land_ref, k_ref, v_ref, h):
    count, rows, _ = got_ref.shape
    cols = rows - 8
    per_head = DH // cols
    parts = [got_ref[h * per_head + j] for j in range(per_head)]
    g_weighted = jnp.concatenate([part[:cols] for part in parts], axis=0)
    tails = [part.astype(F32)[cols:] for part in parts]
    summed = functools.reduce(jnp.add, tails)
    g_totals = summed[0:1] + summed[1:2]
    top = tails[0][3:4]
    score = dot(k_ref[:, head_cols(h)], land_ref[:, head_cols(h)], NT) * SCALE
    exp_three = jnp.exp(score - top)
    g_exp = dot(v_ref[:, head_cols(h)], g_weighted) + g_totals
    return g_weighted, exp_three, (exp_three * g_exp).astype(BF16)


def queryland_body(
    head_ref, got_ref, land_ref, k_ref, v_ref, keyland_ref, ql_ref, kl_ref, out_ref
):
    heads = k_ref.shape[1] // DH
    for h in range(heads):
        g_score = three_back(got_ref, land_ref, k_ref, v_ref, h)[2]
        queryland = dot(g_score, k_ref[:, head_cols(h)], TN) * SCALE
        mine = (head_ref[0] == h).astype(F32)
        out_ref[:, head_cols(h)] = (queryland + mine * ql_ref[...]).astype(BF16)
        out_ref[:, head_cols(heads + h)] = (
            keyland_ref[:, head_cols(h)] + mine * kl_ref[...]
        ).astype(BF16)


def value_body(got_ref, land_ref, k_ref, v_ref, value_ref, key_ref, gain_ref):
    count, rows, _ = got_ref.shape
    cols = rows - 8
    heads = k_ref.shape[1] // DH
    per_head = count // heads
    for h in range(heads):
        g_weighted, exp_three, g_score = three_back(got_ref, land_ref, k_ref, v_ref, h)
        value_ref[:, head_cols(h)] = dot(exp_three.astype(BF16), g_weighted, NT).astype(BF16)
        key_ref[:, head_cols(h)] = dot(g_score, land_ref[:, head_cols(h)]) * SCALE
        gain = got_ref[h * per_head].astype(F32)[cols + 2 : cols + 3]
        gain_ref[:, head_cols(h)] = gain[:, :DH] + gain[:, DH:]


def finish_body(got_ref, query_ref, key_ref, query_out, key_out):
    count, land_dev, both = got_ref.shape
    tok, width = query_ref.shape
    seg_len = tok // land_dev
    got = got_ref[0].astype(F32)
    for place in range(1, count):
        got = got + got_ref[place].astype(F32)
    got = got / seg_len
    for ref, out, land in (
        (query_ref, query_out, got[:, :width]),
        (key_ref, key_out, got[:, width:]),
    ):
        for row in range(land_dev):
            span = slice(row * seg_len, (row + 1) * seg_len)
            out[span] = (ref[span] + land[row : row + 1]).astype(BF16)


def on_device(queries, keys_in, values, norm_gain, out_grad):
    tok, width = queries.shape
    heads = width // DH
    n_ctx = lax.axis_size("ctx")
    n_head = lax.axis_size("head")
    per_head = n_ctx // heads
    cols = DH // per_head
    land_dev = M // n_ctx
    my_head = (lax.axis_index("ctx") // per_head).astype(jnp.int32).reshape(1)
    gain = norm_gain.reshape(1, width)
    packed = shape(n_ctx, cols + 8, M, dtype=BF16)
    wide = shape(tok, width)
    wide_b = shape(tok, width, dtype=BF16)

    (own,) = call(
        means_body, [shape(n_ctx, land_dev, 2 * width, dtype=BF16)], queries, keys_in,
        flops=10**6, name="landmark_means",
    )
    land = exchange(own, "ctx").reshape(M, 2 * width)

    (parts,) = call(
        context_body, [packed], land, keys_in, values, flops=10**8, name="local_context"
    )
    got = exchange(parts, "ctx")
    inverse, factor = call(
        inverse_body, [shape(8, M, M), shape(8, 128)], my_head, land,
        scalars=1, flops=3 * 10**9, name="inverse",
    )
    (kernel_one,) = call(
        kernel_one_body, [shape(heads, tok, M)], queries, land, flops=10**9, name="kernel_one"
    )
    parts, context, stats = call(
        mixing_body, [shape(n_ctx, cols, M, dtype=BF16), shape(cols, M), shape(8, M)],
        got, inverse, flops=10**8, name="mixing",
    )
    mixing = exchange(parts, "ctx").reshape(heads, DH, M)

    output, sums = call(
        output_body, [wide, shape(n_head, 2, tok)], kernel_one, mixing, out_grad, gain,
        flops=10**8, name="output",
    )
    sums = exchange(sums, "head")
    normed, d_output, parts = call(
        norm_body, [wide_b, wide_b, packed], sums, output, out_grad, gain, kernel_one,
        flops=10**8, name="norm",
    )
    got = exchange(parts, "ctx")
    query_one, keyland = call(
        query_body, [wide, shape(M, width)], d_output, mixing, kernel_one, queries, land,
        flops=2 * 10**9, name="kernel_one_back",
    )
    parts, g_mixing = call(
        grad_context_body, [packed, shape(cols, M)], got, inverse, context, stats,
        flops=10**8, name="context_back",
    )
    got = exchange(parts, "ctx")
    ql_two, kl_two = call(
        inverse_back_body, [shape(M, DH), shape(M, DH)],
        my_head, inverse, factor, context, g_mixing, land,
        scalars=1, flops=5 * 10**9, name="inverse_back",
    )
    (both,) = call(
        queryland_body, [shape(M, 2 * width, dtype=BF16)],
        my_head, got, land, keys_in, values, keyland, ql_two, kl_two,
        scalars=1, flops=10**8, name="landmarks_back",
    )
    landed = exchange(both.reshape(n_ctx, land_dev, 2 * width), "ctx")
    value_grad, key_three, gain_grad = call(
        value_body, [wide_b, wide, shape(1, width)], got, land, keys_in, values,
        flops=2 * 10**9, name="kernel_three_back",
    )
    query_grad, key_grad = call(
        finish_body, [wide_b, wide_b], landed, query_one, key_three, flops=10**6, name="finish"
    )
    return (normed, query_grad, key_grad, value_grad, gain_grad.reshape(width))


def solution(mesh):
    return jax.shard_map(
        on_device,
        mesh=mesh,
        in_specs=(
            P("ctx", "head"),
            P("ctx", "head"),
            P("ctx", "head"),
            P("head"),
            P("ctx", "head"),
        ),
        out_specs=(
            P("ctx", "head"),
            P("ctx", "head"),
            P("ctx", "head"),
            P("ctx", "head"),
            P("head"),
        ),
        check_vma=False,
    )
```

```python
import functools

import jax
import jax.numpy as jnp
from jax import lax
from jax.experimental import pallas as pl
from jax.experimental.pallas import tpu as pltpu
from jax.sharding import PartitionSpec as P

DH = 128
M = 256
EPS = 1e-06
F32 = jnp.float32
BF16 = jnp.bfloat16
SCALE = DH ** (-0.5)
VMEM_BYTES = 32 * 1024 * 1024
MOST_VMEM = 60 * 1024 * 1024
HALVES = (slice(0, DH), slice(DH, 2 * DH))

NN = (((1,), (0,)), ((), ()))
NT = (((1,), (1,)), ((), ()))
TN = (((0,), (0,)), ((), ()))


def dot(a, b, dims=NN):
    return lax.dot_general(a, b, dims, preferred_element_type=F32)


def split_up(x):
    high = x.astype(BF16)
    return high, (x - high.astype(F32)).astype(BF16)


def exact(a, b, dims=NN):
    a_high, a_low = a if isinstance(a, tuple) else split_up(a)
    b_high, b_low = b if isinstance(b, tuple) else split_up(b)
    return dot(a_high, b_high, dims) + (dot(a_high, b_low, dims) + dot(a_low, b_high, dims))


def exchange(parts, axis, groups=None):
    return lax.all_to_all(parts, axis, 0, 0, axis_index_groups=groups)


def high_low(x):
    high = x.astype(BF16).astype(F32)
    return high, x - high


def rows_of(*rows):
    index = lax.broadcasted_iota(jnp.int32, (8, rows[0].shape[1]), 0)
    out = jnp.zeros((8, rows[0].shape[1]), F32)
    for place, row in enumerate(rows):
        out = jnp.where(index == place, row, out)
    return out


def eye_times(value):
    row = lax.broadcasted_iota(jnp.int32, (M, M), 0)
    col = lax.broadcasted_iota(jnp.int32, (M, M), 1)
    return jnp.where(row == col, value, 0.0).astype(F32)


def head_cols(h):
    return slice(h * DH, (h + 1) * DH)


def halves(x):
    return jnp.concatenate([x[:, :DH], x[:, DH:]], axis=0)


def joined(x):
    n = x.shape[0] // 2
    return jnp.concatenate([x[:n], x[n:]], axis=1)


def own_head(ids_ref, h):
    return pl.ds(pl.multiple_of((ids_ref[0] * 2 + h) * DH, DH), DH)


def stacked(ids_ref, refs, h):
    return jnp.concatenate([ref[:, own_head(ids_ref, h)] for ref in refs], axis=0)


def rows_of(*rows):
    index = lax.broadcasted_iota(jnp.int32, (8, rows[0].shape[1]), 0)
    out = jnp.zeros((8, rows[0].shape[1]), F32)
    for place, row in enumerate(rows):
        out = jnp.where(index == place, row, out)
    return out


def eye_times(value):
    row = lax.broadcasted_iota(jnp.int32, (M, M), 0)
    col = lax.broadcasted_iota(jnp.int32, (M, M), 1)
    return jnp.where(row == col, value, 0.0).astype(F32)


def head_cols(h):
    return slice(h * DH, (h + 1) * DH)


def halves(x):
    return jnp.concatenate([x[:, :DH], x[:, DH:]], axis=0)


def joined(x):
    n = x.shape[0] // 2
    return jnp.concatenate([x[:n], x[n:]], axis=1)


def both_blocks(mine_ref, other_ref, which, h):
    return jnp.concatenate(
        [ref[which, :, head_cols(h)] for ref in (mine_ref, other_ref)], axis=0
    )


def call(
    body, outs, *args, scalars=0, far_in=(), far_out=(), after=(), flops=0,
    vmem=VMEM_BYTES, name
):
    nbytes = sum(a.size * a.dtype.itemsize for a in (*args, *outs))
    n_in, n_after, n_out = len(args), len(after), len(outs)
    n_far = len(far_in) + len(far_out)

    def whole(*refs):
        ins = list(refs[:n_in])
        results = list(refs[n_in + n_after : n_in + n_after + n_out])
        buffers = refs[n_in + n_after + n_out :]
        loads, stores = [], []
        for k, i in enumerate(far_in):
            loads.append(pltpu.make_async_copy(ins[i], buffers[k], buffers[n_far].at[k]))
            ins[i] = buffers[k]
        for k, i in enumerate(far_out, len(far_in)):
            stores.append(
                pltpu.make_async_copy(buffers[k], results[i], buffers[n_far].at[k])
            )
            results[i] = buffers[k]
        for copy in loads:
            copy.start()
        for copy in loads:
            copy.wait()
        body(*ins, *results)
        for copy in stores:
            copy.start()
        for copy in stores:
            copy.wait()

    def space(place, far):
        return pl.BlockSpec(memory_space=pltpu.HBM if place in far else pltpu.VMEM)

    in_specs = [
        pl.BlockSpec(memory_space=pltpu.SMEM) if i < scalars else space(i, far_in)
        for i in range(n_in)
    ] + [pl.BlockSpec(memory_space=pl.ANY)] * n_after
    scratch = [pltpu.VMEM(args[i].shape, args[i].dtype) for i in far_in]
    scratch += [pltpu.VMEM(outs[i].shape, outs[i].dtype) for i in far_out]
    if n_far:
        scratch.append(pltpu.SemaphoreType.DMA((n_far,)))
    return pl.pallas_call(
        whole,
        out_shape=outs,
        in_specs=in_specs,
        out_specs=[space(i, far_out) for i in range(n_out)],
        scratch_shapes=scratch,
        compiler_params=pltpu.CompilerParams(vmem_limit_bytes=vmem),
        cost_estimate=pl.CostEstimate(flops=flops, bytes_accessed=nbytes, transcendentals=0),
        name=name,
    )(*args, *after)


def shape(*dims, dtype=F32):
    return jax.ShapeDtypeStruct(dims, dtype)


def means_body(q_ref, k_ref, out_ref):
    count, land_dev, both = out_ref.shape
    half = both // 2
    seg_len = q_ref.shape[0] // land_dev
    q_mean, k_mean = [
        jnp.sum(ref[...].astype(F32).reshape(land_dev, seg_len, 2 * half), axis=1) / seg_len
        for ref in (q_ref, k_ref)
    ]
    for core in range(2):
        cols = slice(core * half, (core + 1) * half)
        own = jnp.concatenate([q_mean[:, cols], k_mean[:, cols]], axis=1).astype(BF16)
        for chip in range(count // 2):
            out_ref[2 * chip + core] = own


def stack_body(ids_ref, *refs):
    count = len(refs) // 3
    for mine, there, out in zip(refs[:count], refs[count : 2 * count], refs[2 * count :]):
        for h in range(out.shape[1] // DH):
            out[:, head_cols(h)] = stacked(ids_ref, (mine, there), h)


def context_body(land_ref, k_ref, v_ref, out_ref):
    count = out_ref.shape[0]
    heads = land_ref.shape[1] // (2 * DH)
    per_head = count // heads
    cols = DH // per_head
    for h in range(heads):
        keys = k_ref[:, head_cols(h)]
        vals = v_ref[:, head_cols(h)]
        score = dot(keys, land_ref[:, head_cols(h)], NT) * SCALE
        shift = jnp.max(score, axis=0, keepdims=True).astype(BF16).astype(F32)
        exp_local = jnp.exp(score - shift)
        high, low = high_low(jnp.sum(exp_local, axis=0, keepdims=True))
        weighted = dot(vals, exp_local.astype(BF16), TN)
        stats = rows_of(*[row[:, part] for row in (shift, high, low) for part in HALVES])
        for j in range(per_head):
            out_ref[h * per_head + j] = jnp.concatenate(
                [halves(weighted[j * cols : (j + 1) * cols]), stats], axis=0
            ).astype(BF16)


def inverse_body(ids_ref, land_ref, first_ref, again_ref, out_ref):
    half = land_ref.shape[1] // 2
    at = pl.multiple_of(ids_ref[1] * DH, DH)
    lq = land_ref[:, pl.ds(at, DH)]
    lk = land_ref[:, pl.ds(at + half, DH)]
    score = dot(lq, lk, NT) * SCALE
    top = jnp.exp(score - jnp.max(score, axis=1, keepdims=True))
    ktwo = top / jnp.sum(top, axis=1, keepdims=True)
    factor = column_factor(ktwo)
    ktwo_s = split_up(ktwo)
    x = factor * exact(ktwo_s, ktwo_s, NT)
    x_s = split_up(x)
    h2 = eye_times(15.0) - exact(x_s, eye_times(7.0) - x)
    h3 = eye_times(13.0) - exact(x_s, h2)
    h3_s = split_up(h3)
    p1 = 0.25 * exact(x_s, h3_s)
    p1_s = split_up(p1)
    b2 = eye_times(15.0) - exact(p1_s, eye_times(7.0) - p1)
    b3 = eye_times(13.0) - exact(p1_s, b2)
    inverse = (factor * 0.0625) * exact(b3, exact(h3_s, ktwo_s))
    first_ref[...] = inverse
    again_ref[...] = inverse
    for place, part in enumerate((ktwo, x, h2, h3, p1, b2, b3)):
        out_ref[place] = part


def column_factor(ktwo):
    return 1.0 / jnp.max(jnp.sum(ktwo, axis=0, keepdims=True), axis=1, keepdims=True)


def mixing_body(got_ref, inv_ref, out_ref, kept_ref):
    count, rows, _ = got_ref.shape
    cols = (rows - 8) // 2
    tops = got_ref[0].astype(F32)[rows - 8 :]
    for place in range(1, count):
        tops = jnp.maximum(tops, got_ref[place].astype(F32)[rows - 8 :])
    tops = tops[0:2]
    total = jnp.zeros((2, DH), F32)
    left = jnp.zeros((cols, DH), F32)
    right = jnp.zeros((cols, DH), F32)
    for place in range(count):
        part = got_ref[place].astype(F32)
        stats = part[rows - 8 :]
        fade = jnp.exp(stats[0:2] - tops)
        total = total + fade * (stats[2:4] + stats[4:6])
        left = left + fade[0:1] * part[:cols]
        right = right + fade[1:2] * part[cols : 2 * cols]
    total = joined(total)
    context = jnp.concatenate([left, right], axis=1) / total
    mixing = exact(context, inv_ref[...]).astype(BF16)
    for place in range(count):
        out_ref[place] = mixing
    kept_ref[...] = jnp.concatenate([context, rows_of(total, joined(tops))], axis=0)


def softmax_rows(score):
    top = jnp.exp(score - jnp.max(score, axis=1, keepdims=True))
    return top / jnp.sum(top, axis=1, keepdims=True)


def kernel_one(q_ref, land_ref, h):
    heads = land_ref.shape[1] // (2 * DH)
    score = dot(q_ref[:, head_cols(h)], land_ref[:, head_cols(heads + h)], NT) * SCALE
    return softmax_rows(score)


def ahead_body(
    q_ref, k_ref, land_ref, first_ref, again_ref, exp_ref
):
    heads, tok, _ = first_ref.shape
    for h in range(heads):
        kone = kernel_one(q_ref, land_ref, h).astype(BF16)
        first_ref[h] = kone
        again_ref[h] = kone
        keys = k_ref[:, head_cols(h)]
        score = dot(keys, land_ref[:, head_cols(h)], NT) * SCALE
        shift = jnp.max(score, axis=0, keepdims=True)
        exp_ref[h, :tok] = jnp.exp(score - shift)
        exp_ref[h, tok:] = rows_of(shift)


def output_body(ids_ref, kone_ref, mix_ref, g_ref, gain_ref, out_ref, sum_ref):
    heads, tok, _ = kone_ref.shape
    squares = jnp.zeros((tok, DH), F32)
    slopes = jnp.zeros((tok, DH), F32)
    for h in range(heads):
        out = dot(kone_ref[h], mix_ref[h], NT)
        out_ref[:, head_cols(h)] = out
        grad = g_ref[:, head_cols(h)].astype(F32)
        squares = squares + out * out
        slopes = slopes + grad * gain_ref[:, own_head(ids_ref, h)] * out
    high, low = split_up(jnp.concatenate([squares, slopes], axis=0))
    ones = jnp.ones((8, DH), BF16)
    row = (dot(ones, high, NT) + dot(ones, low, NT))[0:1]
    both = rows_of(
        swap_blocks(ids_ref, row[:, :tok], 1), swap_blocks(ids_ref, row[:, tok:], 1)
    )
    for place in range(sum_ref.shape[0]):
        sum_ref[place] = both[:2]


def swap_blocks(ids_ref, x, axis):
    size = x.shape[axis] // 2
    left = lax.slice_in_dim(x, 0, size, axis=axis)
    right = lax.slice_in_dim(x, size, 2 * size, axis=axis)
    swapped = jnp.concatenate([right, left], axis=axis)
    return jnp.where(ids_ref[0] == 0, x, swapped)


def token_factors(ids_ref, sum_ref, features):
    total = sum_ref[0]
    for place in range(1, sum_ref.shape[0]):
        total = total + sum_ref[place]
    root_inv = lax.rsqrt(total[0:1] / features + EPS)
    slope = total[1:2] * root_inv / features
    columns = jnp.transpose(
        rows_of(
            swap_blocks(ids_ref, root_inv, 1), swap_blocks(ids_ref, root_inv * slope, 1)
        )
    )
    return columns[:, 0:1], columns[:, 1:2]


def output_grad(factors, out, grad, gain):
    root_inv, bent = factors
    return (root_inv * (grad * gain - out * bent)).astype(BF16)


def norm_body(ids_ref, sum_ref, out_ref, g_ref, gain_ref, kone_ref, part_ref):
    heads = kone_ref.shape[0]
    per_head = part_ref.shape[0] // heads
    cols = DH // per_head
    factors = token_factors(ids_ref, sum_ref, heads * DH * sum_ref.shape[0])
    for h in range(heads):
        out = out_ref[:, head_cols(h)]
        grad = g_ref[:, head_cols(h)].astype(F32)
        gain = gain_ref[:, own_head(ids_ref, h)]
        g_mixing = dot(output_grad(factors, out, grad, gain), kone_ref[h], TN)
        gain_sum = jnp.sum(grad * (out * factors[0]), axis=0, keepdims=True)
        tail = rows_of(*high_low(gain_sum))
        for j in range(per_head):
            part_ref[h * per_head + j] = jnp.concatenate(
                [halves(g_mixing[j * cols : (j + 1) * cols]), tail], axis=0
            ).astype(BF16)


def query_body(
    ids_ref, sum_ref, out_ref, g_ref, gain_ref, mix_ref, q_ref, land_ref,
    norm_mine, norm_other, query_mine, query_other, keyland_ref,
):
    heads = mix_ref.shape[0]
    tok = norm_mine.shape[0]
    factors = token_factors(ids_ref, sum_ref, heads * DH * sum_ref.shape[0])
    for h in range(heads):
        out = out_ref[:, head_cols(h)]
        grad = g_ref[:, head_cols(h)].astype(F32)
        gain = gain_ref[:, own_head(ids_ref, h)]
        normed = (out * factors[0] * gain).astype(BF16)
        norm_mine[:, head_cols(h)] = normed[:tok]
        norm_other[:, head_cols(h)] = normed[tok:]
        kone = kernel_one(q_ref, land_ref, h)
        g_kernel = dot(output_grad(factors, out, grad, gain), mix_ref[h])
        inner = jnp.sum(kone * g_kernel, axis=1, keepdims=True)
        g_score = (kone * (g_kernel - inner)).astype(BF16)
        query = dot(g_score, land_ref[:, head_cols(heads + h)]) * SCALE
        query_mine[:, head_cols(h)] = query[:tok]
        query_other[:, head_cols(h)] = query[tok:]
        queries = q_ref[:, head_cols(h)]
        keyland_ref[:, head_cols(h)] = dot(g_score, queries, TN) * SCALE


def grad_context_body(got_ref, inv_ref, kept_ref, out_ref, g_ref):
    count, rows, _ = got_ref.shape
    cols = (rows - 8) // 2
    got = got_ref[0].astype(F32)
    for place in range(1, count):
        got = got + got_ref[place].astype(F32)
    g_mixing = joined(got[: 2 * cols])
    gain = high_low(got[2 * cols : 2 * cols + 1] + got[2 * cols + 1 : 2 * cols + 2])
    context = kept_ref[:cols]
    total = kept_ref[cols : cols + 1]
    top = kept_ref[cols + 1 : cols + 2]
    g_context = exact(g_mixing, inv_ref[...], NT)
    high, low = high_low(-jnp.sum(g_context * context, axis=0, keepdims=True) / total)
    tail = rows_of(
        *[row[:, part] for row in (high, low) for part in HALVES],
        *gain,
        *[top[:, part] for part in HALVES],
    )
    mine = jnp.concatenate([halves(g_context / total), tail], axis=0).astype(BF16)
    for place in range(count):
        out_ref[place] = mine
    g_ref[...] = g_mixing


def inverse_back_body(ids_ref, inv_ref, kept_ref, g_ref, land_ref, keyland_ref, out_ref):
    half = land_ref.shape[1] // 2
    at = pl.multiple_of(ids_ref[1] * DH, DH)
    lq = land_ref[:, pl.ds(at, DH)]
    lk = land_ref[:, pl.ds(at + half, DH)]
    ktwo, x, h2, h3, p1, b2, b3 = [inv_ref[place] for place in range(7)]
    factor = column_factor(ktwo)
    ktwo_s, x_s, h3_s, p1_s, b3_s = [split_up(part) for part in (ktwo, x, h3, p1, b3)]
    g_mixing = split_up(g_ref[...])
    context = split_up(kept_ref[: g_ref.shape[0]])
    inner = split_up(exact(context, b3_s))
    outer = exact(inner, h3_s)
    d_outer = split_up((factor * 0.0625) * exact(g_mixing, ktwo_s, NT))
    d_inner = exact(d_outer, h3_s)
    d_b3 = split_up(exact(context, d_inner, TN))
    d_b2 = split_up(-exact(p1_s, d_b3))
    d_b1 = -exact(p1_s, d_b2)
    d_p1 = -exact(d_b3, b2) - exact(d_b2, eye_times(7.0) - p1) - d_b1
    d_p1 = split_up(d_p1)
    d_h3 = split_up(exact(inner, d_outer, TN) + 0.25 * exact(x_s, d_p1))
    d_h2 = split_up(-exact(x_s, d_h3))
    d_h1 = -exact(x_s, d_h2)
    d_x = 0.25 * exact(d_p1, h3_s) - exact(d_h3, h2) - exact(d_h2, eye_times(7.0) - x) - d_h1
    d_ktwo = (factor * 0.0625) * exact(outer, g_mixing, TN) + factor * exact(
        d_x + jnp.transpose(d_x), ktwo_s
    )
    g_score = ktwo * (d_ktwo - jnp.sum(ktwo * d_ktwo, axis=1, keepdims=True))
    out_ref[:, :half] = jnp.zeros((M, half), F32)
    out_ref[:, half:] = keyland_ref[...]
    high, low = split_up(g_score)
    out_ref[:, pl.ds(at, DH)] = (dot(high, lk) + dot(low, lk)) * SCALE
    out_ref[:, pl.ds(at + half, DH)] = keyland_ref[:, pl.ds(at, DH)] + (
        (dot(high, lq, TN) + dot(low, lq, TN)) * SCALE
    )


def unpacked(got_ref, h, heads):
    count, rows, _ = got_ref.shape
    per_head = count // heads
    cols = (rows - 8) // 2
    parts = [got_ref[h * per_head + j] for j in range(per_head)]
    g_weighted = jnp.concatenate(
        [
            jnp.concatenate([part[:cols], part[cols : 2 * cols]], axis=1)
            for part in parts
        ],
        axis=0,
    )
    tails = [part.astype(F32)[2 * cols :] for part in parts]
    summed = functools.reduce(jnp.add, tails)
    g_totals = joined(summed[0:2] + summed[2:4])
    top = joined(tails[0][6:8])
    gain = tails[0][4:5] + tails[0][5:6]
    return g_weighted, g_totals, top, gain


def queryland_body(got_ref, exp_ref, k_ref, v_ref, extra_ref, out_ref, again_ref):
    heads = exp_ref.shape[0]
    half = heads * DH
    for h in range(heads):
        g_weighted, g_totals, top, _ = unpacked(got_ref, h, heads)
        keys = k_ref[:, head_cols(h)]
        vals = v_ref[:, head_cols(h)]
        tok = keys.shape[0]
        exp_three = exp_ref[h, :tok] * jnp.exp(exp_ref[h, tok : tok + 1] - top)
        g_score = (exp_three * (dot(vals, g_weighted) + g_totals)).astype(BF16)
        queryland = dot(g_score, keys, TN) * SCALE
        out_ref[:, head_cols(h)] = (queryland + extra_ref[:, head_cols(h)]).astype(BF16)
    out_ref[:, half:] = extra_ref[:, half:].astype(BF16)
    again_ref[...] = got_ref[...]


def value_body(
    ids_ref, k_ref, v_ref, land_ref, land_there, got_ref, got_there,
    value_out, key_out, gain_out,
):
    heads = land_ref.shape[1] // (2 * DH)

    def place_halves(core, own, away):
        for place, land, got in ((own, land_ref, got_ref), (away, land_there, got_there)):
            for h in range(heads):
                cols = slice(place.start + h * DH, place.start + (h + 1) * DH)
                g_weighted, g_totals, top, gain = unpacked(got, h, heads)
                lq = land[:, head_cols(h)]
                exp_three = jnp.exp(dot(k_ref[:, cols], lq, NT) * SCALE - top)
                g_exp = dot(v_ref[:, cols], g_weighted) + g_totals
                value_out[:, cols] = dot(exp_three.astype(BF16), g_weighted, NT).astype(BF16)
                key_out[:, cols] = dot((exp_three * g_exp).astype(BF16), lq) * SCALE
                gain_out[:, cols] = gain

    by_core(ids_ref, place_halves)


def by_core(ids_ref, place_halves):
    half = 2 * DH
    left, right = slice(0, half), slice(half, 2 * half)

    @pl.when(ids_ref[0] == 0)
    def _():
        place_halves(0, left, right)

    @pl.when(ids_ref[0] != 0)
    def _():
        place_halves(1, right, left)


def gather_body(ids_ref, norm_mine, norm_there, norm_out):
    def place_halves(core, own, away):
        norm_out[:, own] = norm_mine[...]
        norm_out[:, away] = norm_there[...]

    by_core(ids_ref, place_halves)


def finish_body(
    ids_ref, got_ref, query_mine, query_there, key_ref, query_out, key_out
):
    count, land_dev, both = got_ref.shape
    tok, half = query_mine.shape
    seg_len = tok // land_dev
    lands = []
    for core in range(2):
        got = got_ref[core].astype(F32)
        for chip in range(1, count // 2):
            got = got + got_ref[2 * chip + core].astype(F32)
        lands.append(got / seg_len)
    spans = [(row, slice(row * seg_len, (row + 1) * seg_len)) for row in range(land_dev)]

    def place_halves(core, own, away):
        for place, land, ref in (
            (own, lands[core], query_mine), (away, lands[1 - core], query_there)
        ):
            for row, span in spans:
                query_out[span, place] = (ref[span] + land[row : row + 1, :half]).astype(BF16)

    by_core(ids_ref, place_halves)
    for core in range(2):
        place = slice(core * half, (core + 1) * half)
        for row, span in spans:
            key_out[span, place] = (
                key_ref[span, place] + lands[core][row : row + 1, half:]
            ).astype(BF16)


def on_device(queries, keys_in, values, norm_gain, out_grad):
    tok, width = queries.shape
    half = width // 2
    heads = half // DH
    n_ctx = lax.axis_size("ctx")
    n_head = lax.axis_size("head")
    chips = n_ctx // 2
    per_head = chips // heads
    cols = DH // per_head
    land_dev = M // n_ctx
    here = lax.axis_index("ctx").astype(jnp.int32)
    ids = jnp.stack([lax.rem(here, 2), lax.div(here, 2 * per_head)])
    gain = norm_gain.reshape(1, width)
    same_core = [list(range(core, n_ctx, 2)) for core in range(2)]
    same_chip = [
        [(2 * chip + core) * n_head + z for core in range(2) for z in range(n_head)]
        for chip in range(chips)
    ]
    swap = [(i, i ^ 1) for i in range(n_ctx)]
    packed = shape(chips, 2 * cols + 8, DH, dtype=BF16)
    block = shape(tok, half)
    block_b = shape(tok, half, dtype=BF16)
    wide_b = shape(tok, width, dtype=BF16)
    units = shape(heads, 2 * tok, M, dtype=BF16)

    both_b = shape(2 * tok, half, dtype=BF16)
    k_there, v_there, q_there, g_there = [
        lax.ppermute(x, "ctx", swap) for x in (keys_in, values, queries, out_grad)
    ]
    (own,) = call(
        means_body, [shape(n_ctx, land_dev, 2 * half, dtype=BF16)], queries, keys_in,
        far_in=(0, 1), far_out=(0,), vmem=MOST_VMEM, flops=10**6, name="landmark_means",
    )
    land = exchange(own, "ctx").reshape(M, 2 * half)
    keys, vals = call(
        stack_body, [both_b, both_b], ids, keys_in, values, k_there, v_there,
        scalars=1, after=(own,), flops=10**6, name="stack_kv",
    )

    (parts,) = call(context_body, [packed], land, keys, vals, flops=10**8, name="local_context")
    got = exchange(parts, "ctx", same_core)
    inverse, inverse_again, chain = call(
        inverse_body, [shape(M, M), shape(M, M), shape(7, M, M)], ids, land,
        scalars=1, after=(parts,), flops=3 * 10**9, name="inverse",
    )
    parts, kept = call(
        mixing_body, [shape(chips, cols, M, dtype=BF16), shape(cols + 8, M)],
        got, inverse, flops=10**8, name="mixing",
    )
    land_there = lax.ppermute(land, "ctx", swap)
    qs, grads = call(
        stack_body, [both_b, both_b], ids, queries, out_grad, q_there, g_there,
        scalars=1, after=(parts,), flops=10**6, name="stack_qg",
    )
    kone, kone_again, exp_local = call(
        ahead_body, [units, units, shape(heads, 2 * tok + 8, M)], qs, keys, land,
        far_out=(2,), after=(parts,), flops=2 * 10**9, name="ahead",
    )
    mixing = exchange(parts, "ctx", same_core).reshape(heads, DH, M)

    output, sums = call(
        output_body, [shape(2 * tok, half), shape(2 * n_head, 2, 2 * tok)],
        ids, kone, mixing, grads, gain, scalars=1, flops=10**8, name="output",
    )
    sums = exchange(sums, ("ctx", "head"), same_chip)
    (parts,) = call(
        norm_body, [packed], ids, sums, output, grads, gain, kone_again,
        scalars=1, flops=10**8, name="norm",
    )
    got = exchange(parts, "ctx", same_core)
    norm_mine, norm_other, query_mine, query_other, keyland = call(
        query_body, [block_b, block_b, block, block, shape(M, half)],
        ids, sums, output, grads, gain, mixing, qs, land,
        scalars=1, after=(parts,), flops=2 * 10**9, name="kernel_one_back",
    )
    parts, g_mixing = call(
        grad_context_body, [packed, shape(cols, M)], got, inverse_again, kept,
        after=(keyland,), flops=10**8, name="context_back",
    )
    got = exchange(parts, "ctx", same_core)
    (extra,) = call(
        inverse_back_body, [shape(M, 2 * half)], ids, chain, kept, g_mixing, land, keyland,
        scalars=1, after=(parts,), flops=5 * 10**9, name="inverse_back",
    )
    both, got = call(
        queryland_body, [shape(M, 2 * half, dtype=BF16), packed],
        got, exp_local, keys, vals, extra, far_in=(1,), flops=10**8, name="landmarks_back",
    )
    landed = exchange(both.reshape(n_ctx, land_dev, 2 * half), "ctx")
    norm_there = lax.ppermute(norm_other, "ctx", swap)
    query_there = lax.ppermute(query_other, "ctx", swap)
    got_there = lax.ppermute(got, "ctx", swap)
    (normed,) = call(
        gather_body, [wide_b], ids, norm_mine, norm_there,
        scalars=1, after=(both,), flops=10**6, name="gather",
    )
    value_grad, key_three, gain_grad = call(
        value_body, [wide_b, shape(tok, width), shape(1, width)],
        ids, keys_in, values, land, land_there, got, got_there,
        scalars=1, after=(both,), flops=2 * 10**9, name="kernel_three_back",
    )
    query_grad, key_grad = call(
        finish_body, [wide_b, wide_b], ids, landed, query_mine, query_there, key_three,
        scalars=1, after=(normed,), flops=10**6, name="finish",
    )
    return (normed, query_grad, key_grad, value_grad, gain_grad.reshape(width))


def solution(mesh):
    return jax.shard_map(
        on_device,
        mesh=mesh,
        in_specs=(
            P("ctx", "head"),
            P("ctx", "head"),
            P("ctx", "head"),
            P("head"),
            P("ctx", "head"),
        ),
        out_specs=(
            P("ctx", "head"),
            P("ctx", "head"),
            P("ctx", "head"),
            P("ctx", "head"),
            P("head"),
        ),
        check_vma=False,
    )
```

```python
import functools

import jax
import jax.numpy as jnp
from jax import lax
from jax.experimental import pallas as pl
from jax.experimental.pallas import tpu as pltpu
from jax.sharding import PartitionSpec as P

DH = 128
M = 256
EPS = 1e-06
F32 = jnp.float32
BF16 = jnp.bfloat16
SCALE = DH ** (-0.5)
VMEM_BYTES = 32 * 1024 * 1024
MOST_VMEM = 60 * 1024 * 1024
HALVES = (slice(0, DH), slice(DH, 2 * DH))

NN = (((1,), (0,)), ((), ()))
NT = (((1,), (1,)), ((), ()))
TN = (((0,), (0,)), ((), ()))


def dot(a, b, dims=NN):
    return lax.dot_general(a, b, dims, preferred_element_type=F32)


def split_up(x):
    high = x.astype(BF16)
    return high, (x - high.astype(F32)).astype(BF16)


def exact(a, b, dims=NN):
    a_high, a_low = a if isinstance(a, tuple) else split_up(a)
    b_high, b_low = b if isinstance(b, tuple) else split_up(b)
    return dot(a_high, b_high, dims) + (dot(a_high, b_low, dims) + dot(a_low, b_high, dims))


def exchange(parts, axis, groups=None):
    return lax.all_to_all(parts, axis, 0, 0, axis_index_groups=groups)


def high_low(x):
    high = x.astype(BF16).astype(F32)
    return high, x - high


def rows_of(*rows):
    index = lax.broadcasted_iota(jnp.int32, (8, rows[0].shape[1]), 0)
    out = jnp.zeros((8, rows[0].shape[1]), F32)
    for place, row in enumerate(rows):
        out = jnp.where(index == place, row, out)
    return out


def eye_times(value):
    row = lax.broadcasted_iota(jnp.int32, (M, M), 0)
    col = lax.broadcasted_iota(jnp.int32, (M, M), 1)
    return jnp.where(row == col, value, 0.0).astype(F32)


def head_cols(h):
    return slice(h * DH, (h + 1) * DH)


def halves(x):
    return jnp.concatenate([x[:, :DH], x[:, DH:]], axis=0)


def joined(x):
    n = x.shape[0] // 2
    return jnp.concatenate([x[:n], x[n:]], axis=1)


def own_head(ids_ref, h):
    return pl.ds(pl.multiple_of((ids_ref[0] * 2 + h) * DH, DH), DH)


def stacked(ids_ref, refs, h):
    return jnp.concatenate([ref[:, own_head(ids_ref, h)] for ref in refs], axis=0)


def rows_of(*rows):
    index = lax.broadcasted_iota(jnp.int32, (8, rows[0].shape[1]), 0)
    out = jnp.zeros((8, rows[0].shape[1]), F32)
    for place, row in enumerate(rows):
        out = jnp.where(index == place, row, out)
    return out


def eye_times(value):
    row = lax.broadcasted_iota(jnp.int32, (M, M), 0)
    col = lax.broadcasted_iota(jnp.int32, (M, M), 1)
    return jnp.where(row == col, value, 0.0).astype(F32)


def head_cols(h):
    return slice(h * DH, (h + 1) * DH)


def halves(x):
    return jnp.concatenate([x[:, :DH], x[:, DH:]], axis=0)


def joined(x):
    n = x.shape[0] // 2
    return jnp.concatenate([x[:n], x[n:]], axis=1)


def both_blocks(mine_ref, other_ref, which, h):
    return jnp.concatenate(
        [ref[which, :, head_cols(h)] for ref in (mine_ref, other_ref)], axis=0
    )


def call(
    body, outs, *args, scalars=0, far_in=(), far_out=(), after=(), flops=0,
    vmem=VMEM_BYTES, name
):
    nbytes = sum(a.size * a.dtype.itemsize for a in (*args, *outs))
    n_in, n_after, n_out = len(args), len(after), len(outs)
    n_far = len(far_in) + len(far_out)

    def whole(*refs):
        ins = list(refs[:n_in])
        results = list(refs[n_in + n_after : n_in + n_after + n_out])
        buffers = refs[n_in + n_after + n_out :]
        loads, stores = [], []
        for k, i in enumerate(far_in):
            loads.append(pltpu.make_async_copy(ins[i], buffers[k], buffers[n_far].at[k]))
            ins[i] = buffers[k]
        for k, i in enumerate(far_out, len(far_in)):
            stores.append(
                pltpu.make_async_copy(buffers[k], results[i], buffers[n_far].at[k])
            )
            results[i] = buffers[k]
        for copy in loads:
            copy.start()
        for copy in loads:
            copy.wait()
        body(*ins, *results)
        for copy in stores:
            copy.start()
        for copy in stores:
            copy.wait()

    def space(place, far):
        return pl.BlockSpec(memory_space=pltpu.HBM if place in far else pltpu.VMEM)

    in_specs = [
        pl.BlockSpec(memory_space=pltpu.SMEM) if i < scalars else space(i, far_in)
        for i in range(n_in)
    ] + [pl.BlockSpec(memory_space=pl.ANY)] * n_after
    scratch = [pltpu.VMEM(args[i].shape, args[i].dtype) for i in far_in]
    scratch += [pltpu.VMEM(outs[i].shape, outs[i].dtype) for i in far_out]
    if n_far:
        scratch.append(pltpu.SemaphoreType.DMA((n_far,)))
    return pl.pallas_call(
        whole,
        out_shape=outs,
        in_specs=in_specs,
        out_specs=[space(i, far_out) for i in range(n_out)],
        scratch_shapes=scratch,
        compiler_params=pltpu.CompilerParams(vmem_limit_bytes=vmem),
        cost_estimate=pl.CostEstimate(flops=flops, bytes_accessed=nbytes, transcendentals=0),
        name=name,
    )(*args, *after)


def shape(*dims, dtype=F32):
    return jax.ShapeDtypeStruct(dims, dtype)


def means_body(q_ref, k_ref, out_ref):
    count, land_dev, both = out_ref.shape
    half = both // 2
    seg_len = q_ref.shape[0] // land_dev
    q_mean, k_mean = [
        jnp.sum(ref[...].astype(F32).reshape(land_dev, seg_len, 2 * half), axis=1) / seg_len
        for ref in (q_ref, k_ref)
    ]
    for core in range(2):
        cols = slice(core * half, (core + 1) * half)
        own = jnp.concatenate([q_mean[:, cols], k_mean[:, cols]], axis=1).astype(BF16)
        for chip in range(count // 2):
            out_ref[2 * chip + core] = own


def stack_body(ids_ref, *refs):
    count = len(refs) // 3
    for mine, there, out in zip(refs[:count], refs[count : 2 * count], refs[2 * count :]):
        for h in range(out.shape[1] // DH):
            out[:, head_cols(h)] = stacked(ids_ref, (mine, there), h)


def context_body(land_ref, k_ref, v_ref, out_ref):
    count = out_ref.shape[0]
    heads = land_ref.shape[1] // (2 * DH)
    per_head = count // heads
    cols = DH // per_head
    for h in range(heads):
        keys = k_ref[:, head_cols(h)]
        vals = v_ref[:, head_cols(h)]
        score = dot(keys, land_ref[:, head_cols(h)], NT) * SCALE
        shift = jnp.max(score, axis=0, keepdims=True).astype(BF16).astype(F32)
        exp_local = jnp.exp(score - shift)
        high, low = high_low(jnp.sum(exp_local, axis=0, keepdims=True))
        weighted = dot(vals, exp_local.astype(BF16), TN)
        stats = rows_of(*[row[:, part] for row in (shift, high, low) for part in HALVES])
        for j in range(per_head):
            out_ref[h * per_head + j] = jnp.concatenate(
                [halves(weighted[j * cols : (j + 1) * cols]), stats], axis=0
            ).astype(BF16)


def inverse_body(ids_ref, land_ref, first_ref, again_ref, out_ref):
    half = land_ref.shape[1] // 2
    at = pl.multiple_of(ids_ref[1] * DH, DH)
    lq = land_ref[:, pl.ds(at, DH)]
    lk = land_ref[:, pl.ds(at + half, DH)]
    score = dot(lq, lk, NT) * SCALE
    top = jnp.exp(score - jnp.max(score, axis=1, keepdims=True))
    ktwo = top / jnp.sum(top, axis=1, keepdims=True)
    factor = column_factor(ktwo)
    ktwo_s = split_up(ktwo)
    x = factor * exact(ktwo_s, ktwo_s, NT)
    x_s = split_up(x)
    h2 = eye_times(15.0) - exact(x_s, eye_times(7.0) - x)
    h3 = eye_times(13.0) - exact(x_s, h2)
    h3_s = split_up(h3)
    p1 = 0.25 * exact(x_s, h3_s)
    p1_s = split_up(p1)
    b2 = eye_times(15.0) - exact(p1_s, eye_times(7.0) - p1)
    b3 = eye_times(13.0) - exact(p1_s, b2)
    inverse = (factor * 0.0625) * exact(b3, exact(h3_s, ktwo_s))
    first_ref[...] = inverse
    again_ref[...] = inverse
    for place, part in enumerate((ktwo, x, h2, h3, p1, b2, b3)):
        out_ref[place] = part


def column_factor(ktwo):
    return 1.0 / jnp.max(jnp.sum(ktwo, axis=0, keepdims=True), axis=1, keepdims=True)


def mixing_body(got_ref, inv_ref, out_ref, kept_ref):
    count, rows, _ = got_ref.shape
    cols = (rows - 8) // 2
    tops = got_ref[0].astype(F32)[rows - 8 :]
    for place in range(1, count):
        tops = jnp.maximum(tops, got_ref[place].astype(F32)[rows - 8 :])
    tops = tops[0:2]
    total = jnp.zeros((2, DH), F32)
    left = jnp.zeros((cols, DH), F32)
    right = jnp.zeros((cols, DH), F32)
    for place in range(count):
        part = got_ref[place].astype(F32)
        stats = part[rows - 8 :]
        fade = jnp.exp(stats[0:2] - tops)
        total = total + fade * (stats[2:4] + stats[4:6])
        left = left + fade[0:1] * part[:cols]
        right = right + fade[1:2] * part[cols : 2 * cols]
    total = joined(total)
    context = jnp.concatenate([left, right], axis=1) / total
    mixing = exact(context, inv_ref[...]).astype(BF16)
    for place in range(count):
        out_ref[place] = mixing
    kept_ref[...] = jnp.concatenate([context, rows_of(total, joined(tops))], axis=0)


def softmax_rows(score):
    top = jnp.exp(score - jnp.max(score, axis=1, keepdims=True))
    return top / jnp.sum(top, axis=1, keepdims=True)


def kernel_one(q_ref, land_ref, h):
    heads = land_ref.shape[1] // (2 * DH)
    score = dot(q_ref[:, head_cols(h)], land_ref[:, head_cols(heads + h)], NT) * SCALE
    return softmax_rows(score)


def ahead_body(
    q_ref, k_ref, land_ref, kone_ref, exp_ref
):
    heads, tok, _ = kone_ref.shape
    for h in range(heads):
        kone = kernel_one(q_ref, land_ref, h).astype(BF16)
        kone_ref[h] = kone
        keys = k_ref[:, head_cols(h)]
        score = dot(keys, land_ref[:, head_cols(h)], NT) * SCALE
        shift = jnp.max(score, axis=0, keepdims=True).astype(BF16).astype(F32)
        exp_ref[h, :tok] = jnp.exp(score - shift).astype(BF16)
        exp_ref[h, tok:] = jnp.broadcast_to(shift, (16, M)).astype(BF16)


def output_body(ids_ref, kone_ref, mix_ref, g_ref, gain_ref, out_ref, sum_ref):
    heads, tok, _ = kone_ref.shape
    squares = jnp.zeros((tok, DH), F32)
    slopes = jnp.zeros((tok, DH), F32)
    for h in range(heads):
        out = dot(kone_ref[h], mix_ref[h], NT)
        out_ref[:, head_cols(h)] = out
        grad = g_ref[:, head_cols(h)].astype(F32)
        squares = squares + out * out
        slopes = slopes + grad * gain_ref[:, own_head(ids_ref, h)] * out
    high, low = split_up(jnp.concatenate([squares, slopes], axis=0))
    ones = jnp.ones((8, DH), BF16)
    row = (dot(ones, high, NT) + dot(ones, low, NT))[0:1]
    both = rows_of(
        swap_blocks(ids_ref, row[:, :tok], 1), swap_blocks(ids_ref, row[:, tok:], 1)
    )
    for place in range(sum_ref.shape[0]):
        sum_ref[place] = both[:2]


def swap_blocks(ids_ref, x, axis):
    size = x.shape[axis] // 2
    left = lax.slice_in_dim(x, 0, size, axis=axis)
    right = lax.slice_in_dim(x, size, 2 * size, axis=axis)
    swapped = jnp.concatenate([right, left], axis=axis)
    return jnp.where(ids_ref[0] == 0, x, swapped)


def token_factors(ids_ref, sum_ref, features):
    total = sum_ref[0]
    for place in range(1, sum_ref.shape[0]):
        total = total + sum_ref[place]
    root_inv = lax.rsqrt(total[0:1] / features + EPS)
    slope = total[1:2] * root_inv / features
    columns = jnp.transpose(
        rows_of(
            swap_blocks(ids_ref, root_inv, 1), swap_blocks(ids_ref, root_inv * slope, 1)
        )
    )
    return columns[:, 0:1], columns[:, 1:2]


def output_grad(factors, out, grad, gain):
    root_inv, bent = factors
    return (root_inv * (grad * gain - out * bent)).astype(BF16)


def norm_body(ids_ref, sum_ref, out_ref, g_ref, gain_ref, kone_ref, part_ref):
    heads = kone_ref.shape[0]
    per_head = part_ref.shape[0] // heads
    cols = DH // per_head
    factors = token_factors(ids_ref, sum_ref, heads * DH * sum_ref.shape[0])
    for h in range(heads):
        out = out_ref[:, head_cols(h)]
        grad = g_ref[:, head_cols(h)].astype(F32)
        gain = gain_ref[:, own_head(ids_ref, h)]
        g_mixing = dot(output_grad(factors, out, grad, gain), kone_ref[h], TN)
        gain_sum = jnp.sum(grad * (out * factors[0]), axis=0, keepdims=True)
        tail = rows_of(*high_low(gain_sum))
        for j in range(per_head):
            part_ref[h * per_head + j] = jnp.concatenate(
                [halves(g_mixing[j * cols : (j + 1) * cols]), tail], axis=0
            ).astype(BF16)


def query_body(
    ids_ref, sum_ref, out_ref, g_ref, gain_ref, mix_ref, q_ref, land_ref,
    mine_ref, other_ref, keyland_ref,
):
    heads = mix_ref.shape[0]
    tok = mine_ref.shape[1]
    factors = token_factors(ids_ref, sum_ref, heads * DH * sum_ref.shape[0])
    for h in range(heads):
        out = out_ref[:, head_cols(h)]
        grad = g_ref[:, head_cols(h)].astype(F32)
        gain = gain_ref[:, own_head(ids_ref, h)]
        normed = (out * factors[0] * gain).astype(BF16)
        mine_ref[0, :, head_cols(h)] = normed[:tok]
        other_ref[0, :, head_cols(h)] = normed[tok:]
        kone = kernel_one(q_ref, land_ref, h)
        g_kernel = dot(output_grad(factors, out, grad, gain), mix_ref[h])
        inner = jnp.sum(kone * g_kernel, axis=1, keepdims=True)
        g_score = (kone * (g_kernel - inner)).astype(BF16)
        query = dot(g_score, land_ref[:, head_cols(heads + h)]) * SCALE
        mine_ref[1, :, head_cols(h)] = query[:tok].astype(BF16)
        other_ref[1, :, head_cols(h)] = query[tok:].astype(BF16)
        queries = q_ref[:, head_cols(h)]
        keyland_ref[:, head_cols(h)] = dot(g_score, queries, TN) * SCALE


def grad_context_body(got_ref, inv_ref, kept_ref, out_ref, g_ref):
    count, rows, _ = got_ref.shape
    cols = (rows - 8) // 2
    got = got_ref[0].astype(F32)
    for place in range(1, count):
        got = got + got_ref[place].astype(F32)
    g_mixing = joined(got[: 2 * cols])
    gain = high_low(got[2 * cols : 2 * cols + 1] + got[2 * cols + 1 : 2 * cols + 2])
    context = kept_ref[:cols]
    total = kept_ref[cols : cols + 1]
    top = kept_ref[cols + 1 : cols + 2]
    g_context = exact(g_mixing, inv_ref[...], NT)
    high, low = high_low(-jnp.sum(g_context * context, axis=0, keepdims=True) / total)
    tail = rows_of(
        *[row[:, part] for row in (high, low) for part in HALVES],
        *gain,
        *[top[:, part] for part in HALVES],
    )
    mine = jnp.concatenate([halves(g_context / total), tail], axis=0).astype(BF16)
    for place in range(count):
        out_ref[place] = mine
    g_ref[...] = g_mixing


def inverse_back_body(ids_ref, inv_ref, kept_ref, g_ref, land_ref, keyland_ref, out_ref):
    half = land_ref.shape[1] // 2
    at = pl.multiple_of(ids_ref[1] * DH, DH)
    lq = land_ref[:, pl.ds(at, DH)]
    lk = land_ref[:, pl.ds(at + half, DH)]
    ktwo, x, h2, h3, p1, b2, b3 = [inv_ref[place] for place in range(7)]
    factor = column_factor(ktwo)
    ktwo_s, x_s, h3_s, p1_s, b3_s = [split_up(part) for part in (ktwo, x, h3, p1, b3)]
    g_mixing = split_up(g_ref[...])
    context = split_up(kept_ref[: g_ref.shape[0]])
    inner = split_up(exact(context, b3_s))
    outer = exact(inner, h3_s)
    d_outer = split_up((factor * 0.0625) * exact(g_mixing, ktwo_s, NT))
    d_inner = exact(d_outer, h3_s)
    d_b3 = split_up(exact(context, d_inner, TN))
    d_b2 = split_up(-exact(p1_s, d_b3))
    d_b1 = -exact(p1_s, d_b2)
    d_p1 = -exact(d_b3, b2) - exact(d_b2, eye_times(7.0) - p1) - d_b1
    d_p1 = split_up(d_p1)
    d_h3 = split_up(exact(inner, d_outer, TN) + 0.25 * exact(x_s, d_p1))
    d_h2 = split_up(-exact(x_s, d_h3))
    d_h1 = -exact(x_s, d_h2)
    d_x = 0.25 * exact(d_p1, h3_s) - exact(d_h3, h2) - exact(d_h2, eye_times(7.0) - x) - d_h1
    d_ktwo = (factor * 0.0625) * exact(outer, g_mixing, TN) + factor * exact(
        d_x + jnp.transpose(d_x), ktwo_s
    )
    g_score = ktwo * (d_ktwo - jnp.sum(ktwo * d_ktwo, axis=1, keepdims=True))
    out_ref[:, :half] = jnp.zeros((M, half), F32)
    out_ref[:, half:] = keyland_ref[...]
    high, low = split_up(g_score)
    out_ref[:, pl.ds(at, DH)] = (dot(high, lk) + dot(low, lk)) * SCALE
    out_ref[:, pl.ds(at + half, DH)] = keyland_ref[:, pl.ds(at, DH)] + (
        (dot(high, lq, TN) + dot(low, lq, TN)) * SCALE
    )


def unpacked(got, h, heads):
    count, rows, _ = got.shape
    per_head = count // heads
    cols = (rows - 8) // 2
    parts = [got[h * per_head + j] for j in range(per_head)]
    g_weighted = jnp.concatenate(
        [
            jnp.concatenate([part[:cols], part[cols : 2 * cols]], axis=1)
            for part in parts
        ],
        axis=0,
    )
    tails = [part.astype(F32)[2 * cols :] for part in parts]
    summed = functools.reduce(jnp.add, tails)
    g_totals = joined(summed[0:2] + summed[2:4])
    top = joined(tails[0][6:8])
    gain = tails[0][4:5] + tails[0][5:6]
    return g_weighted, g_totals, top, gain


def queryland_body(
    got_ref, exp_ref, k_ref, v_ref, extra_ref, land_ref, out_ref, pass_ref
):
    heads = exp_ref.shape[0]
    half = heads * DH
    for h in range(heads):
        g_weighted, g_totals, top, _ = unpacked(got_ref, h, heads)
        keys = k_ref[:, head_cols(h)]
        vals = v_ref[:, head_cols(h)]
        tok = keys.shape[0]
        shift = exp_ref[h, tok:].astype(F32)[0:1]
        exp_three = exp_ref[h, :tok].astype(F32) * jnp.exp(shift - top)
        g_score = (exp_three * (dot(vals, g_weighted) + g_totals)).astype(BF16)
        queryland = dot(g_score, keys, TN) * SCALE
        out_ref[:, head_cols(h)] = (queryland + extra_ref[:, head_cols(h)]).astype(BF16)
    out_ref[:, half:] = extra_ref[:, half:].astype(BF16)
    count, rows, _ = got_ref.shape
    for place in range(count):
        pass_ref[place * rows : (place + 1) * rows] = got_ref[place]
    for h in range(heads):
        at = count * rows + h * M
        pass_ref[at : at + M] = land_ref[:, head_cols(h)]


class Parts:
    def __init__(self, ref, count, rows):
        self.ref, self.shape = ref, (count, rows, ref.shape[1])

    def __getitem__(self, place):
        rows = self.shape[1]
        return self.ref[place * rows : (place + 1) * rows]


def value_body(
    count, ids_ref, k_ref, v_ref, pass_ref, pass_there, value_out, key_out, gain_out
):
    heads = k_ref.shape[1] // (2 * DH)
    total = pass_ref.shape[0] - heads * M

    def place_halves(core, own, away):
        for place, ref in ((own, pass_ref), (away, pass_there)):
            for h in range(heads):
                cols = slice(place.start + h * DH, place.start + (h + 1) * DH)
                g_weighted, g_totals, top, gain = unpacked(
                    Parts(ref, count, total // count), h, heads
                )
                lq = ref[total + h * M : total + (h + 1) * M]
                exp_three = jnp.exp(dot(k_ref[:, cols], lq, NT) * SCALE - top)
                g_exp = dot(v_ref[:, cols], g_weighted) + g_totals
                value_out[:, cols] = dot(exp_three.astype(BF16), g_weighted, NT).astype(BF16)
                key_out[:, cols] = dot((exp_three * g_exp).astype(BF16), lq) * SCALE
                gain_out[:, cols] = gain

    by_core(ids_ref, place_halves)


def by_core(ids_ref, place_halves):
    half = 2 * DH
    left, right = slice(0, half), slice(half, 2 * half)

    @pl.when(ids_ref[0] == 0)
    def _():
        place_halves(0, left, right)

    @pl.when(ids_ref[0] != 0)
    def _():
        place_halves(1, right, left)


def gather_body(ids_ref, mine_ref, there_ref, norm_out):
    def place_halves(core, own, away):
        norm_out[:, own] = mine_ref[0]
        norm_out[:, away] = there_ref[0]

    by_core(ids_ref, place_halves)


def finish_body(
    ids_ref, got_ref, mine_ref, there_ref, key_ref, query_out, key_out
):
    count, land_dev, both = got_ref.shape
    _, tok, half = mine_ref.shape
    seg_len = tok // land_dev
    lands = []
    for core in range(2):
        got = got_ref[core].astype(F32)
        for chip in range(1, count // 2):
            got = got + got_ref[2 * chip + core].astype(F32)
        lands.append(got / seg_len)
    spans = [(row, slice(row * seg_len, (row + 1) * seg_len)) for row in range(land_dev)]

    def place_halves(core, own, away):
        for place, land, ref in (
            (own, lands[core], mine_ref), (away, lands[1 - core], there_ref)
        ):
            for row, span in spans:
                query_out[span, place] = (
                    ref[1, span].astype(F32) + land[row : row + 1, :half]
                ).astype(BF16)

    by_core(ids_ref, place_halves)
    for core in range(2):
        place = slice(core * half, (core + 1) * half)
        for row, span in spans:
            key_out[span, place] = (
                key_ref[span, place] + lands[core][row : row + 1, half:]
            ).astype(BF16)


def on_device(queries, keys_in, values, norm_gain, out_grad):
    tok, width = queries.shape
    half = width // 2
    heads = half // DH
    n_ctx = lax.axis_size("ctx")
    n_head = lax.axis_size("head")
    chips = n_ctx // 2
    per_head = chips // heads
    cols = DH // per_head
    land_dev = M // n_ctx
    here = lax.axis_index("ctx").astype(jnp.int32)
    ids = jnp.stack([lax.rem(here, 2), lax.div(here, 2 * per_head)])
    gain = norm_gain.reshape(1, width)
    same_core = [list(range(core, n_ctx, 2)) for core in range(2)]
    same_chip = [
        [(2 * chip + core) * n_head + z for core in range(2) for z in range(n_head)]
        for chip in range(chips)
    ]
    swap = [(i, i ^ 1) for i in range(n_ctx)]
    packed = shape(chips, 2 * cols + 8, DH, dtype=BF16)
    pair = shape(2, tok, half, dtype=BF16)
    wide_b = shape(tok, width, dtype=BF16)
    units = shape(heads, 2 * tok, M, dtype=BF16)

    both_b = shape(2 * tok, half, dtype=BF16)
    (own,) = call(
        means_body, [shape(n_ctx, land_dev, 2 * half, dtype=BF16)], queries, keys_in,
        far_in=(0, 1), far_out=(0,), vmem=MOST_VMEM, flops=10**6, name="landmark_means",
    )
    held = lax.optimization_barrier((own, keys_in, values, queries, out_grad))
    k_there, v_there, q_there, g_there = [lax.ppermute(x, "ctx", swap) for x in held[1:]]
    land = exchange(own, "ctx").reshape(M, 2 * half)
    keys, vals = call(
        stack_body, [both_b, both_b], ids, keys_in, values, k_there, v_there,
        scalars=1, after=(own,), flops=10**6, name="stack_kv",
    )

    (parts,) = call(context_body, [packed], land, keys, vals, flops=10**8, name="local_context")
    got = exchange(parts, "ctx", same_core)
    inverse, inverse_again, chain = call(
        inverse_body, [shape(M, M), shape(M, M), shape(7, M, M)], ids, land,
        scalars=1, after=(parts,), flops=3 * 10**9, name="inverse",
    )
    parts, kept = call(
        mixing_body, [shape(chips, cols, M, dtype=BF16), shape(cols + 8, M)],
        got, inverse, flops=10**8, name="mixing",
    )
    qs, grads = call(
        stack_body, [both_b, both_b], ids, queries, out_grad, q_there, g_there,
        scalars=1, after=(parts,), flops=10**6, name="stack_qg",
    )
    kone, exp_local = call(
        ahead_body, [units, shape(heads, 2 * tok + 16, M, dtype=BF16)], qs, keys, land,
        after=(parts,), flops=2 * 10**9, name="ahead",
    )
    mixing = exchange(parts, "ctx", same_core).reshape(heads, DH, M)

    output, sums = call(
        output_body, [shape(2 * tok, half), shape(2 * n_head, 2, 2 * tok)],
        ids, kone, mixing, grads, gain, scalars=1, flops=10**8, name="output",
    )
    sums = exchange(sums, ("ctx", "head"), same_chip)
    (parts,) = call(
        norm_body, [packed], ids, sums, output, grads, gain, kone,
        scalars=1, flops=10**8, name="norm",
    )
    got = exchange(parts, "ctx", same_core)
    mine, other, keyland = call(
        query_body, [pair, pair, shape(M, half)],
        ids, sums, output, grads, gain, mixing, qs, land,
        scalars=1, after=(parts,), flops=2 * 10**9, name="kernel_one_back",
    )
    parts, g_mixing = call(
        grad_context_body, [packed, shape(cols, M)], got, inverse_again, kept,
        after=(other,), flops=10**8, name="context_back",
    )
    got = exchange(parts, "ctx", same_core)
    (extra,) = call(
        inverse_back_body, [shape(M, 2 * half)], ids, chain, kept, g_mixing, land, keyland,
        scalars=1, after=(parts,), flops=5 * 10**9, name="inverse_back",
    )
    both, passed = call(
        queryland_body,
        [shape(M, 2 * half, dtype=BF16), shape(chips * (2 * cols + 8) + heads * M, DH, dtype=BF16)],
        got, exp_local, keys, vals, extra, land, flops=10**8, name="landmarks_back",
    )
    landed = exchange(both.reshape(n_ctx, land_dev, 2 * half), "ctx")
    there = lax.ppermute(other, "ctx", swap)
    passed_there = lax.ppermute(passed, "ctx", swap)
    (normed,) = call(
        gather_body, [wide_b], ids, mine, there,
        scalars=1, after=(both,), flops=10**6, name="gather",
    )
    value_grad, key_three, gain_grad = call(
        functools.partial(value_body, chips), [wide_b, shape(tok, width), shape(1, width)],
        ids, keys_in, values, passed, passed_there,
        scalars=1, after=(both,), flops=2 * 10**9, name="kernel_three_back",
    )
    query_grad, key_grad = call(
        finish_body, [wide_b, wide_b], ids, landed, mine, there, key_three,
        scalars=1, after=(normed,), flops=10**6, name="finish",
    )
    return (normed, query_grad, key_grad, value_grad, gain_grad.reshape(width))


def solution(mesh):
    return jax.shard_map(
        on_device,
        mesh=mesh,
        in_specs=(
            P("ctx", "head"),
            P("ctx", "head"),
            P("ctx", "head"),
            P("head"),
            P("ctx", "head"),
        ),
        out_specs=(
            P("ctx", "head"),
            P("ctx", "head"),
            P("ctx", "head"),
            P("ctx", "head"),
            P("head"),
        ),
        check_vma=False,
    )
```

```python
import functools

import jax
import jax.numpy as jnp
from jax import lax
from jax.experimental import pallas as pl
from jax.experimental.pallas import tpu as pltpu
from jax.sharding import PartitionSpec as P

DH = 128
M = 256
EPS = 1e-06
F32 = jnp.float32
BF16 = jnp.bfloat16
SCALE = DH ** (-0.5)
VMEM_BYTES = 32 * 1024 * 1024
MOST_VMEM = 60 * 1024 * 1024
HALVES = (slice(0, DH), slice(DH, 2 * DH))

NN = (((1,), (0,)), ((), ()))
NT = (((1,), (1,)), ((), ()))
TN = (((0,), (0,)), ((), ()))


def dot(a, b, dims=NN):
    return lax.dot_general(a, b, dims, preferred_element_type=F32)


def split_up(x):
    high = x.astype(BF16)
    return high, (x - high.astype(F32)).astype(BF16)


def exact(a, b, dims=NN):
    a_high, a_low = a if isinstance(a, tuple) else split_up(a)
    b_high, b_low = b if isinstance(b, tuple) else split_up(b)
    return dot(a_high, b_high, dims) + (dot(a_high, b_low, dims) + dot(a_low, b_high, dims))


def exchange(parts, axis, groups=None):
    return lax.all_to_all(parts, axis, 0, 0, axis_index_groups=groups)


def high_low(x):
    high = x.astype(BF16).astype(F32)
    return high, x - high


def rows_of(*rows):
    index = lax.broadcasted_iota(jnp.int32, (8, rows[0].shape[1]), 0)
    out = jnp.zeros((8, rows[0].shape[1]), F32)
    for place, row in enumerate(rows):
        out = jnp.where(index == place, row, out)
    return out


def eye_times(value):
    row = lax.broadcasted_iota(jnp.int32, (M, M), 0)
    col = lax.broadcasted_iota(jnp.int32, (M, M), 1)
    return jnp.where(row == col, value, 0.0).astype(F32)


def head_cols(h):
    return slice(h * DH, (h + 1) * DH)


def halves(x):
    return jnp.concatenate([x[:, :DH], x[:, DH:]], axis=0)


def joined(x):
    n = x.shape[0] // 2
    return jnp.concatenate([x[:n], x[n:]], axis=1)


def own_head(ids_ref, h):
    return pl.ds(pl.multiple_of((ids_ref[0] * 2 + h) * DH, DH), DH)


def stacked(ids_ref, refs, h):
    return jnp.concatenate([ref[:, own_head(ids_ref, h)] for ref in refs], axis=0)


def rows_of(*rows):
    index = lax.broadcasted_iota(jnp.int32, (8, rows[0].shape[1]), 0)
    out = jnp.zeros((8, rows[0].shape[1]), F32)
    for place, row in enumerate(rows):
        out = jnp.where(index == place, row, out)
    return out


def eye_times(value):
    row = lax.broadcasted_iota(jnp.int32, (M, M), 0)
    col = lax.broadcasted_iota(jnp.int32, (M, M), 1)
    return jnp.where(row == col, value, 0.0).astype(F32)


def head_cols(h):
    return slice(h * DH, (h + 1) * DH)


def halves(x):
    return jnp.concatenate([x[:, :DH], x[:, DH:]], axis=0)


def joined(x):
    n = x.shape[0] // 2
    return jnp.concatenate([x[:n], x[n:]], axis=1)


def both_blocks(mine_ref, other_ref, which, h):
    return jnp.concatenate(
        [ref[which, :, head_cols(h)] for ref in (mine_ref, other_ref)], axis=0
    )


def call(
    body, outs, *args, scalars=0, far_in=(), far_out=(), after=(), flops=0,
    vmem=VMEM_BYTES, name
):
    nbytes = sum(a.size * a.dtype.itemsize for a in (*args, *outs))
    n_in, n_after, n_out = len(args), len(after), len(outs)
    n_far = len(far_in) + len(far_out)

    def whole(*refs):
        ins = list(refs[:n_in])
        results = list(refs[n_in + n_after : n_in + n_after + n_out])
        buffers = refs[n_in + n_after + n_out :]
        loads, stores = [], []
        for k, i in enumerate(far_in):
            loads.append(pltpu.make_async_copy(ins[i], buffers[k], buffers[n_far].at[k]))
            ins[i] = buffers[k]
        for k, i in enumerate(far_out, len(far_in)):
            stores.append(
                pltpu.make_async_copy(buffers[k], results[i], buffers[n_far].at[k])
            )
            results[i] = buffers[k]
        for copy in loads:
            copy.start()
        for copy in loads:
            copy.wait()
        body(*ins, *results)
        for copy in stores:
            copy.start()
        for copy in stores:
            copy.wait()

    def space(place, far):
        return pl.BlockSpec(memory_space=pltpu.HBM if place in far else pltpu.VMEM)

    in_specs = [
        pl.BlockSpec(memory_space=pltpu.SMEM) if i < scalars else space(i, far_in)
        for i in range(n_in)
    ] + [pl.BlockSpec(memory_space=pl.ANY)] * n_after
    scratch = [pltpu.VMEM(args[i].shape, args[i].dtype) for i in far_in]
    scratch += [pltpu.VMEM(outs[i].shape, outs[i].dtype) for i in far_out]
    if n_far:
        scratch.append(pltpu.SemaphoreType.DMA((n_far,)))
    return pl.pallas_call(
        whole,
        out_shape=outs,
        in_specs=in_specs,
        out_specs=[space(i, far_out) for i in range(n_out)],
        scratch_shapes=scratch,
        compiler_params=pltpu.CompilerParams(vmem_limit_bytes=vmem),
        cost_estimate=pl.CostEstimate(flops=flops, bytes_accessed=nbytes, transcendentals=0),
        name=name,
    )(*args, *after)


def shape(*dims, dtype=F32):
    return jax.ShapeDtypeStruct(dims, dtype)


def means_body(q_ref, k_ref, out_ref):
    count, land_dev, both = out_ref.shape
    half = both // 2
    seg_len = q_ref.shape[0] // land_dev
    q_mean, k_mean = [
        jnp.sum(ref[...].astype(F32).reshape(land_dev, seg_len, 2 * half), axis=1) / seg_len
        for ref in (q_ref, k_ref)
    ]
    for core in range(2):
        cols = slice(core * half, (core + 1) * half)
        own = jnp.concatenate([q_mean[:, cols], k_mean[:, cols]], axis=1).astype(BF16)
        for chip in range(count // 2):
            out_ref[2 * chip + core] = own


def stack_body(ids_ref, *refs):
    count = len(refs) // 3
    for mine, there, out in zip(refs[:count], refs[count : 2 * count], refs[2 * count :]):
        for h in range(out.shape[1] // DH):
            out[:, head_cols(h)] = stacked(ids_ref, (mine, there), h)


def context_body(land_ref, k_ref, v_ref, out_ref):
    count = out_ref.shape[0]
    heads = land_ref.shape[1] // (2 * DH)
    per_head = count // heads
    cols = DH // per_head
    for h in range(heads):
        keys = k_ref[:, head_cols(h)]
        vals = v_ref[:, head_cols(h)]
        score = dot(keys, land_ref[:, head_cols(h)], NT) * SCALE
        shift = jnp.max(score, axis=0, keepdims=True).astype(BF16).astype(F32)
        exp_local = jnp.exp(score - shift)
        high, low = high_low(jnp.sum(exp_local, axis=0, keepdims=True))
        weighted = dot(vals, exp_local.astype(BF16), TN)
        stats = rows_of(*[row[:, part] for row in (shift, high, low) for part in HALVES])
        for j in range(per_head):
            out_ref[h * per_head + j] = jnp.concatenate(
                [halves(weighted[j * cols : (j + 1) * cols]), stats], axis=0
            ).astype(BF16)


def inverse_body(ids_ref, land_ref, first_ref, again_ref, out_ref):
    half = land_ref.shape[1] // 2
    at = pl.multiple_of(ids_ref[1] * DH, DH)
    lq = land_ref[:, pl.ds(at, DH)]
    lk = land_ref[:, pl.ds(at + half, DH)]
    score = dot(lq, lk, NT) * SCALE
    top = jnp.exp(score - jnp.max(score, axis=1, keepdims=True))
    ktwo = top / jnp.sum(top, axis=1, keepdims=True)
    factor = column_factor(ktwo)
    ktwo_s = split_up(ktwo)
    x = factor * exact(ktwo_s, ktwo_s, NT)
    x_s = split_up(x)
    h2 = eye_times(15.0) - exact(x_s, eye_times(7.0) - x)
    h3 = eye_times(13.0) - exact(x_s, h2)
    h3_s = split_up(h3)
    p1 = 0.25 * exact(x_s, h3_s)
    p1_s = split_up(p1)
    b2 = eye_times(15.0) - exact(p1_s, eye_times(7.0) - p1)
    b3 = eye_times(13.0) - exact(p1_s, b2)
    inverse = (factor * 0.0625) * exact(b3, exact(h3_s, ktwo_s))
    first_ref[...] = inverse
    again_ref[...] = inverse
    for place, part in enumerate((ktwo, x, h2, h3, p1, b2, b3)):
        out_ref[place] = part


def column_factor(ktwo):
    return 1.0 / jnp.max(jnp.sum(ktwo, axis=0, keepdims=True), axis=1, keepdims=True)


def mixing_body(got_ref, inv_ref, out_ref, kept_ref):
    count, rows, _ = got_ref.shape
    cols = (rows - 8) // 2
    tops = got_ref[0].astype(F32)[rows - 8 :]
    for place in range(1, count):
        tops = jnp.maximum(tops, got_ref[place].astype(F32)[rows - 8 :])
    tops = tops[0:2]
    total = jnp.zeros((2, DH), F32)
    left = jnp.zeros((cols, DH), F32)
    right = jnp.zeros((cols, DH), F32)
    for place in range(count):
        part = got_ref[place].astype(F32)
        stats = part[rows - 8 :]
        fade = jnp.exp(stats[0:2] - tops)
        total = total + fade * (stats[2:4] + stats[4:6])
        left = left + fade[0:1] * part[:cols]
        right = right + fade[1:2] * part[cols : 2 * cols]
    total = joined(total)
    context = jnp.concatenate([left, right], axis=1) / total
    mixing = exact(context, inv_ref[...]).astype(BF16)
    for place in range(count):
        out_ref[place] = mixing
    kept_ref[...] = jnp.concatenate([context, rows_of(total, joined(tops))], axis=0)


def softmax_rows(score):
    top = jnp.exp(score - jnp.max(score, axis=1, keepdims=True))
    return top / jnp.sum(top, axis=1, keepdims=True)


def kernel_one(q_ref, land_ref, h):
    heads = land_ref.shape[1] // (2 * DH)
    score = dot(q_ref[:, head_cols(h)], land_ref[:, head_cols(heads + h)], NT) * SCALE
    return softmax_rows(score)


def ahead_body(
    q_ref, k_ref, land_ref, kone_ref, exp_ref
):
    heads, tok, _ = kone_ref.shape
    for h in range(heads):
        kone = kernel_one(q_ref, land_ref, h).astype(BF16)
        kone_ref[h] = kone
        keys = k_ref[:, head_cols(h)]
        score = dot(keys, land_ref[:, head_cols(h)], NT) * SCALE
        shift = jnp.max(score, axis=0, keepdims=True).astype(BF16).astype(F32)
        exp_ref[h, :tok] = jnp.exp(score - shift).astype(BF16)
        exp_ref[h, tok:] = jnp.broadcast_to(shift, (16, M)).astype(BF16)


def output_body(ids_ref, kone_ref, mix_ref, g_ref, gain_ref, out_ref, sum_ref):
    heads, tok, _ = kone_ref.shape
    squares = jnp.zeros((tok, DH), F32)
    slopes = jnp.zeros((tok, DH), F32)
    for h in range(heads):
        out = dot(kone_ref[h], mix_ref[h], NT)
        out_ref[:, head_cols(h)] = out
        grad = g_ref[:, head_cols(h)].astype(F32)
        squares = squares + out * out
        slopes = slopes + grad * gain_ref[:, own_head(ids_ref, h)] * out
    high, low = split_up(jnp.concatenate([squares, slopes], axis=0))
    ones = jnp.ones((8, DH), BF16)
    row = (dot(ones, high, NT) + dot(ones, low, NT))[0:1]
    both = rows_of(
        swap_blocks(ids_ref, row[:, :tok], 1), swap_blocks(ids_ref, row[:, tok:], 1)
    )
    for place in range(sum_ref.shape[0]):
        sum_ref[place] = both[:2]


def swap_blocks(ids_ref, x, axis):
    size = x.shape[axis] // 2
    left = lax.slice_in_dim(x, 0, size, axis=axis)
    right = lax.slice_in_dim(x, size, 2 * size, axis=axis)
    swapped = jnp.concatenate([right, left], axis=axis)
    return jnp.where(ids_ref[0] == 0, x, swapped)


def token_factors(ids_ref, sum_ref, features):
    total = sum_ref[0]
    for place in range(1, sum_ref.shape[0]):
        total = total + sum_ref[place]
    root_inv = lax.rsqrt(total[0:1] / features + EPS)
    slope = total[1:2] * root_inv / features
    columns = jnp.transpose(
        rows_of(
            swap_blocks(ids_ref, root_inv, 1), swap_blocks(ids_ref, root_inv * slope, 1)
        )
    )
    return columns[:, 0:1], columns[:, 1:2]


def output_grad(factors, out, grad, gain):
    root_inv, bent = factors
    return (root_inv * (grad * gain - out * bent)).astype(BF16)


def norm_body(ids_ref, sum_ref, out_ref, g_ref, gain_ref, kone_ref, part_ref):
    heads = kone_ref.shape[0]
    per_head = part_ref.shape[0] // heads
    cols = DH // per_head
    factors = token_factors(ids_ref, sum_ref, heads * DH * sum_ref.shape[0])
    for h in range(heads):
        out = out_ref[:, head_cols(h)]
        grad = g_ref[:, head_cols(h)].astype(F32)
        gain = gain_ref[:, own_head(ids_ref, h)]
        g_mixing = dot(output_grad(factors, out, grad, gain), kone_ref[h], TN)
        gain_sum = jnp.sum(grad * (out * factors[0]), axis=0, keepdims=True)
        tail = rows_of(*high_low(gain_sum))
        for j in range(per_head):
            part_ref[h * per_head + j] = jnp.concatenate(
                [halves(g_mixing[j * cols : (j + 1) * cols]), tail], axis=0
            ).astype(BF16)


def query_body(
    ids_ref, sum_ref, out_ref, g_ref, gain_ref, mix_ref, q_ref, land_ref,
    mine_ref, other_ref, keyland_ref,
):
    heads = mix_ref.shape[0]
    tok = mine_ref.shape[1]
    factors = token_factors(ids_ref, sum_ref, heads * DH * sum_ref.shape[0])
    for h in range(heads):
        out = out_ref[:, head_cols(h)]
        grad = g_ref[:, head_cols(h)].astype(F32)
        gain = gain_ref[:, own_head(ids_ref, h)]
        normed = (out * factors[0] * gain).astype(BF16)
        mine_ref[0, :, head_cols(h)] = normed[:tok]
        other_ref[0, :, head_cols(h)] = normed[tok:]
        kone = kernel_one(q_ref, land_ref, h)
        g_kernel = dot(output_grad(factors, out, grad, gain), mix_ref[h])
        inner = jnp.sum(kone * g_kernel, axis=1, keepdims=True)
        g_score = (kone * (g_kernel - inner)).astype(BF16)
        query = dot(g_score, land_ref[:, head_cols(heads + h)]) * SCALE
        mine_ref[1, :, head_cols(h)] = query[:tok].astype(BF16)
        other_ref[1, :, head_cols(h)] = query[tok:].astype(BF16)
        queries = q_ref[:, head_cols(h)]
        keyland_ref[:, head_cols(h)] = dot(g_score, queries, TN) * SCALE


def grad_context_body(got_ref, inv_ref, kept_ref, out_ref, g_ref):
    count, rows, _ = got_ref.shape
    cols = (rows - 8) // 2
    got = got_ref[0].astype(F32)
    for place in range(1, count):
        got = got + got_ref[place].astype(F32)
    g_mixing = joined(got[: 2 * cols])
    gain = high_low(got[2 * cols : 2 * cols + 1] + got[2 * cols + 1 : 2 * cols + 2])
    context = kept_ref[:cols]
    total = kept_ref[cols : cols + 1]
    top = kept_ref[cols + 1 : cols + 2]
    g_context = exact(g_mixing, inv_ref[...], NT)
    high, low = high_low(-jnp.sum(g_context * context, axis=0, keepdims=True) / total)
    tail = rows_of(
        *[row[:, part] for row in (high, low) for part in HALVES],
        *gain,
        *[top[:, part] for part in HALVES],
    )
    mine = jnp.concatenate([halves(g_context / total), tail], axis=0).astype(BF16)
    for place in range(count):
        out_ref[place] = mine
    g_ref[...] = g_mixing


def inverse_back_body(ids_ref, inv_ref, kept_ref, g_ref, land_ref, keyland_ref, out_ref):
    half = land_ref.shape[1] // 2
    at = pl.multiple_of(ids_ref[1] * DH, DH)
    lq = land_ref[:, pl.ds(at, DH)]
    lk = land_ref[:, pl.ds(at + half, DH)]
    ktwo, x, h2, h3, p1, b2, b3 = [inv_ref[place] for place in range(7)]
    factor = column_factor(ktwo)
    ktwo_s, x_s, h3_s, p1_s = [split_up(part) for part in (ktwo, x, h3, p1)]
    g_mixing = split_up(g_ref[...])
    n = g_ref.shape[0]
    context = kept_ref[:n]
    once = exact(context, p1_s)
    inner = exact(context, b3)
    u = jnp.concatenate([-context, once, -exact(once, p1_s)], axis=0)
    r0 = jnp.concatenate([inner, 0.25 * exact(u, x_s)], axis=0)
    r1 = exact(r0, x_s)
    left = jnp.concatenate([u, r0, r1, exact(r1, x_s)], axis=0)
    d_outer = (factor * 0.0625) * exact(g_mixing, ktwo_s, NT)
    d = exact(d_outer, h3_s)
    v = jnp.concatenate([exact(d, b2), 7.0 * d - exact(d, p1_s), d], axis=0)
    s0 = jnp.concatenate([d_outer, v], axis=0)
    right = jnp.concatenate(
        [0.25 * exact(v, h3_s), -exact(s0, h2), 7.0 * s0 - exact(s0, x_s), -s0], axis=0
    )
    d_x = exact(left, right, TN)
    outer = exact(inner, h3_s)
    d_ktwo = (factor * 0.0625) * exact(outer, g_mixing, TN) + factor * exact(
        d_x + jnp.transpose(d_x), ktwo_s
    )
    g_score = ktwo * (d_ktwo - jnp.sum(ktwo * d_ktwo, axis=1, keepdims=True))
    out_ref[:, :half] = jnp.zeros((M, half), F32)
    out_ref[:, half:] = keyland_ref[...]
    high, low = split_up(g_score)
    out_ref[:, pl.ds(at, DH)] = (dot(high, lk) + dot(low, lk)) * SCALE
    out_ref[:, pl.ds(at + half, DH)] = keyland_ref[:, pl.ds(at, DH)] + (
        (dot(high, lq, TN) + dot(low, lq, TN)) * SCALE
    )


def unpacked(got, h, heads):
    count, rows, _ = got.shape
    per_head = count // heads
    cols = (rows - 8) // 2
    parts = [got[h * per_head + j] for j in range(per_head)]
    g_weighted = jnp.concatenate(
        [
            jnp.concatenate([part[:cols], part[cols : 2 * cols]], axis=1)
            for part in parts
        ],
        axis=0,
    )
    tails = [part.astype(F32)[2 * cols :] for part in parts]
    summed = functools.reduce(jnp.add, tails)
    g_totals = joined(summed[0:2] + summed[2:4])
    top = joined(tails[0][6:8])
    gain = tails[0][4:5] + tails[0][5:6]
    return g_weighted, g_totals, top, gain


def queryland_body(
    got_ref, exp_ref, k_ref, v_ref, extra_ref, land_ref, out_ref, pass_ref
):
    heads = exp_ref.shape[0]
    half = heads * DH
    for h in range(heads):
        g_weighted, g_totals, top, _ = unpacked(got_ref, h, heads)
        keys = k_ref[:, head_cols(h)]
        vals = v_ref[:, head_cols(h)]
        tok = keys.shape[0]
        shift = exp_ref[h, tok:].astype(F32)[0:1]
        exp_three = exp_ref[h, :tok].astype(F32) * jnp.exp(shift - top)
        g_score = (exp_three * (dot(vals, g_weighted) + g_totals)).astype(BF16)
        queryland = dot(g_score, keys, TN) * SCALE
        out_ref[:, head_cols(h)] = (queryland + extra_ref[:, head_cols(h)]).astype(BF16)
    out_ref[:, half:] = extra_ref[:, half:].astype(BF16)
    count, rows, _ = got_ref.shape
    for place in range(count):
        pass_ref[place * rows : (place + 1) * rows] = got_ref[place]
    for h in range(heads):
        at = count * rows + h * M
        pass_ref[at : at + M] = land_ref[:, head_cols(h)]


class Parts:
    def __init__(self, ref, count, rows):
        self.ref, self.shape = ref, (count, rows, ref.shape[1])

    def __getitem__(self, place):
        rows = self.shape[1]
        return self.ref[place * rows : (place + 1) * rows]


def value_body(
    count, ids_ref, k_ref, v_ref, pass_ref, pass_there, value_out, key_out, gain_out
):
    heads = k_ref.shape[1] // (2 * DH)
    total = pass_ref.shape[0] - heads * M

    def place_halves(core, own, away):
        for place, ref in ((own, pass_ref), (away, pass_there)):
            for h in range(heads):
                cols = slice(place.start + h * DH, place.start + (h + 1) * DH)
                g_weighted, g_totals, top, gain = unpacked(
                    Parts(ref, count, total // count), h, heads
                )
                lq = ref[total + h * M : total + (h + 1) * M]
                exp_three = jnp.exp(dot(k_ref[:, cols], lq, NT) * SCALE - top)
                g_exp = dot(v_ref[:, cols], g_weighted) + g_totals
                value_out[:, cols] = dot(exp_three.astype(BF16), g_weighted, NT).astype(BF16)
                key_out[:, cols] = dot((exp_three * g_exp).astype(BF16), lq) * SCALE
                gain_out[:, cols] = gain

    by_core(ids_ref, place_halves)


def by_core(ids_ref, place_halves):
    half = 2 * DH
    left, right = slice(0, half), slice(half, 2 * half)

    @pl.when(ids_ref[0] == 0)
    def _():
        place_halves(0, left, right)

    @pl.when(ids_ref[0] != 0)
    def _():
        place_halves(1, right, left)


def gather_body(ids_ref, mine_ref, there_ref, norm_out):
    def place_halves(core, own, away):
        norm_out[:, own] = mine_ref[0]
        norm_out[:, away] = there_ref[0]

    by_core(ids_ref, place_halves)


def finish_body(
    ids_ref, got_ref, mine_ref, there_ref, key_ref, query_out, key_out
):
    count, land_dev, both = got_ref.shape
    _, tok, half = mine_ref.shape
    seg_len = tok // land_dev
    lands = []
    for core in range(2):
        got = got_ref[core].astype(F32)
        for chip in range(1, count // 2):
            got = got + got_ref[2 * chip + core].astype(F32)
        lands.append(got / seg_len)
    spans = [(row, slice(row * seg_len, (row + 1) * seg_len)) for row in range(land_dev)]

    def place_halves(core, own, away):
        for place, land, ref in (
            (own, lands[core], mine_ref), (away, lands[1 - core], there_ref)
        ):
            for row, span in spans:
                query_out[span, place] = (
                    ref[1, span].astype(F32) + land[row : row + 1, :half]
                ).astype(BF16)

    by_core(ids_ref, place_halves)
    for core in range(2):
        place = slice(core * half, (core + 1) * half)
        for row, span in spans:
            key_out[span, place] = (
                key_ref[span, place] + lands[core][row : row + 1, half:]
            ).astype(BF16)


def on_device(queries, keys_in, values, norm_gain, out_grad):
    tok, width = queries.shape
    half = width // 2
    heads = half // DH
    n_ctx = lax.axis_size("ctx")
    n_head = lax.axis_size("head")
    chips = n_ctx // 2
    per_head = chips // heads
    cols = DH // per_head
    land_dev = M // n_ctx
    here = lax.axis_index("ctx").astype(jnp.int32)
    ids = jnp.stack([lax.rem(here, 2), lax.div(here, 2 * per_head)])
    gain = norm_gain.reshape(1, width)
    same_core = [list(range(core, n_ctx, 2)) for core in range(2)]
    same_chip = [
        [(2 * chip + core) * n_head + z for core in range(2) for z in range(n_head)]
        for chip in range(chips)
    ]
    swap = [(i, i ^ 1) for i in range(n_ctx)]
    packed = shape(chips, 2 * cols + 8, DH, dtype=BF16)
    pair = shape(2, tok, half, dtype=BF16)
    wide_b = shape(tok, width, dtype=BF16)
    units = shape(heads, 2 * tok, M, dtype=BF16)

    both_b = shape(2 * tok, half, dtype=BF16)
    (own,) = call(
        means_body, [shape(n_ctx, land_dev, 2 * half, dtype=BF16)], queries, keys_in,
        far_in=(0, 1), far_out=(0,), vmem=MOST_VMEM, flops=10**6, name="landmark_means",
    )
    held = lax.optimization_barrier((own, keys_in, values, queries, out_grad))
    k_there, v_there, q_there, g_there = [lax.ppermute(x, "ctx", swap) for x in held[1:]]
    land = exchange(own, "ctx").reshape(M, 2 * half)
    keys, vals = call(
        stack_body, [both_b, both_b], ids, keys_in, values, k_there, v_there,
        scalars=1, after=(own,), flops=10**6, name="stack_kv",
    )

    (parts,) = call(context_body, [packed], land, keys, vals, flops=10**8, name="local_context")
    got = exchange(parts, "ctx", same_core)
    inverse, inverse_again, chain = call(
        inverse_body, [shape(M, M), shape(M, M), shape(7, M, M)], ids, land,
        scalars=1, after=(parts,), flops=3 * 10**9, name="inverse",
    )
    parts, kept = call(
        mixing_body, [shape(chips, cols, M, dtype=BF16), shape(cols + 8, M)],
        got, inverse, flops=10**8, name="mixing",
    )
    qs, grads = call(
        stack_body, [both_b, both_b], ids, queries, out_grad, q_there, g_there,
        scalars=1, after=(parts,), flops=10**6, name="stack_qg",
    )
    kone, exp_local = call(
        ahead_body, [units, shape(heads, 2 * tok + 16, M, dtype=BF16)], qs, keys, land,
        after=(parts,), flops=2 * 10**9, name="ahead",
    )
    mixing = exchange(parts, "ctx", same_core).reshape(heads, DH, M)

    output, sums = call(
        output_body, [shape(2 * tok, half), shape(2 * n_head, 2, 2 * tok)],
        ids, kone, mixing, grads, gain, scalars=1, flops=10**8, name="output",
    )
    sums = exchange(sums, ("ctx", "head"), same_chip)
    (parts,) = call(
        norm_body, [packed], ids, sums, output, grads, gain, kone,
        scalars=1, flops=10**8, name="norm",
    )
    got = exchange(parts, "ctx", same_core)
    mine, other, keyland = call(
        query_body, [pair, pair, shape(M, half)],
        ids, sums, output, grads, gain, mixing, qs, land,
        scalars=1, after=(parts,), flops=2 * 10**9, name="kernel_one_back",
    )
    parts, g_mixing = call(
        grad_context_body, [packed, shape(cols, M)], got, inverse_again, kept,
        after=(other,), flops=10**8, name="context_back",
    )
    got = exchange(parts, "ctx", same_core)
    (extra,) = call(
        inverse_back_body, [shape(M, 2 * half)], ids, chain, kept, g_mixing, land, keyland,
        scalars=1, after=(parts,), flops=5 * 10**9, name="inverse_back",
    )
    both, passed = call(
        queryland_body,
        [shape(M, 2 * half, dtype=BF16), shape(chips * (2 * cols + 8) + heads * M, DH, dtype=BF16)],
        got, exp_local, keys, vals, extra, land, flops=10**8, name="landmarks_back",
    )
    landed = exchange(both.reshape(n_ctx, land_dev, 2 * half), "ctx")
    there = lax.ppermute(other, "ctx", swap)
    passed_there = lax.ppermute(passed, "ctx", swap)
    (normed,) = call(
        gather_body, [wide_b], ids, mine, there,
        scalars=1, after=(both,), flops=10**6, name="gather",
    )
    value_grad, key_three, gain_grad = call(
        functools.partial(value_body, chips), [wide_b, shape(tok, width), shape(1, width)],
        ids, keys_in, values, passed, passed_there,
        scalars=1, after=(both,), flops=2 * 10**9, name="kernel_three_back",
    )
    query_grad, key_grad = call(
        finish_body, [wide_b, wide_b], ids, landed, mine, there, key_three,
        scalars=1, after=(normed,), flops=10**6, name="finish",
    )
    return (normed, query_grad, key_grad, value_grad, gain_grad.reshape(width))


def solution(mesh):
    return jax.shard_map(
        on_device,
        mesh=mesh,
        in_specs=(
            P("ctx", "head"),
            P("ctx", "head"),
            P("ctx", "head"),
            P("head"),
            P("ctx", "head"),
        ),
        out_specs=(
            P("ctx", "head"),
            P("ctx", "head"),
            P("ctx", "head"),
            P("ctx", "head"),
            P("head"),
        ),
        check_vma=False,
    )
```

```python
import functools

import jax
import jax.numpy as jnp
from jax import lax
from jax.experimental import pallas as pl
from jax.experimental.pallas import tpu as pltpu
from jax.sharding import PartitionSpec as P

DH = 128
M = 256
EPS = 1e-06
F32 = jnp.float32
BF16 = jnp.bfloat16
SCALE = DH ** (-0.5)
VMEM_BYTES = 32 * 1024 * 1024
MOST_VMEM = 60 * 1024 * 1024
HALVES = (slice(0, DH), slice(DH, 2 * DH))

NN = (((1,), (0,)), ((), ()))
NT = (((1,), (1,)), ((), ()))
TN = (((0,), (0,)), ((), ()))


def dot(a, b, dims=NN):
    return lax.dot_general(a, b, dims, preferred_element_type=F32)


def split_up(x):
    high = x.astype(BF16)
    return high, (x - high.astype(F32)).astype(BF16)


def exact(a, b, dims=NN):
    a_high, a_low = a if isinstance(a, tuple) else split_up(a)
    b_high, b_low = b if isinstance(b, tuple) else split_up(b)
    if dims == TN:
        return dot(a_high, b_high, dims) + (
            dot(a_high, b_low, dims) + dot(a_low, b_high, dims)
        )
    n = a_high.shape[0]
    both = dot(jnp.concatenate([a_high, a_low], axis=0), b_high, dims)
    return both[:n] + (both[n:] + dot(a_high, b_low, dims))


def exchange(parts, axis, groups=None):
    return lax.all_to_all(parts, axis, 0, 0, axis_index_groups=groups)


def high_low(x):
    high = x.astype(BF16).astype(F32)
    return high, x - high


def rows_of(*rows):
    index = lax.broadcasted_iota(jnp.int32, (8, rows[0].shape[1]), 0)
    out = jnp.zeros((8, rows[0].shape[1]), F32)
    for place, row in enumerate(rows):
        out = jnp.where(index == place, row, out)
    return out


def eye_times(value):
    row = lax.broadcasted_iota(jnp.int32, (M, M), 0)
    col = lax.broadcasted_iota(jnp.int32, (M, M), 1)
    return jnp.where(row == col, value, 0.0).astype(F32)


def head_cols(h):
    return slice(h * DH, (h + 1) * DH)


def halves(x):
    return jnp.concatenate([x[:, :DH], x[:, DH:]], axis=0)


def joined(x):
    n = x.shape[0] // 2
    return jnp.concatenate([x[:n], x[n:]], axis=1)


def own_head(ids_ref, h):
    return pl.ds(pl.multiple_of((ids_ref[0] * 2 + h) * DH, DH), DH)


def stacked(ids_ref, refs, h):
    return jnp.concatenate([ref[:, own_head(ids_ref, h)] for ref in refs], axis=0)


def rows_of(*rows):
    index = lax.broadcasted_iota(jnp.int32, (8, rows[0].shape[1]), 0)
    out = jnp.zeros((8, rows[0].shape[1]), F32)
    for place, row in enumerate(rows):
        out = jnp.where(index == place, row, out)
    return out


def eye_times(value):
    row = lax.broadcasted_iota(jnp.int32, (M, M), 0)
    col = lax.broadcasted_iota(jnp.int32, (M, M), 1)
    return jnp.where(row == col, value, 0.0).astype(F32)


def head_cols(h):
    return slice(h * DH, (h + 1) * DH)


def halves(x):
    return jnp.concatenate([x[:, :DH], x[:, DH:]], axis=0)


def joined(x):
    n = x.shape[0] // 2
    return jnp.concatenate([x[:n], x[n:]], axis=1)


def both_blocks(mine_ref, other_ref, which, h):
    return jnp.concatenate(
        [ref[which, :, head_cols(h)] for ref in (mine_ref, other_ref)], axis=0
    )


def call(
    body, outs, *args, scalars=0, far_in=(), far_out=(), after=(), flops=0,
    vmem=VMEM_BYTES, name
):
    nbytes = sum(a.size * a.dtype.itemsize for a in (*args, *outs))
    n_in, n_after, n_out = len(args), len(after), len(outs)
    n_far = len(far_in) + len(far_out)

    def whole(*refs):
        ins = list(refs[:n_in])
        results = list(refs[n_in + n_after : n_in + n_after + n_out])
        buffers = refs[n_in + n_after + n_out :]
        loads, stores = [], []
        for k, i in enumerate(far_in):
            loads.append(pltpu.make_async_copy(ins[i], buffers[k], buffers[n_far].at[k]))
            ins[i] = buffers[k]
        for k, i in enumerate(far_out, len(far_in)):
            stores.append(
                pltpu.make_async_copy(buffers[k], results[i], buffers[n_far].at[k])
            )
            results[i] = buffers[k]
        for copy in loads:
            copy.start()
        for copy in loads:
            copy.wait()
        body(*ins, *results)
        for copy in stores:
            copy.start()
        for copy in stores:
            copy.wait()

    def space(place, far):
        return pl.BlockSpec(memory_space=pltpu.HBM if place in far else pltpu.VMEM)

    in_specs = [
        pl.BlockSpec(memory_space=pltpu.SMEM) if i < scalars else space(i, far_in)
        for i in range(n_in)
    ] + [pl.BlockSpec(memory_space=pl.ANY)] * n_after
    scratch = [pltpu.VMEM(args[i].shape, args[i].dtype) for i in far_in]
    scratch += [pltpu.VMEM(outs[i].shape, outs[i].dtype) for i in far_out]
    if n_far:
        scratch.append(pltpu.SemaphoreType.DMA((n_far,)))
    return pl.pallas_call(
        whole,
        out_shape=outs,
        in_specs=in_specs,
        out_specs=[space(i, far_out) for i in range(n_out)],
        scratch_shapes=scratch,
        compiler_params=pltpu.CompilerParams(vmem_limit_bytes=vmem),
        cost_estimate=pl.CostEstimate(flops=flops, bytes_accessed=nbytes, transcendentals=0),
        name=name,
    )(*args, *after)


def shape(*dims, dtype=F32):
    return jax.ShapeDtypeStruct(dims, dtype)


def means_body(q_ref, k_ref, out_ref):
    count, land_dev, both = out_ref.shape
    half = both // 2
    seg_len = q_ref.shape[0] // land_dev
    q_mean, k_mean = [
        jnp.sum(ref[...].astype(F32).reshape(land_dev, seg_len, 2 * half), axis=1) / seg_len
        for ref in (q_ref, k_ref)
    ]
    for core in range(2):
        cols = slice(core * half, (core + 1) * half)
        own = jnp.concatenate([q_mean[:, cols], k_mean[:, cols]], axis=1).astype(BF16)
        for chip in range(count // 2):
            out_ref[2 * chip + core] = own


def stack_body(ids_ref, *refs):
    count = len(refs) // 3
    for mine, there, out in zip(refs[:count], refs[count : 2 * count], refs[2 * count :]):
        for h in range(out.shape[1] // DH):
            out[:, head_cols(h)] = stacked(ids_ref, (mine, there), h)


def stack_turned_body(ids_ref, q_ref, g_ref, q_there, g_there, q_out, g_out):
    for h in range(q_out.shape[1] // DH):
        q_out[:, head_cols(h)] = stacked(ids_ref, (q_ref, q_there), h)
        g_out[head_cols(h)] = jnp.transpose(stacked(ids_ref, (g_ref, g_there), h))


def context_body(land_ref, k_ref, v_ref, out_ref):
    count = out_ref.shape[0]
    heads = land_ref.shape[1] // (2 * DH)
    per_head = count // heads
    cols = DH // per_head
    for h in range(heads):
        keys = k_ref[:, head_cols(h)]
        vals = v_ref[:, head_cols(h)]
        score = dot(keys, land_ref[:, head_cols(h)], NT) * SCALE
        shift = jnp.max(score, axis=0, keepdims=True).astype(BF16).astype(F32)
        exp_local = jnp.exp(score - shift)
        high, low = high_low(jnp.sum(exp_local, axis=0, keepdims=True))
        weighted = dot(vals, exp_local.astype(BF16), TN)
        stats = rows_of(*[row[:, part] for row in (shift, high, low) for part in HALVES])
        for j in range(per_head):
            out_ref[h * per_head + j] = jnp.concatenate(
                [halves(weighted[j * cols : (j + 1) * cols]), stats], axis=0
            ).astype(BF16)


def inverse_body(ids_ref, land_ref, first_ref, again_ref, out_ref):
    half = land_ref.shape[1] // 2
    at = pl.multiple_of(ids_ref[1] * DH, DH)
    lq = land_ref[:, pl.ds(at, DH)]
    lk = land_ref[:, pl.ds(at + half, DH)]
    score = dot(lq, lk, NT) * SCALE
    top = jnp.exp(score - jnp.max(score, axis=1, keepdims=True))
    ktwo = top / jnp.sum(top, axis=1, keepdims=True)
    factor = column_factor(ktwo)
    ktwo_s = split_up(ktwo)
    x = factor * exact(ktwo_s, ktwo_s, NT)
    x_s = split_up(x)
    h2 = eye_times(15.0) - exact(x_s, eye_times(7.0) - x)
    h3 = eye_times(13.0) - exact(x_s, h2)
    h3_s = split_up(h3)
    p1 = 0.25 * exact(x_s, h3_s)
    p1_s = split_up(p1)
    b2 = eye_times(15.0) - exact(p1_s, eye_times(7.0) - p1)
    b3 = eye_times(13.0) - exact(p1_s, b2)
    inverse = (factor * 0.0625) * exact(b3, exact(h3_s, ktwo_s))
    first_ref[...] = inverse
    again_ref[...] = inverse
    for place, part in enumerate((ktwo, x, h2, h3, p1, b2, b3)):
        out_ref[place] = part


def column_factor(ktwo):
    return 1.0 / jnp.max(jnp.sum(ktwo, axis=0, keepdims=True), axis=1, keepdims=True)


def mixing_body(got_ref, inv_ref, out_ref, kept_ref):
    count, rows, _ = got_ref.shape
    cols = (rows - 8) // 2
    tops = got_ref[0].astype(F32)[rows - 8 :]
    for place in range(1, count):
        tops = jnp.maximum(tops, got_ref[place].astype(F32)[rows - 8 :])
    tops = tops[0:2]
    total = jnp.zeros((2, DH), F32)
    left = jnp.zeros((cols, DH), F32)
    right = jnp.zeros((cols, DH), F32)
    for place in range(count):
        part = got_ref[place].astype(F32)
        stats = part[rows - 8 :]
        fade = jnp.exp(stats[0:2] - tops)
        total = total + fade * (stats[2:4] + stats[4:6])
        left = left + fade[0:1] * part[:cols]
        right = right + fade[1:2] * part[cols : 2 * cols]
    total = joined(total)
    context = jnp.concatenate([left, right], axis=1) / total
    mixing = exact(context, inv_ref[...]).astype(BF16)
    for place in range(count):
        out_ref[place] = mixing
    kept_ref[...] = jnp.concatenate([context, rows_of(total, joined(tops))], axis=0)


def softmax_rows(score):
    top = jnp.exp(score - jnp.max(score, axis=1, keepdims=True))
    return top / jnp.sum(top, axis=1, keepdims=True)


def kernel_one(q_ref, land_ref, h):
    heads = land_ref.shape[1] // (2 * DH)
    score = dot(q_ref[:, head_cols(h)], land_ref[:, head_cols(heads + h)], NT) * SCALE
    return softmax_rows(score)


def ahead_body(
    q_ref, k_ref, land_ref, kone_ref, exp_ref
):
    heads, tok, _ = kone_ref.shape
    for h in range(heads):
        kone = kernel_one(q_ref, land_ref, h).astype(BF16)
        kone_ref[h] = kone
        keys = k_ref[:, head_cols(h)]
        score = dot(keys, land_ref[:, head_cols(h)], NT) * SCALE
        shift = jnp.max(score, axis=0, keepdims=True).astype(BF16).astype(F32)
        exp_ref[h, :tok] = jnp.exp(score - shift).astype(BF16)
        exp_ref[h, tok:] = jnp.broadcast_to(shift, (16, M)).astype(BF16)


def gain_column(ids_ref, gain_ref, h):
    row = jnp.broadcast_to(gain_ref[:, own_head(ids_ref, h)], (8, DH))
    return jnp.transpose(row)[:, 0:1]


def output_body(ids_ref, kone_ref, mix_ref, g_ref, gain_ref, out_ref, sum_ref):
    heads, tok, _ = kone_ref.shape
    squares = jnp.zeros((DH, tok), F32)
    slopes = jnp.zeros((DH, tok), F32)
    for h in range(heads):
        out = dot(mix_ref[h], kone_ref[h], NT)
        out_ref[head_cols(h)] = out
        scaled = g_ref[head_cols(h)].astype(F32) * gain_column(ids_ref, gain_ref, h)
        squares = squares + out * out
        slopes = slopes + scaled * out
    both = rows_of(
        *[
            swap_blocks(ids_ref, jnp.sum(part, axis=0, keepdims=True), 1)
            for part in (squares, slopes)
        ]
    )
    for place in range(sum_ref.shape[0]):
        sum_ref[place] = both[:2]


def swap_blocks(ids_ref, x, axis):
    size = x.shape[axis] // 2
    left = lax.slice_in_dim(x, 0, size, axis=axis)
    right = lax.slice_in_dim(x, size, 2 * size, axis=axis)
    swapped = jnp.concatenate([right, left], axis=axis)
    return jnp.where(ids_ref[0] == 0, x, swapped)


def token_factors(ids_ref, sum_ref, features):
    total = sum_ref[0]
    for place in range(1, sum_ref.shape[0]):
        total = total + sum_ref[place]
    root_inv = lax.rsqrt(total[0:1] / features + EPS)
    slope = total[1:2] * root_inv / features
    return swap_blocks(ids_ref, root_inv, 1), swap_blocks(ids_ref, root_inv * slope, 1)


def output_grad(factors, out, grad, gain):
    root_inv, bent = factors
    return (root_inv * (grad * gain - out * bent)).astype(BF16)


def norm_body(ids_ref, sum_ref, out_ref, g_ref, gain_ref, kone_ref, part_ref):
    heads = kone_ref.shape[0]
    per_head = part_ref.shape[0] // heads
    cols = DH // per_head
    factors = token_factors(ids_ref, sum_ref, heads * DH * sum_ref.shape[0])
    for h in range(heads):
        out = out_ref[head_cols(h)]
        grad = g_ref[head_cols(h)].astype(F32)
        gain = gain_column(ids_ref, gain_ref, h)
        g_mixing = dot(output_grad(factors, out, grad, gain), kone_ref[h])
        gain_sum = jnp.sum(grad * (out * factors[0]), axis=1, keepdims=True)
        gain_sum = jnp.transpose(jnp.broadcast_to(gain_sum, (DH, DH)))[0:1]
        tail = rows_of(*high_low(gain_sum))
        for j in range(per_head):
            part_ref[h * per_head + j] = jnp.concatenate(
                [halves(g_mixing[j * cols : (j + 1) * cols]), tail], axis=0
            ).astype(BF16)


def query_body(
    ids_ref, sum_ref, out_ref, g_ref, gain_ref, mix_ref, q_ref, land_ref,
    mine_ref, other_ref, keyland_ref,
):
    heads = mix_ref.shape[0]
    tok = mine_ref.shape[1]
    factors = token_factors(ids_ref, sum_ref, heads * DH * sum_ref.shape[0])
    for h in range(heads):
        out = out_ref[head_cols(h)]
        grad = g_ref[head_cols(h)].astype(F32)
        gain = gain_column(ids_ref, gain_ref, h)
        normed = jnp.transpose(out * factors[0] * gain).astype(BF16)
        mine_ref[0, :, head_cols(h)] = normed[:tok]
        other_ref[0, :, head_cols(h)] = normed[tok:]
        kone = kernel_one(q_ref, land_ref, h)
        g_kernel = dot(output_grad(factors, out, grad, gain), mix_ref[h], TN)
        inner = jnp.sum(kone * g_kernel, axis=1, keepdims=True)
        g_score = (kone * (g_kernel - inner)).astype(BF16)
        query = dot(g_score, land_ref[:, head_cols(heads + h)]) * SCALE
        mine_ref[1, :, head_cols(h)] = query[:tok].astype(BF16)
        other_ref[1, :, head_cols(h)] = query[tok:].astype(BF16)
        queries = q_ref[:, head_cols(h)]
        keyland_ref[:, head_cols(h)] = dot(g_score, queries, TN) * SCALE


def grad_context_body(got_ref, inv_ref, kept_ref, out_ref, g_ref):
    count, rows, _ = got_ref.shape
    cols = (rows - 8) // 2
    got = got_ref[0].astype(F32)
    for place in range(1, count):
        got = got + got_ref[place].astype(F32)
    g_mixing = joined(got[: 2 * cols])
    gain = high_low(got[2 * cols : 2 * cols + 1] + got[2 * cols + 1 : 2 * cols + 2])
    context = kept_ref[:cols]
    total = kept_ref[cols : cols + 1]
    top = kept_ref[cols + 1 : cols + 2]
    g_context = exact(g_mixing, inv_ref[...], NT)
    high, low = high_low(-jnp.sum(g_context * context, axis=0, keepdims=True) / total)
    tail = rows_of(
        *[row[:, part] for row in (high, low) for part in HALVES],
        *gain,
        *[top[:, part] for part in HALVES],
    )
    mine = jnp.concatenate([halves(g_context / total), tail], axis=0).astype(BF16)
    for place in range(count):
        out_ref[place] = mine
    g_ref[...] = g_mixing


def inverse_back_body(ids_ref, inv_ref, kept_ref, g_ref, land_ref, keyland_ref, out_ref):
    half = land_ref.shape[1] // 2
    at = pl.multiple_of(ids_ref[1] * DH, DH)
    lq = land_ref[:, pl.ds(at, DH)]
    lk = land_ref[:, pl.ds(at + half, DH)]
    ktwo, x, h2, h3, p1, b2, b3 = [inv_ref[place] for place in range(7)]
    factor = column_factor(ktwo)
    ktwo_s, x_s, h3_s, p1_s = [split_up(part) for part in (ktwo, x, h3, p1)]
    g_mixing = split_up(g_ref[...])
    n = g_ref.shape[0]
    context = kept_ref[:n]
    once = exact(context, p1_s)
    inner = exact(context, b3)
    u = jnp.concatenate([-context, once, -exact(once, p1_s)], axis=0)
    r0 = jnp.concatenate([inner, 0.25 * exact(u, x_s)], axis=0)
    r1 = exact(r0, x_s)
    left = jnp.concatenate([u, r0, r1, exact(r1, x_s)], axis=0)
    d_outer = (factor * 0.0625) * exact(g_mixing, ktwo_s, NT)
    d = exact(d_outer, h3_s)
    v = jnp.concatenate([exact(d, b2), 7.0 * d - exact(d, p1_s), d], axis=0)
    s0 = jnp.concatenate([d_outer, v], axis=0)
    right = jnp.concatenate(
        [0.25 * exact(v, h3_s), -exact(s0, h2), 7.0 * s0 - exact(s0, x_s), -s0], axis=0
    )
    d_x = exact(left, right, TN)
    outer = exact(inner, h3_s)
    d_ktwo = (factor * 0.0625) * exact(outer, g_mixing, TN) + factor * exact(
        d_x + jnp.transpose(d_x), ktwo_s
    )
    g_score = ktwo * (d_ktwo - jnp.sum(ktwo * d_ktwo, axis=1, keepdims=True))
    out_ref[:, :half] = jnp.zeros((M, half), F32)
    out_ref[:, half:] = keyland_ref[...]
    high, low = split_up(g_score)
    out_ref[:, pl.ds(at, DH)] = (dot(high, lk) + dot(low, lk)) * SCALE
    out_ref[:, pl.ds(at + half, DH)] = keyland_ref[:, pl.ds(at, DH)] + (
        (dot(high, lq, TN) + dot(low, lq, TN)) * SCALE
    )


def unpacked(got, h, heads):
    count, rows, _ = got.shape
    per_head = count // heads
    cols = (rows - 8) // 2
    parts = [got[h * per_head + j] for j in range(per_head)]
    g_weighted = jnp.concatenate(
        [
            jnp.concatenate([part[:cols], part[cols : 2 * cols]], axis=1)
            for part in parts
        ],
        axis=0,
    )
    tails = [part.astype(F32)[2 * cols :] for part in parts]
    summed = functools.reduce(jnp.add, tails)
    g_totals = joined(summed[0:2] + summed[2:4])
    top = joined(tails[0][6:8])
    gain = tails[0][4:5] + tails[0][5:6]
    return g_weighted, g_totals, top, gain


def queryland_body(
    got_ref, exp_ref, k_ref, v_ref, extra_ref, land_ref, out_ref, pass_ref
):
    heads = exp_ref.shape[0]
    half = heads * DH
    for h in range(heads):
        g_weighted, g_totals, top, _ = unpacked(got_ref, h, heads)
        keys = k_ref[:, head_cols(h)]
        vals = v_ref[:, head_cols(h)]
        tok = keys.shape[0]
        shift = exp_ref[h, tok:].astype(F32)[0:1]
        exp_three = exp_ref[h, :tok].astype(F32) * jnp.exp(shift - top)
        g_score = (exp_three * (dot(vals, g_weighted) + g_totals)).astype(BF16)
        queryland = dot(g_score, keys, TN) * SCALE
        out_ref[:, head_cols(h)] = (queryland + extra_ref[:, head_cols(h)]).astype(BF16)
    out_ref[:, half:] = extra_ref[:, half:].astype(BF16)
    count, rows, _ = got_ref.shape
    for place in range(count):
        pass_ref[place * rows : (place + 1) * rows] = got_ref[place]
    for h in range(heads):
        at = count * rows + h * M
        pass_ref[at : at + M] = land_ref[:, head_cols(h)]


class Parts:
    def __init__(self, ref, count, rows):
        self.ref, self.shape = ref, (count, rows, ref.shape[1])

    def __getitem__(self, place):
        rows = self.shape[1]
        return self.ref[place * rows : (place + 1) * rows]


def value_body(
    count, ids_ref, k_ref, v_ref, pass_ref, pass_there, value_out, key_out, gain_out
):
    heads = k_ref.shape[1] // (2 * DH)
    total = pass_ref.shape[0] - heads * M

    def place_halves(core, own, away):
        for place, ref in ((own, pass_ref), (away, pass_there)):
            for h in range(heads):
                cols = slice(place.start + h * DH, place.start + (h + 1) * DH)
                g_weighted, g_totals, top, gain = unpacked(
                    Parts(ref, count, total // count), h, heads
                )
                lq = ref[total + h * M : total + (h + 1) * M]
                exp_three = jnp.exp(dot(k_ref[:, cols], lq, NT) * SCALE - top)
                g_exp = dot(v_ref[:, cols], g_weighted) + g_totals
                value_out[:, cols] = dot(exp_three.astype(BF16), g_weighted, NT).astype(BF16)
                key_out[:, cols] = dot((exp_three * g_exp).astype(BF16), lq) * SCALE
                gain_out[:, cols] = gain

    by_core(ids_ref, place_halves)


def by_core(ids_ref, place_halves):
    half = 2 * DH
    left, right = slice(0, half), slice(half, 2 * half)

    @pl.when(ids_ref[0] == 0)
    def _():
        place_halves(0, left, right)

    @pl.when(ids_ref[0] != 0)
    def _():
        place_halves(1, right, left)


def gather_body(ids_ref, mine_ref, there_ref, norm_out):
    def place_halves(core, own, away):
        norm_out[:, own] = mine_ref[0]
        norm_out[:, away] = there_ref[0]

    by_core(ids_ref, place_halves)


def finish_body(
    ids_ref, got_ref, mine_ref, there_ref, key_ref, query_out, key_out
):
    count, land_dev, both = got_ref.shape
    _, tok, half = mine_ref.shape
    seg_len = tok // land_dev
    lands = []
    for core in range(2):
        got = got_ref[core].astype(F32)
        for chip in range(1, count // 2):
            got = got + got_ref[2 * chip + core].astype(F32)
        lands.append(got / seg_len)
    spans = [(row, slice(row * seg_len, (row + 1) * seg_len)) for row in range(land_dev)]

    def place_halves(core, own, away):
        for place, land, ref in (
            (own, lands[core], mine_ref), (away, lands[1 - core], there_ref)
        ):
            for row, span in spans:
                query_out[span, place] = (
                    ref[1, span].astype(F32) + land[row : row + 1, :half]
                ).astype(BF16)

    by_core(ids_ref, place_halves)
    for core in range(2):
        place = slice(core * half, (core + 1) * half)
        for row, span in spans:
            key_out[span, place] = (
                key_ref[span, place] + lands[core][row : row + 1, half:]
            ).astype(BF16)


def on_device(queries, keys_in, values, norm_gain, out_grad):
    tok, width = queries.shape
    half = width // 2
    heads = half // DH
    n_ctx = lax.axis_size("ctx")
    n_head = lax.axis_size("head")
    chips = n_ctx // 2
    per_head = chips // heads
    cols = DH // per_head
    land_dev = M // n_ctx
    here = lax.axis_index("ctx").astype(jnp.int32)
    ids = jnp.stack([lax.rem(here, 2), lax.div(here, 2 * per_head)])
    gain = norm_gain.reshape(1, width)
    same_core = [list(range(core, n_ctx, 2)) for core in range(2)]
    same_chip = [
        [(2 * chip + core) * n_head + z for core in range(2) for z in range(n_head)]
        for chip in range(chips)
    ]
    swap = [(i, i ^ 1) for i in range(n_ctx)]
    packed = shape(chips, 2 * cols + 8, DH, dtype=BF16)
    pair = shape(2, tok, half, dtype=BF16)
    wide_b = shape(tok, width, dtype=BF16)
    units = shape(heads, 2 * tok, M, dtype=BF16)

    both_b = shape(2 * tok, half, dtype=BF16)
    turned_b = shape(half, 2 * tok, dtype=BF16)
    (own,) = call(
        means_body, [shape(n_ctx, land_dev, 2 * half, dtype=BF16)], queries, keys_in,
        far_in=(0, 1), far_out=(0,), vmem=MOST_VMEM, flops=10**6, name="landmark_means",
    )
    held = lax.optimization_barrier((own, keys_in, values, queries, out_grad))
    k_there, v_there, q_there, g_there = [lax.ppermute(x, "ctx", swap) for x in held[1:]]
    land = exchange(own, "ctx").reshape(M, 2 * half)
    keys, vals = call(
        stack_body, [both_b, both_b], ids, keys_in, values, k_there, v_there,
        scalars=1, after=(own,), flops=10**6, name="stack_kv",
    )

    (parts,) = call(context_body, [packed], land, keys, vals, flops=10**8, name="local_context")
    got = exchange(parts, "ctx", same_core)
    inverse, inverse_again, chain = call(
        inverse_body, [shape(M, M), shape(M, M), shape(7, M, M)], ids, land,
        scalars=1, after=(parts,), flops=3 * 10**9, name="inverse",
    )
    parts, kept = call(
        mixing_body, [shape(chips, cols, M, dtype=BF16), shape(cols + 8, M)],
        got, inverse, flops=10**8, name="mixing",
    )
    qs, grads = call(
        stack_turned_body, [both_b, turned_b], ids, queries, out_grad, q_there, g_there,
        scalars=1, after=(parts,), flops=10**6, name="stack_qg",
    )
    kone, exp_local = call(
        ahead_body, [units, shape(heads, 2 * tok + 16, M, dtype=BF16)], qs, keys, land,
        after=(parts,), flops=2 * 10**9, name="ahead",
    )
    mixing = exchange(parts, "ctx", same_core).reshape(heads, DH, M)

    output, sums = call(
        output_body, [shape(half, 2 * tok), shape(2 * n_head, 2, 2 * tok)],
        ids, kone, mixing, grads, gain, scalars=1, flops=10**8, name="output",
    )
    sums = exchange(sums, ("ctx", "head"), same_chip)
    (parts,) = call(
        norm_body, [packed], ids, sums, output, grads, gain, kone,
        scalars=1, flops=10**8, name="norm",
    )
    got = exchange(parts, "ctx", same_core)
    mine, other, keyland = call(
        query_body, [pair, pair, shape(M, half)],
        ids, sums, output, grads, gain, mixing, qs, land,
        scalars=1, after=(parts,), flops=2 * 10**9, name="kernel_one_back",
    )
    parts, g_mixing = call(
        grad_context_body, [packed, shape(cols, M)], got, inverse_again, kept,
        after=(other,), flops=10**8, name="context_back",
    )
    got = exchange(parts, "ctx", same_core)
    (extra,) = call(
        inverse_back_body, [shape(M, 2 * half)], ids, chain, kept, g_mixing, land, keyland,
        scalars=1, after=(parts,), flops=5 * 10**9, name="inverse_back",
    )
    both, passed = call(
        queryland_body,
        [shape(M, 2 * half, dtype=BF16), shape(chips * (2 * cols + 8) + heads * M, DH, dtype=BF16)],
        got, exp_local, keys, vals, extra, land, flops=10**8, name="landmarks_back",
    )
    landed = exchange(both.reshape(n_ctx, land_dev, 2 * half), "ctx")
    there = lax.ppermute(other, "ctx", swap)
    passed_there = lax.ppermute(passed, "ctx", swap)
    (normed,) = call(
        gather_body, [wide_b], ids, mine, there,
        scalars=1, after=(both,), flops=10**6, name="gather",
    )
    value_grad, key_three, gain_grad = call(
        functools.partial(value_body, chips), [wide_b, shape(tok, width), shape(1, width)],
        ids, keys_in, values, passed, passed_there,
        scalars=1, after=(both,), flops=2 * 10**9, name="kernel_three_back",
    )
    query_grad, key_grad = call(
        finish_body, [wide_b, wide_b], ids, landed, mine, there, key_three,
        scalars=1, after=(normed,), flops=10**6, name="finish",
    )
    return (normed, query_grad, key_grad, value_grad, gain_grad.reshape(width))


def solution(mesh):
    return jax.shard_map(
        on_device,
        mesh=mesh,
        in_specs=(
            P("ctx", "head"),
            P("ctx", "head"),
            P("ctx", "head"),
            P("head"),
            P("ctx", "head"),
        ),
        out_specs=(
            P("ctx", "head"),
            P("ctx", "head"),
            P("ctx", "head"),
            P("ctx", "head"),
            P("head"),
        ),
        check_vma=False,
    )
```

```python
import functools

import jax
import jax.numpy as jnp
from jax import lax
from jax.experimental import pallas as pl
from jax.experimental.pallas import tpu as pltpu
from jax.sharding import PartitionSpec as P

DH = 128
M = 256
EPS = 1e-06
F32 = jnp.float32
BF16 = jnp.bfloat16
SCALE = DH ** (-0.5)
VMEM_BYTES = 32 * 1024 * 1024
MOST_VMEM = 60 * 1024 * 1024
HALVES = (slice(0, DH), slice(DH, 2 * DH))

NN = (((1,), (0,)), ((), ()))
NT = (((1,), (1,)), ((), ()))
TN = (((0,), (0,)), ((), ()))


def dot(a, b, dims=NN):
    return lax.dot_general(a, b, dims, preferred_element_type=F32)


def split_up(x):
    high = x.astype(BF16)
    return high, (x - high.astype(F32)).astype(BF16)


def exact(a, b, dims=NN):
    a_high, a_low = a if isinstance(a, tuple) else split_up(a)
    b_high, b_low = b if isinstance(b, tuple) else split_up(b)
    if dims == TN:
        return dot(a_high, b_high, dims) + (
            dot(a_high, b_low, dims) + dot(a_low, b_high, dims)
        )
    n = a_high.shape[0]
    both = dot(jnp.concatenate([a_high, a_low], axis=0), b_high, dims)
    return both[:n] + (both[n:] + dot(a_high, b_low, dims))


def exchange(parts, axis, groups=None):
    return lax.all_to_all(parts, axis, 0, 0, axis_index_groups=groups)


def high_low(x):
    high = x.astype(BF16).astype(F32)
    return high, x - high


def rows_of(*rows):
    index = lax.broadcasted_iota(jnp.int32, (8, rows[0].shape[1]), 0)
    out = jnp.zeros((8, rows[0].shape[1]), F32)
    for place, row in enumerate(rows):
        out = jnp.where(index == place, row, out)
    return out


def eye_times(value):
    row = lax.broadcasted_iota(jnp.int32, (M, M), 0)
    col = lax.broadcasted_iota(jnp.int32, (M, M), 1)
    return jnp.where(row == col, value, 0.0).astype(F32)


def head_cols(h):
    return slice(h * DH, (h + 1) * DH)


def halves(x):
    return jnp.concatenate([x[:, :DH], x[:, DH:]], axis=0)


def joined(x):
    n = x.shape[0] // 2
    return jnp.concatenate([x[:n], x[n:]], axis=1)


def own_head(ids_ref, h):
    return pl.ds(pl.multiple_of((ids_ref[0] * 2 + h) * DH, DH), DH)


def stacked(ids_ref, refs, h):
    return jnp.concatenate([ref[:, own_head(ids_ref, h)] for ref in refs], axis=0)


def rows_of(*rows):
    index = lax.broadcasted_iota(jnp.int32, (8, rows[0].shape[1]), 0)
    out = jnp.zeros((8, rows[0].shape[1]), F32)
    for place, row in enumerate(rows):
        out = jnp.where(index == place, row, out)
    return out


def eye_times(value):
    row = lax.broadcasted_iota(jnp.int32, (M, M), 0)
    col = lax.broadcasted_iota(jnp.int32, (M, M), 1)
    return jnp.where(row == col, value, 0.0).astype(F32)


def head_cols(h):
    return slice(h * DH, (h + 1) * DH)


def halves(x):
    return jnp.concatenate([x[:, :DH], x[:, DH:]], axis=0)


def joined(x):
    n = x.shape[0] // 2
    return jnp.concatenate([x[:n], x[n:]], axis=1)


def both_blocks(mine_ref, other_ref, which, h):
    return jnp.concatenate(
        [ref[which, :, head_cols(h)] for ref in (mine_ref, other_ref)], axis=0
    )


def call(
    body, outs, *args, scalars=0, far_in=(), far_out=(), after=(), flops=0,
    vmem=VMEM_BYTES, name
):
    nbytes = sum(a.size * a.dtype.itemsize for a in (*args, *outs))
    n_in, n_after, n_out = len(args), len(after), len(outs)
    n_far = len(far_in) + len(far_out)

    def whole(*refs):
        ins = list(refs[:n_in])
        results = list(refs[n_in + n_after : n_in + n_after + n_out])
        buffers = refs[n_in + n_after + n_out :]
        loads, stores = [], []
        for k, i in enumerate(far_in):
            loads.append(pltpu.make_async_copy(ins[i], buffers[k], buffers[n_far].at[k]))
            ins[i] = buffers[k]
        for k, i in enumerate(far_out, len(far_in)):
            stores.append(
                pltpu.make_async_copy(buffers[k], results[i], buffers[n_far].at[k])
            )
            results[i] = buffers[k]
        for copy in loads:
            copy.start()
        for copy in loads:
            copy.wait()
        body(*ins, *results)
        for copy in stores:
            copy.start()
        for copy in stores:
            copy.wait()

    def space(place, far):
        return pl.BlockSpec(memory_space=pltpu.HBM if place in far else pltpu.VMEM)

    in_specs = [
        pl.BlockSpec(memory_space=pltpu.SMEM) if i < scalars else space(i, far_in)
        for i in range(n_in)
    ] + [pl.BlockSpec(memory_space=pl.ANY)] * n_after
    scratch = [pltpu.VMEM(args[i].shape, args[i].dtype) for i in far_in]
    scratch += [pltpu.VMEM(outs[i].shape, outs[i].dtype) for i in far_out]
    if n_far:
        scratch.append(pltpu.SemaphoreType.DMA((n_far,)))
    return pl.pallas_call(
        whole,
        out_shape=outs,
        in_specs=in_specs,
        out_specs=[space(i, far_out) for i in range(n_out)],
        scratch_shapes=scratch,
        compiler_params=pltpu.CompilerParams(vmem_limit_bytes=vmem),
        cost_estimate=pl.CostEstimate(flops=flops, bytes_accessed=nbytes, transcendentals=0),
        name=name,
    )(*args, *after)


def shape(*dims, dtype=F32):
    return jax.ShapeDtypeStruct(dims, dtype)


def means_body(q_ref, k_ref, out_ref):
    count, land_dev, both = out_ref.shape
    half = both // 2
    seg_len = q_ref.shape[0] // land_dev
    q_mean, k_mean = [
        jnp.sum(ref[...].astype(F32).reshape(land_dev, seg_len, 2 * half), axis=1) / seg_len
        for ref in (q_ref, k_ref)
    ]
    for core in range(2):
        cols = slice(core * half, (core + 1) * half)
        own = jnp.concatenate([q_mean[:, cols], k_mean[:, cols]], axis=1).astype(BF16)
        for chip in range(count // 2):
            out_ref[2 * chip + core] = own


def stack_body(ids_ref, *refs):
    count = len(refs) // 3
    for mine, there, out in zip(refs[:count], refs[count : 2 * count], refs[2 * count :]):
        for h in range(out.shape[1] // DH):
            out[:, head_cols(h)] = stacked(ids_ref, (mine, there), h)


def stack_turned_body(ids_ref, q_ref, g_ref, q_there, g_there, q_out, g_out):
    for h in range(q_out.shape[1] // DH):
        q_out[:, head_cols(h)] = stacked(ids_ref, (q_ref, q_there), h)
        g_out[head_cols(h)] = jnp.transpose(stacked(ids_ref, (g_ref, g_there), h))


def context_body(land_ref, k_ref, v_ref, out_ref):
    count = out_ref.shape[0]
    heads = land_ref.shape[1] // (2 * DH)
    per_head = count // heads
    cols = DH // per_head
    for h in range(heads):
        keys = k_ref[:, head_cols(h)]
        vals = v_ref[:, head_cols(h)]
        score = dot(keys, land_ref[:, head_cols(h)], NT) * SCALE
        shift = jnp.max(score, axis=0, keepdims=True).astype(BF16).astype(F32)
        exp_local = jnp.exp(score - shift)
        high, low = high_low(jnp.sum(exp_local, axis=0, keepdims=True))
        weighted = dot(vals, exp_local.astype(BF16), TN)
        stats = rows_of(*[row[:, part] for row in (shift, high, low) for part in HALVES])
        for j in range(per_head):
            out_ref[h * per_head + j] = jnp.concatenate(
                [halves(weighted[j * cols : (j + 1) * cols]), stats], axis=0
            ).astype(BF16)


def inverse_body(ids_ref, land_ref, first_ref, again_ref, out_ref):
    half = land_ref.shape[1] // 2
    at = pl.multiple_of(ids_ref[1] * DH, DH)
    lq = land_ref[:, pl.ds(at, DH)]
    lk = land_ref[:, pl.ds(at + half, DH)]
    score = dot(lq, lk, NT) * SCALE
    top = jnp.exp(score - jnp.max(score, axis=1, keepdims=True))
    ktwo = top / jnp.sum(top, axis=1, keepdims=True)
    factor = column_factor(ktwo)
    ktwo_s = split_up(ktwo)
    x = factor * exact(ktwo_s, ktwo_s, NT)
    x_s = split_up(x)
    h2 = eye_times(15.0) - exact(x_s, eye_times(7.0) - x)
    h3 = eye_times(13.0) - exact(x_s, h2)
    h3_s = split_up(h3)
    p1 = 0.25 * exact(x_s, h3_s)
    p1_s = split_up(p1)
    b2 = eye_times(15.0) - exact(p1_s, eye_times(7.0) - p1)
    b3 = eye_times(13.0) - exact(p1_s, b2)
    inverse = (factor * 0.0625) * exact(b3, exact(h3_s, ktwo_s))
    first_ref[...] = inverse
    again_ref[...] = inverse
    for place, part in enumerate((ktwo, x, h2, h3, p1, b2, b3)):
        out_ref[place] = part


def column_factor(ktwo):
    return 1.0 / jnp.max(jnp.sum(ktwo, axis=0, keepdims=True), axis=1, keepdims=True)


def mixing_body(got_ref, inv_ref, out_ref, kept_ref):
    count, rows, _ = got_ref.shape
    cols = (rows - 8) // 2
    tops = got_ref[0].astype(F32)[rows - 8 :]
    for place in range(1, count):
        tops = jnp.maximum(tops, got_ref[place].astype(F32)[rows - 8 :])
    tops = tops[0:2]
    total = jnp.zeros((2, DH), F32)
    left = jnp.zeros((cols, DH), F32)
    right = jnp.zeros((cols, DH), F32)
    for place in range(count):
        part = got_ref[place].astype(F32)
        stats = part[rows - 8 :]
        fade = jnp.exp(stats[0:2] - tops)
        total = total + fade * (stats[2:4] + stats[4:6])
        left = left + fade[0:1] * part[:cols]
        right = right + fade[1:2] * part[cols : 2 * cols]
    total = joined(total)
    context = jnp.concatenate([left, right], axis=1) / total
    mixing = exact(context, inv_ref[...]).astype(BF16)
    for place in range(count):
        out_ref[place] = mixing
    kept_ref[...] = jnp.concatenate([context, rows_of(total, joined(tops))], axis=0)


def softmax_rows(score):
    top = jnp.exp(score - jnp.max(score, axis=1, keepdims=True))
    return top / jnp.sum(top, axis=1, keepdims=True)


def kernel_one(q_ref, land_ref, h):
    heads = land_ref.shape[1] // (2 * DH)
    score = dot(q_ref[:, head_cols(h)], land_ref[:, head_cols(heads + h)], NT) * SCALE
    return softmax_rows(score)


def ahead_body(
    q_ref, k_ref, land_ref, kone_ref, exp_ref
):
    heads, tok, _ = kone_ref.shape
    for h in range(heads):
        kone = kernel_one(q_ref, land_ref, h).astype(BF16)
        kone_ref[h] = kone
        keys = k_ref[:, head_cols(h)]
        score = dot(keys, land_ref[:, head_cols(h)], NT) * SCALE
        shift = jnp.max(score, axis=0, keepdims=True).astype(BF16).astype(F32)
        exp_ref[h, :tok] = jnp.exp(score - shift).astype(BF16)
        exp_ref[h, tok:] = jnp.broadcast_to(shift, (16, M)).astype(BF16)


def gain_column(ids_ref, gain_ref, h):
    row = jnp.broadcast_to(gain_ref[:, own_head(ids_ref, h)], (8, DH))
    return jnp.transpose(row)[:, 0:1]


def output_body(ids_ref, kone_ref, mix_ref, g_ref, gain_ref, out_ref, sum_ref):
    heads, tok, _ = kone_ref.shape
    squares = jnp.zeros((DH, tok), F32)
    slopes = jnp.zeros((DH, tok), F32)
    for h in range(heads):
        out = dot(mix_ref[h], kone_ref[h], NT)
        out_ref[head_cols(h)] = out
        scaled = g_ref[head_cols(h)].astype(F32) * gain_column(ids_ref, gain_ref, h)
        squares = squares + out * out
        slopes = slopes + scaled * out
    both = rows_of(
        *[
            swap_blocks(ids_ref, jnp.sum(part, axis=0, keepdims=True), 1)
            for part in (squares, slopes)
        ]
    )
    for place in range(sum_ref.shape[0]):
        sum_ref[place] = both[:2]


def swap_blocks(ids_ref, x, axis):
    size = x.shape[axis] // 2
    left = lax.slice_in_dim(x, 0, size, axis=axis)
    right = lax.slice_in_dim(x, size, 2 * size, axis=axis)
    swapped = jnp.concatenate([right, left], axis=axis)
    return jnp.where(ids_ref[0] == 0, x, swapped)


def token_factors(ids_ref, sum_ref, features):
    total = sum_ref[0]
    for place in range(1, sum_ref.shape[0]):
        total = total + sum_ref[place]
    root_inv = lax.rsqrt(total[0:1] / features + EPS)
    slope = total[1:2] * root_inv / features
    return swap_blocks(ids_ref, root_inv, 1), swap_blocks(ids_ref, root_inv * slope, 1)


def output_grad(factors, out, grad, gain):
    root_inv, bent = factors
    return (root_inv * (grad * gain - out * bent)).astype(BF16)


def norm_body(ids_ref, sum_ref, out_ref, g_ref, gain_ref, kone_ref, part_ref):
    heads = kone_ref.shape[0]
    per_head = part_ref.shape[0] // heads
    cols = DH // per_head
    factors = token_factors(ids_ref, sum_ref, heads * DH * sum_ref.shape[0])
    for h in range(heads):
        out = out_ref[head_cols(h)]
        grad = g_ref[head_cols(h)].astype(F32)
        gain = gain_column(ids_ref, gain_ref, h)
        g_mixing = dot(output_grad(factors, out, grad, gain), kone_ref[h])
        gain_sum = jnp.sum(grad * (out * factors[0]), axis=1, keepdims=True)
        gain_sum = jnp.transpose(jnp.broadcast_to(gain_sum, (DH, DH)))[0:1]
        tail = rows_of(*high_low(gain_sum))
        for j in range(per_head):
            part_ref[h * per_head + j] = jnp.concatenate(
                [halves(g_mixing[j * cols : (j + 1) * cols]), tail], axis=0
            ).astype(BF16)


def query_body(
    ids_ref, sum_ref, out_ref, g_ref, gain_ref, mix_ref, q_ref, land_ref,
    mine_ref, other_ref, keyland_ref,
):
    heads = mix_ref.shape[0]
    tok = mine_ref.shape[1]
    factors = token_factors(ids_ref, sum_ref, heads * DH * sum_ref.shape[0])
    for h in range(heads):
        out = out_ref[head_cols(h)]
        grad = g_ref[head_cols(h)].astype(F32)
        gain = gain_column(ids_ref, gain_ref, h)
        normed = jnp.transpose(out * factors[0] * gain).astype(BF16)
        mine_ref[0, :, head_cols(h)] = normed[:tok]
        other_ref[0, :, head_cols(h)] = normed[tok:]
        kone = kernel_one(q_ref, land_ref, h)
        g_kernel = dot(output_grad(factors, out, grad, gain), mix_ref[h], TN)
        inner = jnp.sum(kone * g_kernel, axis=1, keepdims=True)
        g_score = (kone * (g_kernel - inner)).astype(BF16)
        query = dot(g_score, land_ref[:, head_cols(heads + h)]) * SCALE
        mine_ref[1, :, head_cols(h)] = query[:tok].astype(BF16)
        other_ref[1, :, head_cols(h)] = query[tok:].astype(BF16)
        queries = q_ref[:, head_cols(h)]
        keyland_ref[:, head_cols(h)] = (dot(g_score, queries, TN) * SCALE).astype(BF16)


def grad_context_body(got_ref, inv_ref, kept_ref, out_ref, g_ref):
    count, rows, _ = got_ref.shape
    cols = (rows - 8) // 2
    got = got_ref[0].astype(F32)
    for place in range(1, count):
        got = got + got_ref[place].astype(F32)
    g_mixing = joined(got[: 2 * cols])
    gain = high_low(got[2 * cols : 2 * cols + 1] + got[2 * cols + 1 : 2 * cols + 2])
    context = kept_ref[:cols]
    total = kept_ref[cols : cols + 1]
    top = kept_ref[cols + 1 : cols + 2]
    g_context = exact(g_mixing, inv_ref[...], NT)
    high, low = high_low(-jnp.sum(g_context * context, axis=0, keepdims=True) / total)
    tail = rows_of(
        *[row[:, part] for row in (high, low) for part in HALVES],
        *gain,
        *[top[:, part] for part in HALVES],
    )
    mine = jnp.concatenate([halves(g_context / total), tail], axis=0).astype(BF16)
    for place in range(count):
        out_ref[place] = mine
    g_ref[...] = g_mixing


def inverse_back_body(ids_ref, inv_ref, kept_ref, g_ref, land_ref, out_ref):
    half = land_ref.shape[1] // 2
    at = pl.multiple_of(ids_ref[1] * DH, DH)
    lq = land_ref[:, pl.ds(at, DH)]
    lk = land_ref[:, pl.ds(at + half, DH)]
    ktwo, x, h2, h3, p1, b2, b3 = [inv_ref[place] for place in range(7)]
    factor = column_factor(ktwo)
    ktwo_s, x_s, h3_s, p1_s = [split_up(part) for part in (ktwo, x, h3, p1)]
    g_mixing = split_up(g_ref[...])
    n = g_ref.shape[0]
    context = kept_ref[:n]
    once = exact(context, p1_s)
    inner = exact(context, b3)
    u = jnp.concatenate([-context, once, -exact(once, p1_s)], axis=0)
    r0 = jnp.concatenate([inner, 0.25 * exact(u, x_s)], axis=0)
    r1 = exact(r0, x_s)
    left = jnp.concatenate([u, r0, r1, exact(r1, x_s)], axis=0)
    d_outer = (factor * 0.0625) * exact(g_mixing, ktwo_s, NT)
    d = exact(d_outer, h3_s)
    v = jnp.concatenate([exact(d, b2), 7.0 * d - exact(d, p1_s), d], axis=0)
    s0 = jnp.concatenate([d_outer, v], axis=0)
    right = jnp.concatenate(
        [0.25 * exact(v, h3_s), -exact(s0, h2), 7.0 * s0 - exact(s0, x_s), -s0], axis=0
    )
    d_x = exact(left, right, TN)
    outer = exact(inner, h3_s)
    d_ktwo = (factor * 0.0625) * exact(outer, g_mixing, TN) + factor * exact(
        d_x + jnp.transpose(d_x), ktwo_s
    )
    g_score = ktwo * (d_ktwo - jnp.sum(ktwo * d_ktwo, axis=1, keepdims=True))
    out_ref[...] = jnp.zeros((M, 2 * half), F32)
    high, low = split_up(g_score)
    out_ref[:, pl.ds(at, DH)] = (dot(high, lk) + dot(low, lk)) * SCALE
    out_ref[:, pl.ds(at + half, DH)] = (dot(high, lq, TN) + dot(low, lq, TN)) * SCALE


def unpacked(got, h, heads):
    count, rows, _ = got.shape
    per_head = count // heads
    cols = (rows - 8) // 2
    parts = [got[h * per_head + j] for j in range(per_head)]
    g_weighted = jnp.concatenate(
        [
            jnp.concatenate([part[:cols], part[cols : 2 * cols]], axis=1)
            for part in parts
        ],
        axis=0,
    )
    tails = [part.astype(F32)[2 * cols :] for part in parts]
    summed = functools.reduce(jnp.add, tails)
    g_totals = joined(summed[0:2] + summed[2:4])
    top = joined(tails[0][6:8])
    gain = tails[0][4:5] + tails[0][5:6]
    return g_weighted, g_totals, top, gain


def queryland_body(
    got_ref, exp_ref, k_ref, v_ref, extra_ref, keyland_ref, land_ref, out_ref, pass_ref
):
    heads = exp_ref.shape[0]
    half = heads * DH
    for h in range(heads):
        g_weighted, g_totals, top, _ = unpacked(got_ref, h, heads)
        keys = k_ref[:, head_cols(h)]
        vals = v_ref[:, head_cols(h)]
        tok = keys.shape[0]
        shift = exp_ref[h, tok:].astype(F32)[0:1]
        exp_three = exp_ref[h, :tok].astype(F32) * jnp.exp(shift - top)
        g_score = (exp_three * (dot(vals, g_weighted) + g_totals)).astype(BF16)
        queryland = dot(g_score, keys, TN) * SCALE
        out_ref[:, head_cols(h)] = (queryland + extra_ref[:, head_cols(h)]).astype(BF16)
    out_ref[:, half:] = (extra_ref[:, half:] + keyland_ref[...].astype(F32)).astype(BF16)
    count, rows, _ = got_ref.shape
    for place in range(count):
        pass_ref[place * rows : (place + 1) * rows] = got_ref[place]
    for h in range(heads):
        at = count * rows + h * M
        pass_ref[at : at + M] = land_ref[:, head_cols(h)]


class Parts:
    def __init__(self, ref, count, rows):
        self.ref, self.shape = ref, (count, rows, ref.shape[1])

    def __getitem__(self, place):
        rows = self.shape[1]
        return self.ref[place * rows : (place + 1) * rows]


def value_body(
    count, ids_ref, k_ref, v_ref, pass_ref, pass_there, value_out, key_out, gain_out
):
    heads = k_ref.shape[1] // (2 * DH)
    total = pass_ref.shape[0] - heads * M

    def place_halves(core, own, away):
        for place, ref in ((own, pass_ref), (away, pass_there)):
            for h in range(heads):
                cols = slice(place.start + h * DH, place.start + (h + 1) * DH)
                g_weighted, g_totals, top, gain = unpacked(
                    Parts(ref, count, total // count), h, heads
                )
                lq = ref[total + h * M : total + (h + 1) * M]
                exp_three = jnp.exp(dot(k_ref[:, cols], lq, NT) * SCALE - top)
                g_exp = dot(v_ref[:, cols], g_weighted) + g_totals
                value_out[:, cols] = dot(exp_three.astype(BF16), g_weighted, NT).astype(BF16)
                key_out[:, cols] = dot((exp_three * g_exp).astype(BF16), lq) * SCALE
                gain_out[:, cols] = gain

    by_core(ids_ref, place_halves)


def by_core(ids_ref, place_halves):
    half = 2 * DH
    left, right = slice(0, half), slice(half, 2 * half)

    @pl.when(ids_ref[0] == 0)
    def _():
        place_halves(0, left, right)

    @pl.when(ids_ref[0] != 0)
    def _():
        place_halves(1, right, left)


def gather_body(ids_ref, mine_ref, there_ref, norm_out):
    def place_halves(core, own, away):
        norm_out[:, own] = mine_ref[0]
        norm_out[:, away] = there_ref[0]

    by_core(ids_ref, place_halves)


def finish_body(
    ids_ref, got_ref, mine_ref, there_ref, key_ref, query_out, key_out
):
    count, land_dev, both = got_ref.shape
    _, tok, half = mine_ref.shape
    seg_len = tok // land_dev
    lands = []
    for core in range(2):
        got = got_ref[core].astype(F32)
        for chip in range(1, count // 2):
            got = got + got_ref[2 * chip + core].astype(F32)
        lands.append(got / seg_len)
    spans = [(row, slice(row * seg_len, (row + 1) * seg_len)) for row in range(land_dev)]

    def place_halves(core, own, away):
        for place, land, ref in (
            (own, lands[core], mine_ref), (away, lands[1 - core], there_ref)
        ):
            for row, span in spans:
                query_out[span, place] = (
                    ref[1, span].astype(F32) + land[row : row + 1, :half]
                ).astype(BF16)

    by_core(ids_ref, place_halves)
    for core in range(2):
        place = slice(core * half, (core + 1) * half)
        for row, span in spans:
            key_out[span, place] = (
                key_ref[span, place] + lands[core][row : row + 1, half:]
            ).astype(BF16)


def on_device(queries, keys_in, values, norm_gain, out_grad):
    tok, width = queries.shape
    half = width // 2
    heads = half // DH
    n_ctx = lax.axis_size("ctx")
    n_head = lax.axis_size("head")
    chips = n_ctx // 2
    per_head = chips // heads
    cols = DH // per_head
    land_dev = M // n_ctx
    here = lax.axis_index("ctx").astype(jnp.int32)
    ids = jnp.stack([lax.rem(here, 2), lax.div(here, 2 * per_head)])
    gain = norm_gain.reshape(1, width)
    same_core = [list(range(core, n_ctx, 2)) for core in range(2)]
    same_chip = [
        [(2 * chip + core) * n_head + z for core in range(2) for z in range(n_head)]
        for chip in range(chips)
    ]
    swap = [(i, i ^ 1) for i in range(n_ctx)]
    packed = shape(chips, 2 * cols + 8, DH, dtype=BF16)
    pair = shape(2, tok, half, dtype=BF16)
    wide_b = shape(tok, width, dtype=BF16)
    units = shape(heads, 2 * tok, M, dtype=BF16)

    both_b = shape(2 * tok, half, dtype=BF16)
    turned_b = shape(half, 2 * tok, dtype=BF16)
    (own,) = call(
        means_body, [shape(n_ctx, land_dev, 2 * half, dtype=BF16)], queries, keys_in,
        far_in=(0, 1), far_out=(0,), vmem=MOST_VMEM, flops=10**6, name="landmark_means",
    )
    held = lax.optimization_barrier((own, keys_in, values, queries, out_grad))
    k_there, v_there, q_there, g_there = [lax.ppermute(x, "ctx", swap) for x in held[1:]]
    land = exchange(own, "ctx").reshape(M, 2 * half)
    keys, vals = call(
        stack_body, [both_b, both_b], ids, keys_in, values, k_there, v_there,
        scalars=1, after=(own,), flops=10**6, name="stack_kv",
    )

    (parts,) = call(context_body, [packed], land, keys, vals, flops=10**8, name="local_context")
    got = exchange(parts, "ctx", same_core)
    inverse, inverse_again, chain = call(
        inverse_body, [shape(M, M), shape(M, M), shape(7, M, M)], ids, land,
        scalars=1, after=(parts,), flops=3 * 10**9, name="inverse",
    )
    parts, kept = call(
        mixing_body, [shape(chips, cols, M, dtype=BF16), shape(cols + 8, M)],
        got, inverse, flops=10**8, name="mixing",
    )
    qs, grads = call(
        stack_turned_body, [both_b, turned_b], ids, queries, out_grad, q_there, g_there,
        scalars=1, after=(parts,), flops=10**6, name="stack_qg",
    )
    kone, exp_local = call(
        ahead_body, [units, shape(heads, 2 * tok + 16, M, dtype=BF16)], qs, keys, land,
        after=(parts,), flops=2 * 10**9, name="ahead",
    )
    mixing = exchange(parts, "ctx", same_core).reshape(heads, DH, M)

    output, sums = call(
        output_body, [shape(half, 2 * tok), shape(2 * n_head, 2, 2 * tok)],
        ids, kone, mixing, grads, gain, scalars=1, flops=10**8, name="output",
    )
    sums = exchange(sums, ("ctx", "head"), same_chip)
    (parts,) = call(
        norm_body, [packed], ids, sums, output, grads, gain, kone,
        scalars=1, flops=10**8, name="norm",
    )
    got = exchange(parts, "ctx", same_core)
    mine, other, keyland = call(
        query_body, [pair, pair, shape(M, half, dtype=BF16)],
        ids, sums, output, grads, gain, mixing, qs, land,
        scalars=1, after=(parts,), flops=2 * 10**9, name="kernel_one_back",
    )
    parts, g_mixing = call(
        grad_context_body, [packed, shape(cols, M)], got, inverse_again, kept,
        after=(other,), flops=10**8, name="context_back",
    )
    got = exchange(parts, "ctx", same_core)
    (extra,) = call(
        inverse_back_body, [shape(M, 2 * half)], ids, chain, kept, g_mixing, land,
        scalars=1, after=(parts,), flops=5 * 10**9, name="inverse_back",
    )
    both, passed = call(
        queryland_body,
        [shape(M, 2 * half, dtype=BF16), shape(chips * (2 * cols + 8) + heads * M, DH, dtype=BF16)],
        got, exp_local, keys, vals, extra, keyland, land, flops=10**8, name="landmarks_back",
    )
    landed = exchange(both.reshape(n_ctx, land_dev, 2 * half), "ctx")
    there = lax.ppermute(other, "ctx", swap)
    passed_there = lax.ppermute(passed, "ctx", swap)
    (normed,) = call(
        gather_body, [wide_b], ids, mine, there,
        scalars=1, after=(both,), flops=10**6, name="gather",
    )
    value_grad, key_three, gain_grad = call(
        functools.partial(value_body, chips), [wide_b, shape(tok, width), shape(1, width)],
        ids, keys_in, values, passed, passed_there,
        scalars=1, after=(both,), flops=2 * 10**9, name="kernel_three_back",
    )
    query_grad, key_grad = call(
        finish_body, [wide_b, wide_b], ids, landed, mine, there, key_three,
        scalars=1, after=(normed,), flops=10**6, name="finish",
    )
    return (normed, query_grad, key_grad, value_grad, gain_grad.reshape(width))


def solution(mesh):
    return jax.shard_map(
        on_device,
        mesh=mesh,
        in_specs=(
            P("ctx", "head"),
            P("ctx", "head"),
            P("ctx", "head"),
            P("head"),
            P("ctx", "head"),
        ),
        out_specs=(
            P("ctx", "head"),
            P("ctx", "head"),
            P("ctx", "head"),
            P("ctx", "head"),
            P("head"),
        ),
        check_vma=False,
    )
```

```python
import functools

import jax
import jax.numpy as jnp
from jax import lax
from jax.experimental import pallas as pl
from jax.experimental.pallas import tpu as pltpu
from jax.sharding import PartitionSpec as P

DH = 128
M = 256
EPS = 1e-06
F32 = jnp.float32
BF16 = jnp.bfloat16
SCALE = DH ** (-0.5)
VMEM_BYTES = 32 * 1024 * 1024
MOST_VMEM = 60 * 1024 * 1024
HALVES = (slice(0, DH), slice(DH, 2 * DH))

NN = (((1,), (0,)), ((), ()))
NT = (((1,), (1,)), ((), ()))
TN = (((0,), (0,)), ((), ()))


def dot(a, b, dims=NN):
    return lax.dot_general(a, b, dims, preferred_element_type=F32)


def split_up(x):
    high = x.astype(BF16)
    return high, (x - high.astype(F32)).astype(BF16)


def exact(a, b, dims=NN):
    a_high, a_low = a if isinstance(a, tuple) else split_up(a)
    b_high, b_low = b if isinstance(b, tuple) else split_up(b)
    if dims == TN:
        return dot(a_high, b_high, dims) + (
            dot(a_high, b_low, dims) + dot(a_low, b_high, dims)
        )
    n = a_high.shape[0]
    both = dot(jnp.concatenate([a_high, a_low], axis=0), b_high, dims)
    return both[:n] + (both[n:] + dot(a_high, b_low, dims))


def exchange(parts, axis, groups=None):
    return lax.all_to_all(parts, axis, 0, 0, axis_index_groups=groups)


def high_low(x):
    high = x.astype(BF16).astype(F32)
    return high, x - high


def rows_of(*rows):
    index = lax.broadcasted_iota(jnp.int32, (8, rows[0].shape[1]), 0)
    out = jnp.zeros((8, rows[0].shape[1]), F32)
    for place, row in enumerate(rows):
        out = jnp.where(index == place, row, out)
    return out


def eye_times(value):
    row = lax.broadcasted_iota(jnp.int32, (M, M), 0)
    col = lax.broadcasted_iota(jnp.int32, (M, M), 1)
    return jnp.where(row == col, value, 0.0).astype(F32)


def head_cols(h):
    return slice(h * DH, (h + 1) * DH)


def halves(x):
    return jnp.concatenate([x[:, :DH], x[:, DH:]], axis=0)


def joined(x):
    n = x.shape[0] // 2
    return jnp.concatenate([x[:n], x[n:]], axis=1)


def own_head(ids_ref, h):
    return pl.ds(pl.multiple_of((ids_ref[0] * 2 + h) * DH, DH), DH)


def stacked(ids_ref, refs, h):
    return jnp.concatenate([ref[:, own_head(ids_ref, h)] for ref in refs], axis=0)


def rows_of(*rows):
    index = lax.broadcasted_iota(jnp.int32, (8, rows[0].shape[1]), 0)
    out = jnp.zeros((8, rows[0].shape[1]), F32)
    for place, row in enumerate(rows):
        out = jnp.where(index == place, row, out)
    return out


def eye_times(value):
    row = lax.broadcasted_iota(jnp.int32, (M, M), 0)
    col = lax.broadcasted_iota(jnp.int32, (M, M), 1)
    return jnp.where(row == col, value, 0.0).astype(F32)


def head_cols(h):
    return slice(h * DH, (h + 1) * DH)


def halves(x):
    return jnp.concatenate([x[:, :DH], x[:, DH:]], axis=0)


def joined(x):
    n = x.shape[0] // 2
    return jnp.concatenate([x[:n], x[n:]], axis=1)


def both_blocks(mine_ref, other_ref, which, h):
    return jnp.concatenate(
        [ref[which, :, head_cols(h)] for ref in (mine_ref, other_ref)], axis=0
    )


def call(
    body, outs, *args, scalars=0, far_in=(), far_out=(), after=(), flops=0,
    vmem=VMEM_BYTES, early=False, name
):
    nbytes = sum(a.size * a.dtype.itemsize for a in (*args, *outs))
    n_in, n_after, n_out = len(args), len(after), len(outs)
    n_far = len(far_in) + len(far_out)

    def whole(*refs):
        ins = list(refs[:n_in])
        results = list(refs[n_in + n_after : n_in + n_after + n_out])
        buffers = refs[n_in + n_after + n_out :]
        loads, stores = [], []
        for k, i in enumerate(far_in):
            loads.append(pltpu.make_async_copy(ins[i], buffers[k], buffers[n_far].at[k]))
            ins[i] = buffers[k]
        for k, i in enumerate(far_out, len(far_in)):
            stores.append(
                pltpu.make_async_copy(buffers[k], results[i], buffers[n_far].at[k])
            )
            results[i] = buffers[k]
        for copy in loads:
            copy.start()
        for copy in loads:
            copy.wait()
        if early:
            body(*ins, *results, [copy.start for copy in stores])
        else:
            body(*ins, *results)
            for copy in stores:
                copy.start()
        for copy in stores:
            copy.wait()

    def space(place, far):
        return pl.BlockSpec(memory_space=pltpu.HBM if place in far else pltpu.VMEM)

    in_specs = [
        pl.BlockSpec(memory_space=pltpu.SMEM) if i < scalars else space(i, far_in)
        for i in range(n_in)
    ] + [pl.BlockSpec(memory_space=pl.ANY)] * n_after
    scratch = [pltpu.VMEM(args[i].shape, args[i].dtype) for i in far_in]
    scratch += [pltpu.VMEM(outs[i].shape, outs[i].dtype) for i in far_out]
    if n_far:
        scratch.append(pltpu.SemaphoreType.DMA((n_far,)))
    return pl.pallas_call(
        whole,
        out_shape=outs,
        in_specs=in_specs,
        out_specs=[space(i, far_out) for i in range(n_out)],
        scratch_shapes=scratch,
        compiler_params=pltpu.CompilerParams(vmem_limit_bytes=vmem),
        cost_estimate=pl.CostEstimate(flops=flops, bytes_accessed=nbytes, transcendentals=0),
        name=name,
    )(*args, *after)


def shape(*dims, dtype=F32):
    return jax.ShapeDtypeStruct(dims, dtype)


def means_body(q_ref, k_ref, out_ref):
    count, land_dev, both = out_ref.shape
    half = both // 2
    seg_len = q_ref.shape[0] // land_dev
    q_mean, k_mean = [
        jnp.sum(ref[...].astype(F32).reshape(land_dev, seg_len, 2 * half), axis=1) / seg_len
        for ref in (q_ref, k_ref)
    ]
    for core in range(2):
        cols = slice(core * half, (core + 1) * half)
        own = jnp.concatenate([q_mean[:, cols], k_mean[:, cols]], axis=1).astype(BF16)
        for chip in range(count // 2):
            out_ref[2 * chip + core] = own


def stack_body(ids_ref, *refs):
    count = len(refs) // 3
    for mine, there, out in zip(refs[:count], refs[count : 2 * count], refs[2 * count :]):
        for h in range(out.shape[1] // DH):
            out[:, head_cols(h)] = stacked(ids_ref, (mine, there), h)


def stack_turned_body(ids_ref, q_ref, g_ref, q_there, g_there, q_out, g_out):
    for h in range(q_out.shape[1] // DH):
        q_out[:, head_cols(h)] = stacked(ids_ref, (q_ref, q_there), h)
        g_out[head_cols(h)] = jnp.transpose(stacked(ids_ref, (g_ref, g_there), h))


def context_body(land_ref, k_ref, v_ref, out_ref):
    count = out_ref.shape[0]
    heads = land_ref.shape[1] // (2 * DH)
    per_head = count // heads
    cols = DH // per_head
    for h in range(heads):
        keys = k_ref[:, head_cols(h)]
        vals = v_ref[:, head_cols(h)]
        score = dot(keys, land_ref[:, head_cols(h)], NT) * SCALE
        shift = jnp.max(score, axis=0, keepdims=True).astype(BF16).astype(F32)
        exp_local = jnp.exp(score - shift)
        high, low = high_low(jnp.sum(exp_local, axis=0, keepdims=True))
        weighted = dot(vals, exp_local.astype(BF16), TN)
        stats = rows_of(*[row[:, part] for row in (shift, high, low) for part in HALVES])
        for j in range(per_head):
            out_ref[h * per_head + j] = jnp.concatenate(
                [halves(weighted[j * cols : (j + 1) * cols]), stats], axis=0
            ).astype(BF16)


def inverse_body(ids_ref, land_ref, first_ref, again_ref, out_ref):
    half = land_ref.shape[1] // 2
    at = pl.multiple_of(ids_ref[1] * DH, DH)
    lq = land_ref[:, pl.ds(at, DH)]
    lk = land_ref[:, pl.ds(at + half, DH)]
    score = dot(lq, lk, NT) * SCALE
    top = jnp.exp(score - jnp.max(score, axis=1, keepdims=True))
    ktwo = top / jnp.sum(top, axis=1, keepdims=True)
    factor = column_factor(ktwo)
    ktwo_s = split_up(ktwo)
    x = factor * exact(ktwo_s, ktwo_s, NT)
    x_s = split_up(x)
    h2 = eye_times(15.0) - exact(x_s, eye_times(7.0) - x)
    h3 = eye_times(13.0) - exact(x_s, h2)
    h3_s = split_up(h3)
    p1 = 0.25 * exact(x_s, h3_s)
    p1_s = split_up(p1)
    b2 = eye_times(15.0) - exact(p1_s, eye_times(7.0) - p1)
    b3 = eye_times(13.0) - exact(p1_s, b2)
    inverse = (factor * 0.0625) * exact(b3, exact(h3_s, ktwo_s))
    first_ref[...] = inverse
    again_ref[...] = inverse
    for place, part in enumerate((ktwo, x, h2, h3, p1, b2, b3)):
        out_ref[place] = part


def column_factor(ktwo):
    return 1.0 / jnp.max(jnp.sum(ktwo, axis=0, keepdims=True), axis=1, keepdims=True)


def mixing_body(got_ref, inv_ref, out_ref, kept_ref):
    count, rows, _ = got_ref.shape
    cols = (rows - 8) // 2
    tops = got_ref[0].astype(F32)[rows - 8 :]
    for place in range(1, count):
        tops = jnp.maximum(tops, got_ref[place].astype(F32)[rows - 8 :])
    tops = tops[0:2]
    total = jnp.zeros((2, DH), F32)
    left = jnp.zeros((cols, DH), F32)
    right = jnp.zeros((cols, DH), F32)
    for place in range(count):
        part = got_ref[place].astype(F32)
        stats = part[rows - 8 :]
        fade = jnp.exp(stats[0:2] - tops)
        total = total + fade * (stats[2:4] + stats[4:6])
        left = left + fade[0:1] * part[:cols]
        right = right + fade[1:2] * part[cols : 2 * cols]
    total = joined(total)
    context = jnp.concatenate([left, right], axis=1) / total
    mixing = exact(context, inv_ref[...]).astype(BF16)
    for place in range(count):
        out_ref[place] = mixing
    kept_ref[...] = jnp.concatenate([context, rows_of(total, joined(tops))], axis=0)


def softmax_rows(score):
    top = jnp.exp(score - jnp.max(score, axis=1, keepdims=True))
    return top / jnp.sum(top, axis=1, keepdims=True)


def kernel_one(q_ref, land_ref, h):
    heads = land_ref.shape[1] // (2 * DH)
    score = dot(q_ref[:, head_cols(h)], land_ref[:, head_cols(heads + h)], NT) * SCALE
    return softmax_rows(score)


def ahead_body(
    q_ref, k_ref, land_ref, kone_ref, exp_ref
):
    heads, tok, _ = kone_ref.shape
    for h in range(heads):
        kone = kernel_one(q_ref, land_ref, h).astype(BF16)
        kone_ref[h] = kone
        keys = k_ref[:, head_cols(h)]
        score = dot(keys, land_ref[:, head_cols(h)], NT) * SCALE
        shift = jnp.max(score, axis=0, keepdims=True).astype(BF16).astype(F32)
        exp_ref[h, :tok] = jnp.exp(score - shift).astype(BF16)
        exp_ref[h, tok:] = jnp.broadcast_to(shift, (16, M)).astype(BF16)


def gain_column(ids_ref, gain_ref, h):
    row = jnp.broadcast_to(gain_ref[:, own_head(ids_ref, h)], (8, DH))
    return jnp.transpose(row)[:, 0:1]


def output_body(ids_ref, kone_ref, mix_ref, g_ref, gain_ref, out_ref, sum_ref):
    heads, tok, _ = kone_ref.shape
    squares = jnp.zeros((DH, tok), F32)
    slopes = jnp.zeros((DH, tok), F32)
    for h in range(heads):
        out = dot(mix_ref[h], kone_ref[h], NT)
        out_ref[head_cols(h)] = out
        scaled = g_ref[head_cols(h)].astype(F32) * gain_column(ids_ref, gain_ref, h)
        squares = squares + out * out
        slopes = slopes + scaled * out
    both = rows_of(
        *[
            swap_blocks(ids_ref, jnp.sum(part, axis=0, keepdims=True), 1)
            for part in (squares, slopes)
        ]
    )
    for place in range(sum_ref.shape[0]):
        sum_ref[place] = both[:2]


def swap_blocks(ids_ref, x, axis):
    size = x.shape[axis] // 2
    left = lax.slice_in_dim(x, 0, size, axis=axis)
    right = lax.slice_in_dim(x, size, 2 * size, axis=axis)
    swapped = jnp.concatenate([right, left], axis=axis)
    return jnp.where(ids_ref[0] == 0, x, swapped)


def token_factors(ids_ref, sum_ref, features):
    total = sum_ref[0]
    for place in range(1, sum_ref.shape[0]):
        total = total + sum_ref[place]
    root_inv = lax.rsqrt(total[0:1] / features + EPS)
    slope = total[1:2] * root_inv / features
    return swap_blocks(ids_ref, root_inv, 1), swap_blocks(ids_ref, root_inv * slope, 1)


def output_grad(factors, out, grad, gain):
    root_inv, bent = factors
    return (root_inv * (grad * gain - out * bent)).astype(BF16)


def norm_body(ids_ref, sum_ref, out_ref, g_ref, gain_ref, kone_ref, part_ref):
    heads = kone_ref.shape[0]
    per_head = part_ref.shape[0] // heads
    cols = DH // per_head
    factors = token_factors(ids_ref, sum_ref, heads * DH * sum_ref.shape[0])
    for h in range(heads):
        out = out_ref[head_cols(h)]
        grad = g_ref[head_cols(h)].astype(F32)
        gain = gain_column(ids_ref, gain_ref, h)
        g_mixing = dot(output_grad(factors, out, grad, gain), kone_ref[h])
        gain_sum = jnp.sum(grad * (out * factors[0]), axis=1, keepdims=True)
        gain_sum = jnp.transpose(jnp.broadcast_to(gain_sum, (DH, DH)))[0:1]
        tail = rows_of(*high_low(gain_sum))
        for j in range(per_head):
            part_ref[h * per_head + j] = jnp.concatenate(
                [halves(g_mixing[j * cols : (j + 1) * cols]), tail], axis=0
            ).astype(BF16)


def query_body(
    ids_ref, sum_ref, out_ref, g_ref, gain_ref, mix_ref, q_ref, land_ref,
    mine_ref, other_ref, keyland_ref,
):
    heads = mix_ref.shape[0]
    tok = mine_ref.shape[1]
    factors = token_factors(ids_ref, sum_ref, heads * DH * sum_ref.shape[0])
    for h in range(heads):
        out = out_ref[head_cols(h)]
        grad = g_ref[head_cols(h)].astype(F32)
        gain = gain_column(ids_ref, gain_ref, h)
        normed = jnp.transpose(out * factors[0] * gain).astype(BF16)
        mine_ref[0, :, head_cols(h)] = normed[:tok]
        other_ref[0, :, head_cols(h)] = normed[tok:]
        kone = kernel_one(q_ref, land_ref, h)
        g_kernel = dot(output_grad(factors, out, grad, gain), mix_ref[h], TN)
        inner = jnp.sum(kone * g_kernel, axis=1, keepdims=True)
        g_score = (kone * (g_kernel - inner)).astype(BF16)
        query = dot(g_score, land_ref[:, head_cols(heads + h)]) * SCALE
        mine_ref[1, :, head_cols(h)] = query[:tok].astype(BF16)
        other_ref[1, :, head_cols(h)] = query[tok:].astype(BF16)
        queries = q_ref[:, head_cols(h)]
        keyland_ref[:, head_cols(h)] = (dot(g_score, queries, TN) * SCALE).astype(BF16)


def grad_context_body(got_ref, inv_ref, kept_ref, out_ref, g_ref):
    count, rows, _ = got_ref.shape
    cols = (rows - 8) // 2
    got = got_ref[0].astype(F32)
    for place in range(1, count):
        got = got + got_ref[place].astype(F32)
    g_mixing = joined(got[: 2 * cols])
    gain = high_low(got[2 * cols : 2 * cols + 1] + got[2 * cols + 1 : 2 * cols + 2])
    context = kept_ref[:cols]
    total = kept_ref[cols : cols + 1]
    top = kept_ref[cols + 1 : cols + 2]
    g_context = exact(g_mixing, inv_ref[...], NT)
    high, low = high_low(-jnp.sum(g_context * context, axis=0, keepdims=True) / total)
    tail = rows_of(
        *[row[:, part] for row in (high, low) for part in HALVES],
        *gain,
        *[top[:, part] for part in HALVES],
    )
    mine = jnp.concatenate([halves(g_context / total), tail], axis=0).astype(BF16)
    for place in range(count):
        out_ref[place] = mine
    g_ref[...] = g_mixing


def inverse_back_body(ids_ref, inv_ref, kept_ref, g_ref, land_ref, out_ref):
    half = land_ref.shape[1] // 2
    at = pl.multiple_of(ids_ref[1] * DH, DH)
    lq = land_ref[:, pl.ds(at, DH)]
    lk = land_ref[:, pl.ds(at + half, DH)]
    ktwo, x, h2, h3, p1, b2, b3 = [inv_ref[place] for place in range(7)]
    factor = column_factor(ktwo)
    ktwo_s, x_s, h3_s, p1_s = [split_up(part) for part in (ktwo, x, h3, p1)]
    g_mixing = split_up(g_ref[...])
    n = g_ref.shape[0]
    context = kept_ref[:n]
    once = exact(context, p1_s)
    inner = exact(context, b3)
    u = jnp.concatenate([-context, once, -exact(once, p1_s)], axis=0)
    r0 = jnp.concatenate([inner, 0.25 * exact(u, x_s)], axis=0)
    r1 = exact(r0, x_s)
    left = jnp.concatenate([u, r0, r1, exact(r1, x_s)], axis=0)
    d_outer = (factor * 0.0625) * exact(g_mixing, ktwo_s, NT)
    d = exact(d_outer, h3_s)
    v = jnp.concatenate([exact(d, b2), 7.0 * d - exact(d, p1_s), d], axis=0)
    s0 = jnp.concatenate([d_outer, v], axis=0)
    right = jnp.concatenate(
        [0.25 * exact(v, h3_s), -exact(s0, h2), 7.0 * s0 - exact(s0, x_s), -s0], axis=0
    )
    d_x = exact(left, right, TN)
    outer = exact(inner, h3_s)
    d_ktwo = (factor * 0.0625) * exact(outer, g_mixing, TN) + factor * exact(
        d_x + jnp.transpose(d_x), ktwo_s
    )
    g_score = ktwo * (d_ktwo - jnp.sum(ktwo * d_ktwo, axis=1, keepdims=True))
    out_ref[...] = jnp.zeros((M, 2 * half), F32)
    high, low = split_up(g_score)
    out_ref[:, pl.ds(at, DH)] = (dot(high, lk) + dot(low, lk)) * SCALE
    out_ref[:, pl.ds(at + half, DH)] = (dot(high, lq, TN) + dot(low, lq, TN)) * SCALE


def unpacked(got, h, heads):
    count, rows, _ = got.shape
    per_head = count // heads
    cols = (rows - 8) // 2
    parts = [got[h * per_head + j] for j in range(per_head)]
    g_weighted = jnp.concatenate(
        [
            jnp.concatenate([part[:cols], part[cols : 2 * cols]], axis=1)
            for part in parts
        ],
        axis=0,
    )
    tails = [part.astype(F32)[2 * cols :] for part in parts]
    summed = functools.reduce(jnp.add, tails)
    g_totals = joined(summed[0:2] + summed[2:4])
    top = joined(tails[0][6:8])
    gain = tails[0][4:5] + tails[0][5:6]
    return g_weighted, g_totals, top, gain


def queryland_body(
    got_ref, exp_ref, k_ref, v_ref, extra_ref, keyland_ref, land_ref, out_ref, pass_ref
):
    heads = exp_ref.shape[0]
    half = heads * DH
    for h in range(heads):
        g_weighted, g_totals, top, _ = unpacked(got_ref, h, heads)
        keys = k_ref[:, head_cols(h)]
        vals = v_ref[:, head_cols(h)]
        tok = keys.shape[0]
        shift = exp_ref[h, tok:].astype(F32)[0:1]
        exp_three = exp_ref[h, :tok].astype(F32) * jnp.exp(shift - top)
        g_score = (exp_three * (dot(vals, g_weighted) + g_totals)).astype(BF16)
        queryland = dot(g_score, keys, TN) * SCALE
        out_ref[:, head_cols(h)] = (queryland + extra_ref[:, head_cols(h)]).astype(BF16)
    out_ref[:, half:] = (extra_ref[:, half:] + keyland_ref[...].astype(F32)).astype(BF16)
    count, rows, _ = got_ref.shape
    for place in range(count):
        pass_ref[place * rows : (place + 1) * rows] = got_ref[place]
    for h in range(heads):
        at = count * rows + h * M
        pass_ref[at : at + M] = land_ref[:, head_cols(h)]


class Parts:
    def __init__(self, ref, count, rows):
        self.ref, self.shape = ref, (count, rows, ref.shape[1])

    def __getitem__(self, place):
        rows = self.shape[1]
        return self.ref[place * rows : (place + 1) * rows]


def value_body(
    count, ids_ref, k_ref, v_ref, pass_ref, pass_there, value_out, key_out, gain_out
):
    heads = k_ref.shape[1] // (2 * DH)
    total = pass_ref.shape[0] - heads * M

    def place_halves(core, own, away):
        for place, ref in ((own, pass_ref), (away, pass_there)):
            for h in range(heads):
                cols = slice(place.start + h * DH, place.start + (h + 1) * DH)
                g_weighted, g_totals, top, gain = unpacked(
                    Parts(ref, count, total // count), h, heads
                )
                lq = ref[total + h * M : total + (h + 1) * M]
                exp_three = jnp.exp(dot(k_ref[:, cols], lq, NT) * SCALE - top)
                g_exp = dot(v_ref[:, cols], g_weighted) + g_totals
                value_out[:, cols] = dot(exp_three.astype(BF16), g_weighted, NT).astype(BF16)
                key_out[:, cols] = dot((exp_three * g_exp).astype(BF16), lq) * SCALE
                gain_out[:, cols] = gain

    by_core(ids_ref, place_halves)


def by_core(ids_ref, place_halves):
    half = 2 * DH
    left, right = slice(0, half), slice(half, 2 * half)

    @pl.when(ids_ref[0] == 0)
    def _():
        place_halves(0, left, right)

    @pl.when(ids_ref[0] != 0)
    def _():
        place_halves(1, right, left)


def gather_body(ids_ref, mine_ref, there_ref, norm_out):
    def place_halves(core, own, away):
        norm_out[:, own] = mine_ref[0]
        norm_out[:, away] = there_ref[0]

    by_core(ids_ref, place_halves)


def finish_body(
    ids_ref, got_ref, mine_ref, there_ref, key_ref, query_out, key_out, send
):
    count, land_dev, both = got_ref.shape
    _, tok, half = mine_ref.shape
    seg_len = tok // land_dev
    lands = []
    for core in range(2):
        got = got_ref[core].astype(F32)
        for chip in range(1, count // 2):
            got = got + got_ref[2 * chip + core].astype(F32)
        lands.append(got / seg_len)
    spans = [(row, slice(row * seg_len, (row + 1) * seg_len)) for row in range(land_dev)]

    def place_halves(core, own, away):
        for place, land, ref in (
            (own, lands[core], mine_ref), (away, lands[1 - core], there_ref)
        ):
            for row, span in spans:
                query_out[span, place] = (
                    ref[1, span].astype(F32) + land[row : row + 1, :half]
                ).astype(BF16)

    by_core(ids_ref, place_halves)
    send[0]()
    for core in range(2):
        place = slice(core * half, (core + 1) * half)
        for row, span in spans:
            key_out[span, place] = (
                key_ref[span, place] + lands[core][row : row + 1, half:]
            ).astype(BF16)
    send[1]()


def on_device(queries, keys_in, values, norm_gain, out_grad):
    tok, width = queries.shape
    half = width // 2
    heads = half // DH
    n_ctx = lax.axis_size("ctx")
    n_head = lax.axis_size("head")
    chips = n_ctx // 2
    per_head = chips // heads
    cols = DH // per_head
    land_dev = M // n_ctx
    here = lax.axis_index("ctx").astype(jnp.int32)
    ids = jnp.stack([lax.rem(here, 2), lax.div(here, 2 * per_head)])
    gain = norm_gain.reshape(1, width)
    same_core = [list(range(core, n_ctx, 2)) for core in range(2)]
    same_chip = [
        [(2 * chip + core) * n_head + z for core in range(2) for z in range(n_head)]
        for chip in range(chips)
    ]
    swap = [(i, i ^ 1) for i in range(n_ctx)]
    packed = shape(chips, 2 * cols + 8, DH, dtype=BF16)
    pair = shape(2, tok, half, dtype=BF16)
    wide_b = shape(tok, width, dtype=BF16)
    units = shape(heads, 2 * tok, M, dtype=BF16)

    both_b = shape(2 * tok, half, dtype=BF16)
    turned_b = shape(half, 2 * tok, dtype=BF16)
    (own,) = call(
        means_body, [shape(n_ctx, land_dev, 2 * half, dtype=BF16)], queries, keys_in,
        far_in=(0, 1), far_out=(0,), vmem=MOST_VMEM, flops=10**6, name="landmark_means",
    )
    held = lax.optimization_barrier((own, keys_in, values, queries, out_grad))
    k_there, v_there, q_there, g_there = [lax.ppermute(x, "ctx", swap) for x in held[1:]]
    land = exchange(own, "ctx").reshape(M, 2 * half)
    keys, vals = call(
        stack_body, [both_b, both_b], ids, keys_in, values, k_there, v_there,
        scalars=1, after=(own,), flops=10**6, name="stack_kv",
    )

    (parts,) = call(context_body, [packed], land, keys, vals, flops=10**8, name="local_context")
    got = exchange(parts, "ctx", same_core)
    inverse, inverse_again, chain = call(
        inverse_body, [shape(M, M), shape(M, M), shape(7, M, M)], ids, land,
        scalars=1, after=(parts,), flops=3 * 10**9, name="inverse",
    )
    parts, kept = call(
        mixing_body, [shape(chips, cols, M, dtype=BF16), shape(cols + 8, M)],
        got, inverse, flops=10**8, name="mixing",
    )
    qs, grads = call(
        stack_turned_body, [both_b, turned_b], ids, queries, out_grad, q_there, g_there,
        scalars=1, after=(parts,), flops=10**6, name="stack_qg",
    )
    kone, exp_local = call(
        ahead_body, [units, shape(heads, 2 * tok + 16, M, dtype=BF16)], qs, keys, land,
        after=(parts,), flops=2 * 10**9, name="ahead",
    )
    mixing = exchange(parts, "ctx", same_core).reshape(heads, DH, M)

    output, sums = call(
        output_body, [shape(half, 2 * tok), shape(2 * n_head, 2, 2 * tok)],
        ids, kone, mixing, grads, gain, scalars=1, flops=10**8, name="output",
    )
    sums = exchange(sums, ("ctx", "head"), same_chip)
    (parts,) = call(
        norm_body, [packed], ids, sums, output, grads, gain, kone,
        scalars=1, flops=10**8, name="norm",
    )
    got = exchange(parts, "ctx", same_core)
    mine, other, keyland = call(
        query_body, [pair, pair, shape(M, half, dtype=BF16)],
        ids, sums, output, grads, gain, mixing, qs, land,
        scalars=1, after=(parts,), flops=2 * 10**9, name="kernel_one_back",
    )
    parts, g_mixing = call(
        grad_context_body, [packed, shape(cols, M)], got, inverse_again, kept,
        after=(other,), flops=10**8, name="context_back",
    )
    got = exchange(parts, "ctx", same_core)
    (extra,) = call(
        inverse_back_body, [shape(M, 2 * half)], ids, chain, kept, g_mixing, land,
        scalars=1, after=(parts,), flops=5 * 10**9, name="inverse_back",
    )
    both, passed = call(
        queryland_body,
        [shape(M, 2 * half, dtype=BF16), shape(chips * (2 * cols + 8) + heads * M, DH, dtype=BF16)],
        got, exp_local, keys, vals, extra, keyland, land, flops=10**8, name="landmarks_back",
    )
    landed = exchange(both.reshape(n_ctx, land_dev, 2 * half), "ctx")
    there = lax.ppermute(other, "ctx", swap)
    passed_there = lax.ppermute(passed, "ctx", swap)
    (normed,) = call(
        gather_body, [wide_b], ids, mine, there,
        scalars=1, after=(both,), flops=10**6, name="gather",
    )
    value_grad, key_three, gain_grad = call(
        functools.partial(value_body, chips), [wide_b, shape(tok, width), shape(1, width)],
        ids, keys_in, values, passed, passed_there,
        scalars=1, after=(both,), flops=2 * 10**9, name="kernel_three_back",
    )
    query_grad, key_grad = call(
        finish_body, [wide_b, wide_b], ids, landed, mine, there, key_three,
        scalars=1, far_out=(0, 1), early=True, after=(normed,), flops=10**6, name="finish",
    )
    return (normed, query_grad, key_grad, value_grad, gain_grad.reshape(width))


def solution(mesh):
    return jax.shard_map(
        on_device,
        mesh=mesh,
        in_specs=(
            P("ctx", "head"),
            P("ctx", "head"),
            P("ctx", "head"),
            P("head"),
            P("ctx", "head"),
        ),
        out_specs=(
            P("ctx", "head"),
            P("ctx", "head"),
            P("ctx", "head"),
            P("ctx", "head"),
            P("head"),
        ),
        check_vma=False,
    )
```
